32 devices in a mesh: groups: 2 (over x), segment: 8 (over z, y), slab: 2 (over core).
Axes of the slice: x: 2, y: 2, z: 4, core: 2. Of those that a mesh axis runs over, the one named last changes fastest.
Arguments:
- fields: float32 [8, 3, 16, 16, 16], P('groups', None, 'slab'), parts along dimension 0, may hold values from -6 to 6
- anchors: int32 [8, 3], P('groups'), parts along dimension 0, may hold values from 0 to 4095
- lift_weight: float32 [64, 6], replicated, may hold values from -2.5 to 2.5
- conv_weight: bfloat16 [8, 3, 9, 64, 192], P('segment'), may hold values from -0.03125 to 0.03125
- conv_bias: float32 [8, 3, 64], P('segment'), may hold values from -1.25 to 1.25
- proj_weight: float32 [3, 64], replicated, may hold values from -0.75 to 0.75
Outputs:
- trajectory: float32 [2, 8, 3, 16, 16, 16], P(None, 'groups', None, 'slab', None, 'segment'), parts along dimension 1
The draws below stay inside these ranges and needn't reach their ends.
There are 2 independent parts, one for each index of `groups`. The reference program is written for one: setup_inputs(seed, part) draws one part's arguments, and reference() takes and returns one part's arrays. A program takes and returns all parts, laid end to end along the dimension named above; an argument that names none is the same for every part. Nothing has to cross between parts.
All inputs are finite; a program needn't handle non-finite values.
Results may differ from the reference program's by a relative error of at most 0.028.
Values may be sent and summed in bfloat16 or wider, within the bound.
No kernel may reach another device: no remote copies, remote signals or barrier semaphores. Data moves between devices by JAX's collectives and lax.ppermute only.
A program may use at most 64 MiB of HBM per device.

```python
import jax
import jax.numpy as jnp
from jax import lax

CH = 64
LAYERS = 3
STEPS = 2
FIELD = 4096
CROPS = 4
Y = 16
Z = 16
SECTIONS = 8
X = 16


def plant(array, key, smallest, high):
    extent = array.shape
    place = [jax.random.randint(jax.random.fold_in(key, axis), (), 0, extent[axis]) for axis in range(len(extent))]
    array = array.at[tuple(place)].set(smallest)
    longest = extent.index(max(extent))
    place[longest] = (place[longest] + 1) % extent[longest]
    return array.at[tuple(place)].set(high)


def block_scale(own_key, extent, pieces, low, largest):
    factor_of, own = 1.0, jax.random.fold_in(own_key, 6)
    for dim, parts in pieces:
        steps = jnp.exp(jax.random.uniform(jax.random.fold_in(own, dim), (parts,), jnp.float32, low / len(pieces), largest / len(pieces)))
        factor_of = factor_of * jnp.repeat(steps, extent[dim] // parts).reshape([-1 if axis == dim else 1 for axis in range(len(extent))])
    return factor_of


def bell_draw(own_key, extent, deviation, reach, shards=(), held_as=jnp.bfloat16):
    array = jax.random.normal(own_key, extent, jnp.float32) * deviation
    if len(shards) > 0:
        array = block_scale(own_key, extent, shards, -0.22, 0.18) * array
    return jnp.clip(array, min=-reach, max=reach).astype(held_as)


def setup_inputs(seed: int = 0, part: int = 0) -> dict:
    keys = jax.random.split(jax.random.key(seed), 7)
    own_keys = jax.random.split(jax.random.fold_in(keys[6], part), 7)
    return {
        "fields": bell_draw(own_keys[0], (CROPS, 3, X, Y, Z), 1.0, 6.0, ((2, 2),), jnp.float32),
        "anchors": plant(jax.random.randint(own_keys[1], (CROPS, 3), 0, FIELD), jax.random.fold_in(own_keys[1], 1), 0, FIELD - 1).astype(jnp.int32),
        "lift_weight": bell_draw(keys[2], (CH, 6), 6 ** -0.5, 2.5, (), jnp.float32),
        "conv_weight": bell_draw(keys[3], (SECTIONS, LAYERS, 9, CH, 3 * CH), (27 * CH * LAYERS * SECTIONS) ** -0.5, 0.03125, ((0, 8),)),
        "conv_bias": bell_draw(keys[4], (SECTIONS, LAYERS, CH), 0.2, 1.25, ((0, 8),), jnp.float32),
        "proj_weight": bell_draw(keys[5], (3, CH), CH ** -0.5, 0.75, (), jnp.float32),
    }


def dilated_conv(activated, layer_weights, dilation):
    summed = jnp.zeros(activated.shape, jnp.float32)
    for tap_y in (-1, 0, 1):
        columns = jnp.concatenate([jnp.roll(activated, (-tap_y * dilation, -tap_z * dilation), axis=(3, 4)) for tap_z in (-1, 0, 1)], axis=0)
        for tap_x in (-1, 0, 1):
            moved = jnp.roll(columns, -tap_x * dilation, axis=2)
            product = jnp.dot(layer_weights[(tap_x + 1) * 3 + tap_y + 1], moved.reshape(moved.shape[0], -1), preferred_element_type=jnp.float32)
            summed = summed + product.reshape(activated.shape)
    return summed


def axis_wave(anchors, column, length):
    position = (anchors[:, column][:, None] + jnp.arange(length, dtype=jnp.int32)[None, :]) % FIELD
    return jnp.sin(2.0 * jnp.pi * position.astype(jnp.float32) / FIELD)


def section(hidden, params):
    weights, biases = params
    state = hidden.astype(jnp.float32)
    for layer in range(LAYERS):
        dilation = 2 ** layer
        activated = jax.nn.silu(state).astype(jnp.bfloat16)
        state = state + dilated_conv(activated, weights[layer], dilation) + biases[layer][:, None, None, None, None]
    return state.astype(jnp.bfloat16), None


def reference(fields, anchors, lift_weight, conv_weight, conv_bias, proj_weight):
    full_shape = (CROPS, X, Y, Z)
    wave_x = jnp.broadcast_to(axis_wave(anchors, 0, X)[:, :, None, None], full_shape)
    wave_y = jnp.broadcast_to(axis_wave(anchors, 1, Y)[:, None, :, None], full_shape)
    wave_z = jnp.broadcast_to(axis_wave(anchors, 2, Z)[:, None, None, :], full_shape)
    waves = jnp.stack([wave_x, wave_y, wave_z], axis=1)
    current = fields
    outputs = []
    for roll_step in range(STEPS):
        inputs = jnp.concatenate([current, waves], axis=1)
        hidden = jnp.einsum('oc,ncxyz->onxyz', lift_weight, inputs, precision=lax.Precision.HIGHEST).astype(jnp.bfloat16)
        hidden, unused = lax.scan(section, hidden, (conv_weight, conv_bias))
        current = current + jnp.einsum('oc,cnxyz->noxyz', proj_weight, hidden.astype(jnp.float32), precision=lax.Precision.HIGHEST)
        outputs.append(current)
    return jnp.stack(outputs)
```

```python
import jax
import jax.numpy as jnp
from jax import lax
from jax.experimental import pallas as pl
from jax.experimental.pallas import tpu as pltpu
from jax.sharding import PartitionSpec as P

STEPS = 2
FIELD = 4096
LAYERS = 3
CH = 64
ROWS = 960
VMEM_BYTES = 48 * 1024 * 1024

MOVES = (
    [(4 * b + m, 4 * b + 2 + m, 4 * m + b, 4 * m + 2 + b) for m in range(2) for b in range(2)],
    [(2 * m, 2 * m + 1, m, 4 + m) for m in range(4)],
    [(4 * p + 2 * m, 4 * p + 2 * m + 1, 2 * p + m, 2 * (2 + p) + m) for p in range(2) for m in range(2)],
)
NEXT = (
    [(k + 1) % 8 for k in range(8)],
    [4 * (k // 4) + (k % 4 + 1) % 4 for k in range(8)],
    [2 * (k // 2) + (k % 2 + 1) % 2 for k in range(8)],
)


def low_lanes(shape):
    return lax.broadcasted_iota(jnp.int32, shape, len(shape) - 1) < CH


def nt_dot(a, b):
    return lax.dot_general(a, b, (((1,), (1,)), ((), ())), preferred_element_type=jnp.float32)


def pack_kernel(raw_ref, eye_ref, out_ref):
    eye = eye_ref[...]
    for layer in range(LAYERS):
        for ty in range(3):
            pair = jnp.concatenate([raw_ref[layer, 3 + ty], raw_ref[layer, ty]], axis=0)
            out_ref[layer, ty * 192 : (ty + 1) * 192, :] = nt_dot(eye, pair).astype(jnp.bfloat16)
        pair = jnp.concatenate([raw_ref[layer, 6], raw_ref[layer, 7]], axis=0)
        out_ref[layer, 576:768, :] = nt_dot(eye, pair).astype(jnp.bfloat16)
        pair = jnp.concatenate([raw_ref[layer, 8], raw_ref[layer, 8]], axis=0)
        out_ref[layer, 768:960, :] = nt_dot(eye, pair).astype(jnp.bfloat16)


def expand(packed_ref, section, layer, w_ref):
    low = low_lanes((192, 128))
    zero = jnp.zeros((192, 128), jnp.float32)
    for ty in range(3):
        mid = packed_ref[section, layer, ty * 192 : (ty + 1) * 192, :].astype(jnp.float32)
        rolled = pltpu.roll(mid, CH, 1)
        begin = 576 if ty < 2 else 768
        last = packed_ref[section, layer, begin : begin + 192, :].astype(jnp.float32)
        last_rolled = pltpu.roll(last, CH, 1)
        if ty == 1:
            last, last_rolled = last_rolled, last
        blocks = (
            jnp.where(low, rolled, zero),
            mid,
            jnp.where(low, last, rolled),
            jnp.where(low, zero, last_rolled),
        )
        for a, block in enumerate(blocks):
            block = block.astype(jnp.bfloat16)
            for tz in range(3):
                w_ref[ty * 256 + a * CH : ty * 256 + (a + 1) * CH, tz * 128 : (tz + 1) * 128] = block[
                    tz * CH : (tz + 1) * CH
                ]


def spread(state_in, state_out, f_ref, layer):
    d = 2**layer
    low = low_lanes((16, 16, 128))
    for u_at, v_at, low_at, high_at in MOVES[layer]:
        u = state_in[u_at]
        v = state_in[v_at]
        pairs = (
            (low_at, jnp.where(low, u, pltpu.roll(v, CH, 2))),
            (high_at, jnp.where(low, pltpu.roll(u, CH, 2), v)),
        )
        for at, value in pairs:
            state_out[at] = value
            activated = value * (0.5 * jnp.tanh(0.5 * value) + 0.5)
            turned = pltpu.roll(activated, CH, 2).astype(jnp.bfloat16)
            following = NEXT[layer][at]
            for place, lanes in ((at, slice(CH, 128)), (following, slice(0, CH))):
                part = turned[:, :, lanes]
                f_ref[place, 4:20, :, lanes] = part
                f_ref[place, 4 - d : 4, :, lanes] = part[16 - d :]
                f_ref[place, 20 : 20 + d, :, lanes] = part[:d]


def convolve(state, f_ref, w_ref, bias, layer):
    d = 2**layer
    for k in range(8):
        following = NEXT[layer][k]
        columns = []
        for ty in (-1, 0, 1):
            begin = 4 + d * ty
            columns.append(f_ref[k, begin : begin + 16].reshape(256, 128))
            columns.append(f_ref[following, begin : begin + 16].reshape(256, 128))
        product = jnp.dot(jnp.concatenate(columns, axis=1), w_ref[...], preferred_element_type=jnp.float32)
        product = product.reshape(16, 16, 384)
        total = state[k] + bias + product[:, :, 128:256]
        total = total + pltpu.roll(product[:, :, 0:128], d, 1) + pltpu.roll(product[:, :, 256:384], 16 - d, 1)
        if layer == LAYERS - 1:
            total = total.astype(jnp.bfloat16).astype(jnp.float32)
        state[k] = total


def rollout_kernel(x_ref, lift_ref, proj_ref, packed_ref, bias_ref, out_ref, s_a, s_b, f_ref, w_ref, cur):
    cur[...] = x_ref[...]

    def rollout_step(t, unused):
        x = cur[...]
        high = x.astype(jnp.bfloat16).astype(jnp.float32)
        columns = jnp.concatenate([high, x - high, high], axis=0).T.astype(jnp.bfloat16)
        hidden = jnp.dot(columns, lift_ref[...], preferred_element_type=jnp.float32)
        s_a[...] = hidden.astype(jnp.bfloat16).astype(jnp.float32).reshape(8, 16, 16, 128)

        def section(s, unused):
            states = (s_a, s_b)
            for layer in range(LAYERS):
                before, after = states[layer % 2], states[1 - layer % 2]
                expand(packed_ref, s, layer, w_ref)
                spread(before, after, f_ref, layer)
                convolve(after, f_ref, w_ref, bias_ref[s, layer][None], layer)
            s_a[...] = s_b[...]
            return 0

        lax.fori_loop(0, packed_ref.shape[0], section, 0)
        last = s_a[...].reshape(2048, 128).astype(jnp.bfloat16)
        gain = nt_dot(proj_ref[...], last)
        renewed = cur[...] + gain[:16] + gain[16:32] + gain[32:48]
        cur[...] = renewed
        out_ref[t] = renewed
        return 0

    lax.fori_loop(0, STEPS, rollout_step, 0)


def split_terms(matrix):
    first = matrix.astype(jnp.bfloat16)
    rest = matrix - first.astype(jnp.float32)
    second = rest.astype(jnp.bfloat16)
    third = (rest - second.astype(jnp.float32)).astype(jnp.bfloat16)
    return first, second, third


def shards(fields, anchors, lift_weight, conv_weight, conv_bias, proj_weight):
    segments = lax.axis_size("segment")
    segment_id = lax.axis_index("segment")
    slab_id = lax.axis_index("slab")
    crop_count, comps, slab_rows, y_cells, z_cells = fields.shape
    slot = segment_id % crop_count
    vmem = pl.BlockSpec(memory_space=pltpu.VMEM)

    packed = pl.pallas_call(
        pack_kernel,
        out_shape=jax.ShapeDtypeStruct((LAYERS, ROWS, 128), jnp.bfloat16),
        in_specs=[vmem, vmem],
        out_specs=vmem,
        compiler_params=pltpu.CompilerParams(vmem_limit_bytes=VMEM_BYTES),
    )(conv_weight[0], jnp.eye(192, dtype=jnp.bfloat16))
    packed = lax.all_gather(packed, "segment")
    biases = lax.all_gather(conv_bias[0], "segment")
    biases = jnp.concatenate([biases, biases], axis=2)[:, :, None, :]

    mine = lax.dynamic_index_in_dim(fields, slot, 0, keepdims=False)
    other = lax.ppermute(mine, "slab", [(0, 1), (1, 0)])
    halves = jnp.where(slab_id == 0, jnp.stack([mine, other]), jnp.stack([other, mine]))
    anchor = lax.dynamic_index_in_dim(anchors, slot, 0, keepdims=False)

    def wave(column, length):
        position = (anchor[column] + jnp.arange(length, dtype=jnp.int32)) % FIELD
        return jnp.sin(2.0 * jnp.pi * position.astype(jnp.float32) / FIELD)

    shape = (2, 2, 4, y_cells, z_cells)
    current = halves.reshape(2, comps, 2, 4, y_cells, z_cells).transpose(2, 1, 3, 0, 4, 5).reshape(6, 2048)
    wave_x = jnp.broadcast_to(wave(0, 2 * slab_rows).reshape(2, 2, 4, 1, 1), shape)
    wave_y = jnp.broadcast_to(wave(1, y_cells)[:, None], shape)
    wave_z = jnp.broadcast_to(wave(2, z_cells), shape)
    waves = jnp.stack([wave_x, wave_y, wave_z]).transpose(2, 0, 3, 1, 4, 5).reshape(6, 2048)
    x = jnp.concatenate([current, waves, jnp.zeros((4, 2048), jnp.float32)], axis=0)

    half = jnp.eye(2, dtype=jnp.float32)
    lift_cur = jnp.einsum("ab,of->afbo", half, lift_weight[:, :comps]).reshape(6, 128)
    lift_wave = jnp.einsum("ab,of->afbo", half, lift_weight[:, comps:]).reshape(6, 128)
    lift = jnp.concatenate([lift_cur, lift_wave, jnp.zeros((4, 128), jnp.float32)], axis=0)
    first, second, unused = split_terms(lift)
    lift = jnp.concatenate([first, first, second], axis=0)
    proj = jnp.einsum("ab,oc->aobc", half, proj_weight).reshape(6, 128)
    proj = jnp.concatenate([proj, jnp.zeros((10, 128), jnp.float32)], axis=0)
    proj = jnp.concatenate(split_terms(proj), axis=0)

    result = pl.pallas_call(
        rollout_kernel,
        out_shape=jax.ShapeDtypeStruct((STEPS, 16, 2048), jnp.float32),
        in_specs=[vmem] * 5,
        out_specs=vmem,
        scratch_shapes=[
            pltpu.VMEM((8, 16, 16, 128), jnp.float32),
            pltpu.VMEM((8, 16, 16, 128), jnp.float32),
            pltpu.VMEM((8, 24, 16, 128), jnp.bfloat16),
            pltpu.VMEM((768, 384), jnp.bfloat16),
            pltpu.VMEM((16, 2048), jnp.float32),
        ],
        compiler_params=pltpu.CompilerParams(vmem_limit_bytes=VMEM_BYTES),
    )(x, lift, proj, packed, biases)

    own = result[:, :6].astype(jnp.bfloat16).reshape(STEPS, 2, comps, 4, 2, y_cells, z_cells)
    own = lax.dynamic_index_in_dim(own, slab_id, 4, keepdims=False)
    own = own.transpose(0, 2, 1, 3, 4, 5).reshape(STEPS, comps, slab_rows, y_cells, segments, z_cells // segments)
    base = segment_id - slot

    def part_for(target):
        return lax.dynamic_index_in_dim(own, target, 4, keepdims=False)

    parts = [part_for(segment_id)]
    for shift in range(1, crop_count):
        pairs = [(s, s - s % crop_count + (s + shift) % crop_count) for s in range(segments)]
        parts.append(lax.ppermute(part_for(base + (slot + shift) % crop_count), "segment", pairs))
    parts = jnp.stack(parts)
    order = (slot - jnp.arange(crop_count)) % crop_count
    return jnp.take(parts, order, axis=0).transpose(1, 0, 2, 3, 4, 5).astype(jnp.float32)


def solution(mesh):
    in_specs = (
        P("groups", None, "slab", None, None),
        P("groups", None),
        P(),
        P("segment", None, None, None, None),
        P("segment", None, None),
        P(),
    )
    out_specs = P(None, "groups", None, "slab", None, "segment")
    return jax.shard_map(shards, mesh=mesh, in_specs=in_specs, out_specs=out_specs, check_vma=False)
```

```python
import functools

import jax
import jax.numpy as jnp
from jax import lax
from jax.experimental import pallas as pl
from jax.experimental.pallas import tpu as pltpu
from jax.sharding import PartitionSpec as P

STEPS = 2
FIELD = 4096
LAYERS = 3
CH = 64
ROWS = 992
HALF = ROWS // 2
VMEM_BYTES = 48 * 1024 * 1024

MOVES = (
    [(4 * b + m, 4 * b + 2 + m, 4 * m + b, 4 * m + 2 + b) for m in range(2) for b in range(2)],
    [(2 * m, 2 * m + 1, m, 4 + m) for m in range(4)],
    [(4 * p + 2 * m, 4 * p + 2 * m + 1, 2 * p + m, 2 * (2 + p) + m) for p in range(2) for m in range(2)],
)
NEXT = (
    [(k + 1) % 8 for k in range(8)],
    [4 * (k // 4) + (k % 4 + 1) % 4 for k in range(8)],
    [2 * (k // 2) + (k % 2 + 1) % 2 for k in range(8)],
)


def low_lanes(shape):
    return lax.broadcasted_iota(jnp.int32, shape, len(shape) - 1) < CH


def nt_dot(a, b):
    return lax.dot_general(a, b, (((1,), (1,)), ((), ())), preferred_element_type=jnp.float32)


def pack_kernel(ids_ref, raw_ref, bias_ref, eye_ref, mine_ref, other_ref, packed):
    eye = eye_ref[...]
    for layer in range(LAYERS):
        for ty in range(3):
            pair = jnp.concatenate([raw_ref[layer, 3 + ty], raw_ref[layer, ty]], axis=0)
            packed[layer, ty * 192 : (ty + 1) * 192, :] = nt_dot(eye, pair).astype(jnp.bfloat16)
        pair = jnp.concatenate([raw_ref[layer, 6], raw_ref[layer, 7]], axis=0)
        packed[layer, 576:768, :] = nt_dot(eye, pair).astype(jnp.bfloat16)
        pair = jnp.concatenate([raw_ref[layer, 8], raw_ref[layer, 8]], axis=0)
        packed[layer, 768:960, :] = nt_dot(eye, pair).astype(jnp.bfloat16)
        packed[layer, 960:992, :] = bias_ref[layer]
    slab = ids_ref[0]
    mine_ref[...] = packed[:, pl.ds(pl.multiple_of(slab * HALF, 16), HALF), :]
    other_ref[...] = packed[:, pl.ds(pl.multiple_of((1 - slab) * HALF, 16), HALF), :]


def expand(packed, w_ref, bias_ref):
    low = low_lanes((192, 128))
    zero = jnp.zeros((192, 128), jnp.float32)
    for ty in range(3):
        mid = packed[ty * 192 : (ty + 1) * 192, :].astype(jnp.float32)
        rolled = pltpu.roll(mid, CH, 1)
        begin = 576 if ty < 2 else 768
        last = packed[begin : begin + 192, :].astype(jnp.float32)
        last_rolled = pltpu.roll(last, CH, 1)
        if ty == 1:
            last, last_rolled = last_rolled, last
        blocks = (
            jnp.where(low, rolled, zero),
            mid,
            jnp.where(low, last, rolled),
            jnp.where(low, zero, last_rolled),
        )
        for a, block in enumerate(blocks):
            block = block.astype(jnp.bfloat16)
            for tz in range(3):
                w_ref[ty * 256 + a * CH : ty * 256 + (a + 1) * CH, tz * 128 : (tz + 1) * 128] = block[
                    tz * CH : (tz + 1) * CH
                ]


    terms = packed[960:976, :].astype(jnp.float32)
    bias_ref[...] = jnp.broadcast_to(terms[0:1] + terms[1:2] + terms[2:3], (8, 128))


def spread(state_in, state_out, f_ref, layer):
    d = 2**layer
    low = low_lanes((16, 16, 128))
    for u_at, v_at, low_at, high_at in MOVES[layer]:
        u = state_in[u_at]
        v = state_in[v_at]
        pairs = (
            (low_at, jnp.where(low, u, pltpu.roll(v, CH, 2))),
            (high_at, jnp.where(low, pltpu.roll(u, CH, 2), v)),
        )
        for at, value in pairs:
            state_out[at] = value
            activated = value * (0.5 * jnp.tanh(0.5 * value) + 0.5)
            turned = pltpu.roll(activated, CH, 2).astype(jnp.bfloat16)
            following = NEXT[layer][at]
            for place, lanes in ((at, slice(CH, 128)), (following, slice(0, CH))):
                part = turned[:, :, lanes]
                f_ref[place, 4:20, :, lanes] = part
                f_ref[place, 4 - d : 4, :, lanes] = part[16 - d :]
                f_ref[place, 20 : 20 + d, :, lanes] = part[:d]


def convolve(state, f_ref, w_ref, bias, layer):
    d = 2**layer
    for k in range(8):
        following = NEXT[layer][k]
        columns = []
        for ty in (-1, 0, 1):
            begin = 4 + d * ty
            columns.append(f_ref[k, begin : begin + 16].reshape(256, 128))
            columns.append(f_ref[following, begin : begin + 16].reshape(256, 128))
        product = jnp.dot(jnp.concatenate(columns, axis=1), w_ref[...], preferred_element_type=jnp.float32)
        product = product.reshape(16, 16, 384)
        total = state[k] + bias + product[:, :, 128:256]
        total = total + pltpu.roll(product[:, :, 0:128], d, 1) + pltpu.roll(product[:, :, 256:384], 16 - d, 1)
        if layer == LAYERS - 1:
            total = total.astype(jnp.bfloat16).astype(jnp.float32)
        state[k] = total


def run_section(s_a, s_b, f_ref, w_refs, bias_refs, prepare):
    states = (s_a, s_b)
    for layer in range(LAYERS):
        before, after = states[layer % 2], states[1 - layer % 2]
        prepare(layer)
        spread(before, after, f_ref, layer)
        convolve(after, f_ref, w_refs[layer], bias_refs[layer][0:1][None], layer)
    s_a[...] = s_b[...]


def lift_into(x, lift_ref, s_a):
    high = x.astype(jnp.bfloat16).astype(jnp.float32)
    columns = jnp.concatenate([high, x - high, high], axis=0).T.astype(jnp.bfloat16)
    hidden = jnp.dot(columns, lift_ref[...], preferred_element_type=jnp.float32)
    s_a[...] = hidden.astype(jnp.bfloat16).astype(jnp.float32).reshape(8, 16, 16, 128)


def renewed_fields(x, proj_ref, s_a):
    gain = nt_dot(proj_ref[...], s_a[...].reshape(2048, 128).astype(jnp.bfloat16))
    return x + gain[:16] + gain[16:32] + gain[32:48]


def level_kernel(level, first, last, *refs):
    (ids_ref, o_mine, o_other, r_mine, r_other, x_ref, lift_ref, proj_ref) = refs[:8]
    (w_out, b_out, leaving, x_out, s_a, s_b, f_ref, packed, w_all, b_all, sems) = refs[-11:]
    slab, line = ids_ref[0], ids_ref[1]
    if first:
        lift_into(x_ref[...], lift_ref, s_a)
    else:
        s_a[...] = refs[8][...].astype(jnp.float32)

    def copies(j):
        return (
            pltpu.make_async_copy(w_all.at[j], w_out.at[2 * level + j], sems.at[j, 0]),
            pltpu.make_async_copy(b_all.at[j], b_out.at[2 * level + j], sems.at[j, 1]),
        )

    def section(j, unused):
        def prepare(layer):
            for wanted, (mine, other) in ((True, (o_mine, o_other)), (False, (r_mine, r_other))):

                @pl.when((j == line) == wanted)
                def take(mine=mine, other=other):
                    packed[pl.ds(pl.multiple_of(slab * HALF, 16), HALF), :] = mine[layer]
                    packed[pl.ds(pl.multiple_of((1 - slab) * HALF, 16), HALF), :] = other[layer]

            expand(packed, w_all.at[j, layer], b_all.at[j, layer])

        run_section(s_a, s_b, f_ref, [w_all.at[j, i] for i in range(LAYERS)], [b_all.at[j, i] for i in range(LAYERS)], prepare)
        for copy in copies(j):
            copy.start()
        return 0

    lax.fori_loop(0, 2, section, 0)
    leaving[...] = s_a[...].astype(jnp.bfloat16)
    x_out[...] = renewed_fields(x_ref[...], proj_ref, s_a) if last else x_ref[...]
    for j in range(2):
        for copy in copies(j):
            copy.wait()


def second_kernel(x_ref, lift_ref, proj_ref, w_ref, b_ref, x_out, s_a, s_b, f_ref):
    s = pl.program_id(0)

    @pl.when(s == 0)
    def begin():
        lift_into(x_ref[...], lift_ref, s_a)

    run_section(s_a, s_b, f_ref, [w_ref.at[0, i] for i in range(LAYERS)], [b_ref.at[0, i] for i in range(LAYERS)], lambda layer: None)

    @pl.when(s == pl.num_programs(0) - 1)
    def finish():
        x_out[...] = renewed_fields(x_ref[...], proj_ref, s_a)


def split_terms(matrix):
    first = matrix.astype(jnp.bfloat16)
    rest = matrix - first.astype(jnp.float32)
    second = rest.astype(jnp.bfloat16)
    third = (rest - second.astype(jnp.float32)).astype(jnp.bfloat16)
    return first, second, third


def state_scratch():
    return [
        pltpu.VMEM((8, 16, 16, 128), jnp.float32),
        pltpu.VMEM((8, 16, 16, 128), jnp.float32),
        pltpu.VMEM((8, 24, 16, 128), jnp.bfloat16),
    ]


def shards(fields, anchors, lift_weight, conv_weight, conv_bias, proj_weight):
    segments = lax.axis_size("segment")
    slabs = lax.axis_size("slab")
    segment_id = lax.axis_index("segment")
    slab_id = lax.axis_index("slab")
    crop_count, comps, slab_rows, y_cells, z_cells = fields.shape
    lines = crop_count // slabs
    levels = segments // lines
    line = segment_id % lines
    slot = line * slabs + slab_id
    swap = [(0, 1), (1, 0)]
    vmem = pl.BlockSpec(memory_space=pltpu.VMEM)
    smem = pl.BlockSpec(memory_space=pltpu.SMEM)
    anyspace = pl.BlockSpec(memory_space=pl.ANY)
    params = pltpu.CompilerParams(vmem_limit_bytes=VMEM_BYTES)
    ids = jnp.stack([slab_id, line]).astype(jnp.int32)

    bias = jnp.concatenate([conv_bias[0], conv_bias[0]], axis=1)
    bias = jnp.pad(jnp.stack(split_terms(bias), axis=1), ((0, 0), (0, 29), (0, 0)))
    half_shape = jax.ShapeDtypeStruct((LAYERS, HALF, 128), jnp.bfloat16)
    mine, other = pl.pallas_call(
        pack_kernel,
        out_shape=(half_shape, half_shape),
        in_specs=[smem, vmem, vmem, vmem],
        out_specs=(vmem, vmem),
        scratch_shapes=[pltpu.VMEM((LAYERS, ROWS, 128), jnp.bfloat16)],
        compiler_params=params,
    )(ids, conv_weight[0], bias, jnp.eye(192, dtype=jnp.bfloat16))

    def between_cores(value):
        return lax.ppermute(value, "slab", swap)

    own, crossed = [(mine, other)], []
    for level in range(levels):
        if level > 0:
            pairs = [(s, s - lines) for s in range(lines, segments - lines * (level - 1))]
            mine = lax.ppermute(mine, "segment", pairs)
            own.append((mine, between_cores(mine)))
        got = lax.ppermute(mine, "segment", swap)
        crossed.append((got, between_cores(got)))

    kept = lax.dynamic_index_in_dim(fields, slot, 0, keepdims=False)
    given = lax.dynamic_index_in_dim(fields, line * slabs + (1 - slab_id), 0, keepdims=False)
    got = between_cores(given)
    halves = jnp.where(slab_id == 0, jnp.stack([kept, got]), jnp.stack([got, kept]))
    anchor = lax.dynamic_index_in_dim(anchors, slot, 0, keepdims=False)

    def wave(column, length):
        position = (anchor[column] + jnp.arange(length, dtype=jnp.int32)) % FIELD
        return jnp.sin(2.0 * jnp.pi * position.astype(jnp.float32) / FIELD)

    shape = (2, 2, 4, y_cells, z_cells)
    current = halves.reshape(2, comps, 2, 4, y_cells, z_cells).transpose(2, 1, 3, 0, 4, 5).reshape(6, 2048)
    wave_x = jnp.broadcast_to(wave(0, 2 * slab_rows).reshape(2, 2, 4, 1, 1), shape)
    wave_y = jnp.broadcast_to(wave(1, y_cells)[:, None], shape)
    wave_z = jnp.broadcast_to(wave(2, z_cells), shape)
    waves = jnp.stack([wave_x, wave_y, wave_z]).transpose(2, 0, 3, 1, 4, 5).reshape(6, 2048)
    x = jnp.concatenate([current, waves, jnp.zeros((4, 2048), jnp.float32)], axis=0)

    half = jnp.eye(2, dtype=jnp.float32)
    lift_cur = jnp.einsum("ab,of->afbo", half, lift_weight[:, :comps]).reshape(6, 128)
    lift_wave = jnp.einsum("ab,of->afbo", half, lift_weight[:, comps:]).reshape(6, 128)
    lift = jnp.concatenate([lift_cur, lift_wave, jnp.zeros((4, 128), jnp.float32)], axis=0)
    first, second, unused = split_terms(lift)
    lift = jnp.concatenate([first, first, second], axis=0)
    proj = jnp.einsum("ab,oc->aobc", half, proj_weight).reshape(6, 128)
    proj = jnp.concatenate([proj, jnp.zeros((10, 128), jnp.float32)], axis=0)
    proj = jnp.concatenate(split_terms(proj), axis=0)

    w_shape = jax.ShapeDtypeStruct((segments, LAYERS, 768, 384), jnp.bfloat16)
    b_shape = jax.ShapeDtypeStruct((segments, LAYERS, 8, 128), jnp.float32)
    h_shape = jax.ShapeDtypeStruct((8, 16, 16, 128), jnp.bfloat16)
    x_shape = jax.ShapeDtypeStruct((16, 2048), jnp.float32)
    layer_flops = 2 * 2048 * 768 * 512
    kept = ()
    current = x
    for level in range(levels):
        operands = (ids, *own[level], *crossed[level], current, lift, proj, *kept)
        weights, rows, hidden, current = pl.pallas_call(
            functools.partial(level_kernel, level, level == 0, level == levels - 1),
            out_shape=(w_shape, b_shape, h_shape, x_shape),
            in_specs=[smem] + [vmem] * 7 + ([vmem] + [anyspace] * 2 if kept else []),
            out_specs=(anyspace, anyspace, vmem, vmem),
            scratch_shapes=state_scratch()
            + [
                pltpu.VMEM((ROWS, 128), jnp.bfloat16),
                pltpu.VMEM((2, LAYERS, 768, 384), jnp.bfloat16),
                pltpu.VMEM((2, LAYERS, 8, 128), jnp.float32),
                pltpu.SemaphoreType.DMA((2, 2)),
            ],
            input_output_aliases={9: 0, 10: 1} if kept else {},
            compiler_params=params,
            cost_estimate=pl.CostEstimate(flops=2 * LAYERS * layer_flops, bytes_accessed=4 << 20, transcendentals=0),
        )(*operands)
        kept = (hidden, weights, rows)
    first_result = current
    second_result = pl.pallas_call(
        second_kernel,
        grid=(segments,),
        out_shape=x_shape,
        in_specs=[vmem] * 3
        + [
            pl.BlockSpec((1, LAYERS, 768, 384), lambda s: (s, 0, 0, 0)),
            pl.BlockSpec((1, LAYERS, 8, 128), lambda s: (s, 0, 0, 0)),
        ],
        out_specs=vmem,
        scratch_shapes=state_scratch(),
        compiler_params=params,
        cost_estimate=pl.CostEstimate(flops=segments * LAYERS * layer_flops, bytes_accessed=16 << 20, transcendentals=0),
    )(first_result, lift, proj, weights, rows)

    result = jnp.stack([first_result[:6], second_result[:6]]).astype(jnp.bfloat16)
    result = result.reshape(STEPS, 2, comps, 4, 2, y_cells, z_cells)
    kept = lax.dynamic_index_in_dim(result, slab_id, 4, keepdims=False)
    got = between_cores(lax.dynamic_index_in_dim(result, 1 - slab_id, 4, keepdims=False))
    pair = jnp.where(slab_id == 0, jnp.stack([kept, got]), jnp.stack([got, kept]))
    got = lax.ppermute(pair, "segment", swap)
    crops = jnp.where(line == 0, jnp.concatenate([pair, got]), jnp.concatenate([got, pair]))
    crops = crops.transpose(1, 0, 3, 2, 4, 5, 6)
    crops = crops.reshape(STEPS, crop_count, comps, slab_rows, y_cells, z_cells)
    share = z_cells // segments

    def part_for(target):
        return lax.dynamic_slice_in_dim(crops, target * share, share, 5)

    out = jnp.where(segment_id < lines, part_for(segment_id), 0)
    for level in range(1, levels):
        pairs = [(s, level * lines + s) for s in range(lines)]
        out = out + lax.ppermute(part_for(segment_id + level * lines), "segment", pairs)
    return out.astype(jnp.float32)


def solution(mesh):
    in_specs = (
        P("groups", None, "slab", None, None),
        P("groups", None),
        P(),
        P("segment", None, None, None, None),
        P("segment", None, None),
        P(),
    )
    out_specs = P(None, "groups", None, "slab", None, "segment")
    return jax.shard_map(shards, mesh=mesh, in_specs=in_specs, out_specs=out_specs, check_vma=False)
```

```python
import functools

import jax
import jax.numpy as jnp
from jax import lax
from jax.experimental import pallas as pl
from jax.experimental.pallas import tpu as pltpu
from jax.sharding import PartitionSpec as P

STEPS = 2
FIELD = 4096
LAYERS = 3
CH = 64
ROWS = 992
HALF = ROWS // 2
VMEM_BYTES = 48 * 1024 * 1024

MOVES = (
    [(4 * b + m, 4 * b + 2 + m, 4 * m + b, 4 * m + 2 + b) for m in range(2) for b in range(2)],
    [(2 * m, 2 * m + 1, m, 4 + m) for m in range(4)],
    [(4 * p + 2 * m, 4 * p + 2 * m + 1, 2 * p + m, 2 * (2 + p) + m) for p in range(2) for m in range(2)],
)
NEXT = (
    [(k + 1) % 8 for k in range(8)],
    [4 * (k // 4) + (k % 4 + 1) % 4 for k in range(8)],
    [2 * (k // 2) + (k % 2 + 1) % 2 for k in range(8)],
)


def low_lanes(shape):
    return lax.broadcasted_iota(jnp.int32, shape, len(shape) - 1) < CH


def nt_dot(a, b):
    return lax.dot_general(a, b, (((1,), (1,)), ((), ())), preferred_element_type=jnp.float32)


def pack_kernel(ids_ref, raw_ref, bias_ref, eye_ref, mine_ref, other_ref, packed):
    eye = eye_ref[...]
    for layer in range(LAYERS):
        for ty in range(3):
            pair = jnp.concatenate([raw_ref[layer, 3 + ty], raw_ref[layer, ty]], axis=0)
            packed[layer, ty * 192 : (ty + 1) * 192, :] = nt_dot(eye, pair).astype(jnp.bfloat16)
        pair = jnp.concatenate([raw_ref[layer, 6], raw_ref[layer, 7]], axis=0)
        packed[layer, 576:768, :] = nt_dot(eye, pair).astype(jnp.bfloat16)
        pair = jnp.concatenate([raw_ref[layer, 8], raw_ref[layer, 8]], axis=0)
        packed[layer, 768:960, :] = nt_dot(eye, pair).astype(jnp.bfloat16)
        bias = bias_ref[layer : layer + 1, :]
        terms = jnp.concatenate([term.astype(jnp.float32) for term in split_terms(bias)], axis=0)
        terms = jnp.concatenate([terms, jnp.zeros((29, CH), jnp.float32)], axis=0)
        packed[layer, 960:992, :] = jnp.concatenate([terms, terms], axis=1).astype(jnp.bfloat16)
    slab = ids_ref[0]
    mine_ref[...] = packed[:, pl.ds(pl.multiple_of(slab * HALF, 16), HALF), :]
    other_ref[...] = packed[:, pl.ds(pl.multiple_of((1 - slab) * HALF, 16), HALF), :]


def expand(packed, w_ref, bias_ref):
    low = low_lanes((192, 128))
    zero = jnp.zeros((192, 128), jnp.float32)
    for ty in range(3):
        mid = packed[ty * 192 : (ty + 1) * 192, :].astype(jnp.float32)
        rolled = pltpu.roll(mid, CH, 1)
        begin = 576 if ty < 2 else 768
        last = packed[begin : begin + 192, :].astype(jnp.float32)
        last_rolled = pltpu.roll(last, CH, 1)
        if ty == 1:
            last, last_rolled = last_rolled, last
        blocks = (
            jnp.where(low, rolled, zero),
            mid,
            jnp.where(low, last, rolled),
            jnp.where(low, zero, last_rolled),
        )
        for a, block in enumerate(blocks):
            block = block.astype(jnp.bfloat16)
            for tz in range(3):
                w_ref[ty * 256 + a * CH : ty * 256 + (a + 1) * CH, tz * 128 : (tz + 1) * 128] = block[
                    tz * CH : (tz + 1) * CH
                ]


    terms = packed[960:976, :].astype(jnp.float32)
    bias_ref[...] = jnp.broadcast_to(terms[0:1] + terms[1:2] + terms[2:3], (8, 128))


def spread(state_in, state_out, f_ref, layer):
    d = 2**layer
    low = low_lanes((16, 16, 128))
    for u_at, v_at, low_at, high_at in MOVES[layer]:
        u = state_in[u_at]
        v = state_in[v_at]
        pairs = (
            (low_at, jnp.where(low, u, pltpu.roll(v, CH, 2))),
            (high_at, jnp.where(low, pltpu.roll(u, CH, 2), v)),
        )
        for at, value in pairs:
            state_out[at] = value
            activated = value * (0.5 * jnp.tanh(0.5 * value) + 0.5)
            turned = pltpu.roll(activated, CH, 2).astype(jnp.bfloat16)
            following = NEXT[layer][at]
            for place, lanes in ((at, slice(CH, 128)), (following, slice(0, CH))):
                part = turned[:, :, lanes]
                f_ref[place, 4:20, :, lanes] = part
                f_ref[place, 4 - d : 4, :, lanes] = part[16 - d :]
                f_ref[place, 20 : 20 + d, :, lanes] = part[:d]


def convolve(state, f_ref, w_ref, bias, layer):
    d = 2**layer
    for k in range(8):
        following = NEXT[layer][k]
        columns = []
        for ty in (-1, 0, 1):
            begin = 4 + d * ty
            columns.append(f_ref[k, begin : begin + 16].reshape(256, 128))
            columns.append(f_ref[following, begin : begin + 16].reshape(256, 128))
        product = jnp.dot(jnp.concatenate(columns, axis=1), w_ref[...], preferred_element_type=jnp.float32)
        product = product.reshape(16, 16, 384)
        total = state[k] + bias + product[:, :, 128:256]
        total = total + pltpu.roll(product[:, :, 0:128], d, 1) + pltpu.roll(product[:, :, 256:384], 16 - d, 1)
        if layer == LAYERS - 1:
            total = total.astype(jnp.bfloat16).astype(jnp.float32)
        state[k] = total


def run_section(s_a, s_b, f_ref, w_refs, bias_refs, prepare):
    states = (s_a, s_b)
    for layer in range(LAYERS):
        before, after = states[layer % 2], states[1 - layer % 2]
        prepare(layer)
        spread(before, after, f_ref, layer)
        convolve(after, f_ref, w_refs[layer], bias_refs[layer][0:1][None], layer)
    s_a[...] = s_b[...]


def lift_into(x, lift_ref, s_a):
    high = x.astype(jnp.bfloat16).astype(jnp.float32)
    columns = jnp.concatenate([high, x - high, high], axis=0).T.astype(jnp.bfloat16)
    hidden = jnp.dot(columns, lift_ref[...], preferred_element_type=jnp.float32)
    s_a[...] = hidden.astype(jnp.bfloat16).astype(jnp.float32).reshape(8, 16, 16, 128)


def renewed_fields(x, proj_ref, s_a):
    gain = nt_dot(proj_ref[...], s_a[...].reshape(2048, 128).astype(jnp.bfloat16))
    return x + gain[:16] + gain[16:32] + gain[32:48]


def section_kernel(section, turn, first, last, *refs):
    (ids_ref, o_mine, o_other, r_mine, r_other, x_ref, lift_ref, proj_ref) = refs[:8]
    (w_out, b_out, leaving, x_out, s_a, s_b, f_ref, packed, w_all, b_all, sems) = refs[-11:]
    slab, line = ids_ref[0], ids_ref[1]
    if first:
        lift_into(x_ref[...], lift_ref, s_a)
    else:
        s_a[...] = refs[8][...].astype(jnp.float32)
    copies = [pltpu.make_async_copy(w_all.at[i], w_out.at[section, i], sems.at[i]) for i in range(LAYERS)]
    copies.append(pltpu.make_async_copy(b_all, b_out.at[section], sems.at[LAYERS]))

    def prepare(layer):
        for wanted, (mine, other) in ((True, (o_mine, o_other)), (False, (r_mine, r_other))):

            @pl.when((turn == line) == wanted)
            def take(mine=mine, other=other):
                packed[pl.ds(pl.multiple_of(slab * HALF, 16), HALF), :] = mine[layer]
                packed[pl.ds(pl.multiple_of((1 - slab) * HALF, 16), HALF), :] = other[layer]

        expand(packed, w_all.at[layer], b_all.at[layer])
        copies[layer].start()

    run_section(s_a, s_b, f_ref, [w_all.at[i] for i in range(LAYERS)], [b_all.at[i] for i in range(LAYERS)], prepare)
    copies[LAYERS].start()
    leaving[...] = s_a[...].astype(jnp.bfloat16)
    x_out[...] = renewed_fields(x_ref[...], proj_ref, s_a) if last else x_ref[...]
    for copy in copies:
        copy.wait()


def cells_in_rows(both, half):
    blocks = []
    for x_ref in both:
        for r in range(4):
            for upper in range(2):
                begin = pl.multiple_of(((2 * r + half) * 2 + upper) * 128, 128)
                blocks.append(x_ref[0:8, pl.ds(begin, 128)])
    row = lax.broadcasted_iota(jnp.int32, (128, 128), 0)
    lane = lax.broadcasted_iota(jnp.int32, (128, 128), 1)
    turned = ((row >> 3) == (lane & 15)) & ((row & 7) == (lane >> 4))
    turned = jnp.where(turned, 1.0, 0.0).astype(jnp.bfloat16)
    return nt_dot(turned, jnp.concatenate(blocks, axis=0).astype(jnp.bfloat16)).astype(jnp.bfloat16)


def second_kernel(ids_ref, x_ref, lift_ref, proj_ref, w_ref, b_ref, kept, given, s_a, s_b, f_ref, x_new):
    s = pl.program_id(0)

    @pl.when(s == 0)
    def begin():
        lift_into(x_ref[...], lift_ref, s_a)

    run_section(s_a, s_b, f_ref, [w_ref.at[0, i] for i in range(LAYERS)], [b_ref.at[0, i] for i in range(LAYERS)], lambda layer: None)

    @pl.when(s == pl.num_programs(0) - 1)
    def finish():
        x_new[...] = renewed_fields(x_ref[...], proj_ref, s_a)
        kept[...] = cells_in_rows((x_ref, x_new), ids_ref[0])
        given[...] = cells_in_rows((x_ref, x_new), 1 - ids_ref[0])


def split_terms(matrix):
    first = matrix.astype(jnp.bfloat16)
    rest = matrix - first.astype(jnp.float32)
    second = rest.astype(jnp.bfloat16)
    third = (rest - second.astype(jnp.float32)).astype(jnp.bfloat16)
    return first, second, third


def state_scratch():
    return [
        pltpu.VMEM((8, 16, 16, 128), jnp.float32),
        pltpu.VMEM((8, 16, 16, 128), jnp.float32),
        pltpu.VMEM((8, 24, 16, 128), jnp.bfloat16),
    ]


def shards(fields, anchors, lift_weight, conv_weight, conv_bias, proj_weight):
    segments = lax.axis_size("segment")
    slabs = lax.axis_size("slab")
    segment_id = lax.axis_index("segment")
    slab_id = lax.axis_index("slab")
    crop_count, comps, slab_rows, y_cells, z_cells = fields.shape
    lines = crop_count // slabs
    levels = segments // lines
    line = segment_id % lines
    slot = line * slabs + slab_id
    swap = [(0, 1), (1, 0)]
    vmem = pl.BlockSpec(memory_space=pltpu.VMEM)
    smem = pl.BlockSpec(memory_space=pltpu.SMEM)
    anyspace = pl.BlockSpec(memory_space=pl.ANY)
    params = pltpu.CompilerParams(vmem_limit_bytes=VMEM_BYTES)
    ids = jnp.stack([slab_id, line]).astype(jnp.int32)

    half_shape = jax.ShapeDtypeStruct((LAYERS, HALF, 128), jnp.bfloat16)
    mine, other = pl.pallas_call(
        pack_kernel,
        out_shape=(half_shape, half_shape),
        in_specs=[smem, vmem, vmem, vmem],
        out_specs=(vmem, vmem),
        scratch_shapes=[pltpu.VMEM((LAYERS, ROWS, 128), jnp.bfloat16)],
        compiler_params=params,
    )(ids, conv_weight[0], conv_bias[0], jnp.eye(192, dtype=jnp.bfloat16))

    def between_cores(value):
        return lax.ppermute(value, "slab", swap)

    kept = lax.dynamic_index_in_dim(fields, slot, 0, keepdims=False)
    given = lax.dynamic_index_in_dim(fields, line * slabs + (1 - slab_id), 0, keepdims=False)
    got = between_cores(given)
    halves = jnp.where(slab_id == 0, jnp.stack([kept, got]), jnp.stack([got, kept]))
    anchor = lax.dynamic_index_in_dim(anchors, slot, 0, keepdims=False)

    def wave(column, length):
        position = (anchor[column] + jnp.arange(length, dtype=jnp.int32)) % FIELD
        return jnp.sin(2.0 * jnp.pi * position.astype(jnp.float32) / FIELD)

    shape = (2, 2, 4, y_cells, z_cells)
    current = halves.reshape(2, comps, 2, 4, y_cells, z_cells).transpose(2, 1, 3, 0, 4, 5).reshape(6, 2048)
    wave_x = jnp.broadcast_to(wave(0, 2 * slab_rows).reshape(2, 2, 4, 1, 1), shape)
    wave_y = jnp.broadcast_to(wave(1, y_cells)[:, None], shape)
    wave_z = jnp.broadcast_to(wave(2, z_cells), shape)
    waves = jnp.stack([wave_x, wave_y, wave_z]).transpose(2, 0, 3, 1, 4, 5).reshape(6, 2048)
    x = jnp.concatenate([current, waves, jnp.zeros((4, 2048), jnp.float32)], axis=0)

    half = jnp.eye(2, dtype=jnp.float32)
    lift_cur = jnp.einsum("ab,of->afbo", half, lift_weight[:, :comps]).reshape(6, 128)
    lift_wave = jnp.einsum("ab,of->afbo", half, lift_weight[:, comps:]).reshape(6, 128)
    lift = jnp.concatenate([lift_cur, lift_wave, jnp.zeros((4, 128), jnp.float32)], axis=0)
    first, second, unused = split_terms(lift)
    lift = jnp.concatenate([first, first, second], axis=0)
    proj = jnp.einsum("ab,oc->aobc", half, proj_weight).reshape(6, 128)
    proj = jnp.concatenate([proj, jnp.zeros((10, 128), jnp.float32)], axis=0)
    proj = jnp.concatenate(split_terms(proj), axis=0)

    w_shape = jax.ShapeDtypeStruct((segments, LAYERS, 768, 384), jnp.bfloat16)
    b_shape = jax.ShapeDtypeStruct((segments, LAYERS, 8, 128), jnp.float32)
    h_shape = jax.ShapeDtypeStruct((8, 16, 16, 128), jnp.bfloat16)
    x_shape = jax.ShapeDtypeStruct((16, 2048), jnp.float32)
    layer_flops = 2 * 2048 * 768 * 512
    above, across = {0: mine}, {}
    own, crossed = {0: (mine, other)}, {}

    def descend(level):
        pairs = [(s, s - lines) for s in range(lines, segments - lines * (level - 1))]
        above[level] = lax.ppermute(above[level - 1], "segment", pairs)

    def cross(level):
        across[level] = lax.ppermute(above[level], "segment", swap)

    def fill_own(level):
        own[level] = (above[level], between_cores(above[level]))

    def fill_crossed(level):
        crossed[level] = (across[level], between_cores(across[level]))

    def after(value, *earlier):
        return lax.optimization_barrier((value, *earlier))[0]

    cross(0)
    descend(1)
    fill_crossed(0)
    fill_own(1)
    cross(1)
    kept = ()
    current = x
    for section in range(segments):
        level, turn = section // lines, section % lines
        operands = (ids, *own[level], *crossed[level], current, lift, proj, *kept)
        weights, rows, hidden, current = pl.pallas_call(
            functools.partial(section_kernel, section, turn, section == 0, section == segments - 1),
            out_shape=(w_shape, b_shape, h_shape, x_shape),
            in_specs=[smem] + [vmem] * 7 + ([vmem] + [anyspace] * 2 if kept else []),
            out_specs=(anyspace, anyspace, vmem, vmem),
            scratch_shapes=state_scratch()
            + [
                pltpu.VMEM((ROWS, 128), jnp.bfloat16),
                pltpu.VMEM((LAYERS, 768, 384), jnp.bfloat16),
                pltpu.VMEM((LAYERS, 8, 128), jnp.float32),
                pltpu.SemaphoreType.DMA((LAYERS + 1,)),
            ],
            input_output_aliases={9: 0, 10: 1} if kept else {},
            compiler_params=params,
            cost_estimate=pl.CostEstimate(flops=LAYERS * layer_flops, bytes_accessed=4 << 20, transcendentals=0),
        )(*operands)
        kept = (hidden, weights, rows)
        if turn == 0 and level + 1 < levels:
            across[level + 1] = after(across[level + 1], hidden)
            fill_crossed(level + 1)
            if level + 2 < levels:
                above[level + 1] = after(above[level + 1], hidden)
                descend(level + 2)
        elif turn == 1 and level + 2 < levels:
            above[level + 2] = after(above[level + 2], hidden)
            fill_own(level + 2)
            cross(level + 2)
    first_result = current
    kept, given = pl.pallas_call(
        second_kernel,
        grid=(segments,),
        out_shape=(jax.ShapeDtypeStruct((128, 128), jnp.bfloat16),) * 2,
        in_specs=[smem]
        + [vmem] * 3
        + [
            pl.BlockSpec((1, LAYERS, 768, 384), lambda s: (s, 0, 0, 0)),
            pl.BlockSpec((1, LAYERS, 8, 128), lambda s: (s, 0, 0, 0)),
        ],
        out_specs=(vmem, vmem),
        scratch_shapes=state_scratch() + [pltpu.VMEM((16, 2048), jnp.float32)],
        compiler_params=params,
        cost_estimate=pl.CostEstimate(flops=segments * LAYERS * layer_flops, bytes_accessed=16 << 20, transcendentals=0),
    )(ids, first_result, lift, proj, weights, rows)

    got = between_cores(given)
    pair = jnp.where(slab_id == 0, jnp.stack([kept, got]), jnp.stack([got, kept]))
    got = lax.ppermute(pair, "segment", swap)
    crops = jnp.where(line == 0, jnp.concatenate([pair, got]), jnp.concatenate([got, pair]))
    share = z_cells // segments

    def part_for(target):
        return lax.dynamic_slice_in_dim(crops, target * share * 8, share * 8, 1)

    out = jnp.where(segment_id < lines, part_for(segment_id), 0)
    for level in range(1, levels):
        pairs = [(s, level * lines + s) for s in range(lines)]
        out = out + lax.ppermute(part_for(segment_id + level * lines), "segment", pairs)
    out = out.reshape(crop_count, share, 8, STEPS, 4, 2, 8)[..., : 2 * comps]
    out = out.reshape(crop_count, share, 8, STEPS, 4, 2, 2, comps).transpose(3, 0, 7, 6, 4, 5, 2, 1)
    return out.reshape(STEPS, crop_count, comps, slab_rows, y_cells, share).astype(jnp.float32)


def solution(mesh):
    in_specs = (
        P("groups", None, "slab", None, None),
        P("groups", None),
        P(),
        P("segment", None, None, None, None),
        P("segment", None, None),
        P(),
    )
    out_specs = P(None, "groups", None, "slab", None, "segment")
    return jax.shard_map(shards, mesh=mesh, in_specs=in_specs, out_specs=out_specs, check_vma=False)
```

```python
import functools

import jax
import jax.numpy as jnp
from jax import lax
from jax.experimental import pallas as pl
from jax.experimental.pallas import tpu as pltpu
from jax.sharding import PartitionSpec as P

STEPS = 2
FIELD = 4096
LAYERS = 3
CH = 64
ROWS = 992
HALF = ROWS // 2
VMEM_BYTES = 48 * 1024 * 1024

MOVES = (
    [(4 * b + m, 4 * b + 2 + m, 4 * m + b, 4 * m + 2 + b) for b in range(2) for m in range(2)],
    [(2 * m, 2 * m + 1, m, 4 + m) for m in range(4)],
    [(4 * p + 2 * m, 4 * p + 2 * m + 1, 2 * p + m, 2 * (2 + p) + m) for p in range(2) for m in range(2)],
)
CYCLES = (
    [list(range(8))],
    [list(range(4)), list(range(4, 8))],
    [[2 * r, 2 * r + 1] for r in range(4)],
)


def neighbour(layer, tile, step):
    cycle = next(cycle for cycle in CYCLES[layer] if tile in cycle)
    return cycle[(cycle.index(tile) + step) % len(cycle)]


def low_lanes(shape):
    return lax.broadcasted_iota(jnp.int32, shape, len(shape) - 1) < CH


def nt_dot(a, b):
    return lax.dot_general(a, b, (((1,), (1,)), ((), ())), preferred_element_type=jnp.float32)


def pack_kernel(ids_ref, raw_ref, bias_ref, eye_ref, mine_ref, other_ref, packed):
    eye = eye_ref[...]
    for layer in range(LAYERS):
        for ty in range(3):
            pair = jnp.concatenate([raw_ref[layer, 3 + ty], raw_ref[layer, ty]], axis=0)
            packed[layer, ty * 192 : (ty + 1) * 192, :] = nt_dot(eye, pair).astype(jnp.bfloat16)
        pair = jnp.concatenate([raw_ref[layer, 6], raw_ref[layer, 7]], axis=0)
        packed[layer, 576:768, :] = nt_dot(eye, pair).astype(jnp.bfloat16)
        pair = jnp.concatenate([raw_ref[layer, 8], raw_ref[layer, 8]], axis=0)
        packed[layer, 768:960, :] = nt_dot(eye, pair).astype(jnp.bfloat16)
        bias = bias_ref[layer : layer + 1, :]
        terms = jnp.concatenate([term.astype(jnp.float32) for term in split_terms(bias)], axis=0)
        terms = jnp.concatenate([terms, jnp.zeros((29, CH), jnp.float32)], axis=0)
        packed[layer, 960:992, :] = jnp.concatenate([terms, terms], axis=1).astype(jnp.bfloat16)
    slab = ids_ref[0]
    mine_ref[...] = packed[:, pl.ds(pl.multiple_of(slab * HALF, 16), HALF), :]
    other_ref[...] = packed[:, pl.ds(pl.multiple_of((1 - slab) * HALF, 16), HALF), :]


def combined(taps):
    before, here, behind = taps
    ends = 0.5 * (before + behind)
    return before, ends + 0.5 * here, ends - 0.5 * here, behind


def expand(packed, w_ref, bias_ref):
    low = low_lanes((192, 128))
    zero = jnp.zeros((192, 128), jnp.float32)
    mids = combined([packed[ty * 192 : (ty + 1) * 192, :].astype(jnp.float32) for ty in range(3)])
    both = packed[576:768, :].astype(jnp.float32)
    lasts = combined([both, pltpu.roll(both, CH, 1), packed[768:960, :].astype(jnp.float32)])
    for index, (mid, last) in enumerate(zip(mids, lasts)):
        rolled = pltpu.roll(mid, CH, 1)
        blocks = (
            mid,
            jnp.where(low, last, rolled),
            jnp.where(low, zero, pltpu.roll(last, CH, 1)),
            jnp.where(low, rolled, zero),
        )
        for a, block in enumerate(blocks):
            block = block.astype(jnp.bfloat16)
            for tz in range(3):
                w_ref[index, a * CH : (a + 1) * CH, tz * 128 : (tz + 1) * 128] = block[tz * CH : (tz + 1) * CH]
    terms = packed[960:976, :].astype(jnp.float32)
    bias_ref[...] = jnp.broadcast_to(terms[0:1] + terms[1:2] + terms[2:3], (8, 128))


def activate_into(v_ref, tile, value, layer):
    d = 2**layer
    activated = value * (0.5 * jnp.tanh(0.5 * value) + 0.5)
    pairs = activated.reshape(8 // d, 2, d, 16, 128)
    first, second = pairs[:, 0], pairs[:, 1]
    before = jnp.concatenate([second[-1:], second[:-1]], axis=0)
    behind = jnp.concatenate([first[1:], first[:1]], axis=0)
    mixed = (before - second, first + second, second - first, first - behind)
    for index, value in enumerate(mixed):
        v_ref[index, tile] = value.reshape(128, 128).astype(jnp.bfloat16)


def spread(move, u, v, state_out, v_ref, layer):
    low = low_lanes((16, 16, 128))
    for at, value in (
        (move[2], jnp.where(low, u, pltpu.roll(v, CH, 2))),
        (move[3], jnp.where(low, pltpu.roll(u, CH, 2), v)),
    ):
        state_out[at] = value
        activate_into(v_ref, at, value, layer)


def convolve(v_ref, w_ref, tiles, layer):
    d = 2**layer
    low = low_lanes((128, 128))
    products = []
    for index in range(4):
        rows = []
        for tile in tiles:
            after = v_ref[index, neighbour(layer, tile, 1)]
            before = v_ref[index, neighbour(layer, tile, -1)]
            rows.append(jnp.concatenate([v_ref[index, tile], jnp.where(low, after, before)], axis=1))
        rows = jnp.concatenate(rows, axis=0)
        products.append(jnp.dot(rows, w_ref[index], preferred_element_type=jnp.float32))
    first = products[0] + products[1] + products[2]
    second = products[1] - products[2] - products[3]
    results = []
    for at in range(len(tiles)):
        halves = []
        for half in (first, second):
            half = half[at * 128 : (at + 1) * 128].reshape(8, 16, 384)
            total = half[:, :, 128:256] + pltpu.roll(half[:, :, 0:128], d, 1) + pltpu.roll(half[:, :, 256:384], 16 - d, 1)
            halves.append(total.reshape(8 // d, 1, d, 16, 128))
        results.append(jnp.concatenate(halves, axis=1).reshape(16, 16, 128))
    return results


def run_section(state, v_refs, w_refs, bias_refs, prepare):
    s_a, s_b, s_c = state
    for move in MOVES[0]:
        spread(move, s_a[move[0]], s_a[move[1]], s_b, v_refs[0], 0)
    prepare(0)
    for layer in range(LAYERS):
        held, following = (s_b, s_c)[layer % 2], (s_c, s_b)[layer % 2]
        if layer + 1 < LAYERS:
            prepare(layer + 1)
        bias = bias_refs[layer][0:1][None]
        moves = MOVES[(layer + 1) % LAYERS]
        for chosen in (moves[0:2], moves[2:4]):
            tiles = [tile for move in chosen for tile in move[:2]]
            sums = convolve(v_refs[layer % 2], w_refs[layer], tiles, layer)
            sums = [held[tile] + bias + total for tile, total in zip(tiles, sums)]
            if layer + 1 < LAYERS:
                for at, move in enumerate(chosen):
                    spread(move, sums[2 * at], sums[2 * at + 1], following, v_refs[(layer + 1) % 2], layer + 1)
            else:
                for tile, total in zip(tiles, sums):
                    s_a[tile] = total.astype(jnp.bfloat16).astype(jnp.float32)


def lift_into(x, lift_ref, s_a):
    high = x.astype(jnp.bfloat16).astype(jnp.float32)
    columns = jnp.concatenate([high, x - high, high], axis=0).T.astype(jnp.bfloat16)
    hidden = jnp.dot(columns, lift_ref[...], preferred_element_type=jnp.float32)
    s_a[...] = hidden.astype(jnp.bfloat16).astype(jnp.float32).reshape(8, 16, 16, 128)


def renewed_fields(x, proj_ref, s_a):
    gain = nt_dot(proj_ref[...], s_a[...].reshape(2048, 128).astype(jnp.bfloat16))
    return x + gain[:16] + gain[16:32] + gain[32:48]


def section_kernel(section, turn, first, last, *refs):
    (ids_ref, o_mine, o_other, r_mine, r_other, x_ref, lift_ref, proj_ref) = refs[:8]
    (w_out, b_out, leaving, x_out, s_a, s_b, s_c, v_a, v_b, packed, w_all, b_all, sems) = refs[-13:]
    slab, line = ids_ref[0], ids_ref[1]
    if first:
        lift_into(x_ref[...], lift_ref, s_a)
    else:
        s_a[...] = refs[8][...].astype(jnp.float32)
    copies = [pltpu.make_async_copy(w_all.at[i], w_out.at[section, i], sems.at[i]) for i in range(LAYERS)]
    copies.append(pltpu.make_async_copy(b_all, b_out.at[section], sems.at[LAYERS]))

    def prepare(layer):
        for wanted, (mine, other) in ((True, (o_mine, o_other)), (False, (r_mine, r_other))):

            @pl.when((turn == line) == wanted)
            def take(mine=mine, other=other):
                packed[pl.ds(pl.multiple_of(slab * HALF, 16), HALF), :] = mine[layer]
                packed[pl.ds(pl.multiple_of((1 - slab) * HALF, 16), HALF), :] = other[layer]

        expand(packed, w_all.at[layer], b_all.at[layer])
        copies[layer].start()

    run_section((s_a, s_b, s_c), (v_a, v_b), [w_all.at[i] for i in range(LAYERS)], [b_all.at[i] for i in range(LAYERS)], prepare)
    copies[LAYERS].start()
    leaving[...] = s_a[...].astype(jnp.bfloat16)
    x_out[...] = renewed_fields(x_ref[...], proj_ref, s_a) if last else x_ref[...]
    for copy in copies:
        copy.wait()


def cells_in_rows(both, half):
    blocks = []
    for x_ref in both:
        for r in range(4):
            for upper in range(2):
                begin = pl.multiple_of(((2 * r + half) * 2 + upper) * 128, 128)
                blocks.append(x_ref[0:8, pl.ds(begin, 128)])
    row = lax.broadcasted_iota(jnp.int32, (128, 128), 0)
    lane = lax.broadcasted_iota(jnp.int32, (128, 128), 1)
    turned = ((row >> 3) == (lane & 15)) & ((row & 7) == (lane >> 4))
    turned = jnp.where(turned, 1.0, 0.0).astype(jnp.bfloat16)
    return nt_dot(turned, jnp.concatenate(blocks, axis=0).astype(jnp.bfloat16)).astype(jnp.bfloat16)


def second_kernel(ids_ref, x_ref, lift_ref, proj_ref, w_ref, b_ref, kept, given, s_a, s_b, s_c, v_a, v_b, x_new):
    s = pl.program_id(0)

    @pl.when(s == 0)
    def begin():
        lift_into(x_ref[...], lift_ref, s_a)

    run_section((s_a, s_b, s_c), (v_a, v_b), [w_ref.at[0, i] for i in range(LAYERS)], [b_ref.at[0, i] for i in range(LAYERS)], lambda layer: None)

    @pl.when(s == pl.num_programs(0) - 1)
    def finish():
        x_new[...] = renewed_fields(x_ref[...], proj_ref, s_a)
        kept[...] = cells_in_rows((x_ref, x_new), ids_ref[0])
        given[...] = cells_in_rows((x_ref, x_new), 1 - ids_ref[0])


def split_terms(matrix):
    first = matrix.astype(jnp.bfloat16)
    rest = matrix - first.astype(jnp.float32)
    second = rest.astype(jnp.bfloat16)
    third = (rest - second.astype(jnp.float32)).astype(jnp.bfloat16)
    return first, second, third


def state_scratch():
    return [pltpu.VMEM((8, 16, 16, 128), jnp.float32)] * 3 + [pltpu.VMEM((4, 8, 128, 128), jnp.bfloat16)] * 2


def shards(fields, anchors, lift_weight, conv_weight, conv_bias, proj_weight):
    segments = lax.axis_size("segment")
    slabs = lax.axis_size("slab")
    segment_id = lax.axis_index("segment")
    slab_id = lax.axis_index("slab")
    crop_count, comps, slab_rows, y_cells, z_cells = fields.shape
    lines = crop_count // slabs
    levels = segments // lines
    line = segment_id % lines
    slot = line * slabs + slab_id
    swap = [(0, 1), (1, 0)]
    vmem = pl.BlockSpec(memory_space=pltpu.VMEM)
    smem = pl.BlockSpec(memory_space=pltpu.SMEM)
    anyspace = pl.BlockSpec(memory_space=pl.ANY)
    params = pltpu.CompilerParams(vmem_limit_bytes=VMEM_BYTES)
    ids = jnp.stack([slab_id, line]).astype(jnp.int32)

    half_shape = jax.ShapeDtypeStruct((LAYERS, HALF, 128), jnp.bfloat16)
    mine, other = pl.pallas_call(
        pack_kernel,
        out_shape=(half_shape, half_shape),
        in_specs=[smem, vmem, vmem, vmem],
        out_specs=(vmem, vmem),
        scratch_shapes=[pltpu.VMEM((LAYERS, ROWS, 128), jnp.bfloat16)],
        compiler_params=params,
    )(ids, conv_weight[0], conv_bias[0], jnp.eye(192, dtype=jnp.bfloat16))

    def between_cores(value):
        return lax.ppermute(value, "slab", swap)

    kept = lax.dynamic_index_in_dim(fields, slot, 0, keepdims=False)
    given = lax.dynamic_index_in_dim(fields, line * slabs + (1 - slab_id), 0, keepdims=False)
    got = between_cores(given)
    halves = jnp.where(slab_id == 0, jnp.stack([kept, got]), jnp.stack([got, kept]))
    anchor = lax.dynamic_index_in_dim(anchors, slot, 0, keepdims=False)

    def wave(column, length):
        position = (anchor[column] + jnp.arange(length, dtype=jnp.int32)) % FIELD
        return jnp.sin(2.0 * jnp.pi * position.astype(jnp.float32) / FIELD)

    shape = (2, 2, 4, y_cells, z_cells)
    current = halves.reshape(2, comps, 2, 4, y_cells, z_cells).transpose(2, 1, 3, 0, 4, 5).reshape(6, 2048)
    wave_x = jnp.broadcast_to(wave(0, 2 * slab_rows).reshape(2, 2, 4, 1, 1), shape)
    wave_y = jnp.broadcast_to(wave(1, y_cells)[:, None], shape)
    wave_z = jnp.broadcast_to(wave(2, z_cells), shape)
    waves = jnp.stack([wave_x, wave_y, wave_z]).transpose(2, 0, 3, 1, 4, 5).reshape(6, 2048)
    x = jnp.concatenate([current, waves, jnp.zeros((4, 2048), jnp.float32)], axis=0)

    half = jnp.eye(2, dtype=jnp.float32)
    lift_cur = jnp.einsum("ab,of->afbo", half, lift_weight[:, :comps]).reshape(6, 128)
    lift_wave = jnp.einsum("ab,of->afbo", half, lift_weight[:, comps:]).reshape(6, 128)
    lift = jnp.concatenate([lift_cur, lift_wave, jnp.zeros((4, 128), jnp.float32)], axis=0)
    first, second, unused = split_terms(lift)
    lift = jnp.concatenate([first, first, second], axis=0)
    proj = jnp.einsum("ab,oc->aobc", half, proj_weight).reshape(6, 128)
    proj = jnp.concatenate([proj, jnp.zeros((10, 128), jnp.float32)], axis=0)
    proj = jnp.concatenate(split_terms(proj), axis=0)

    w_shape = jax.ShapeDtypeStruct((segments, LAYERS, 4, 256, 384), jnp.bfloat16)
    b_shape = jax.ShapeDtypeStruct((segments, LAYERS, 8, 128), jnp.float32)
    h_shape = jax.ShapeDtypeStruct((8, 16, 16, 128), jnp.bfloat16)
    x_shape = jax.ShapeDtypeStruct((16, 2048), jnp.float32)
    layer_flops = 2 * 4 * 1024 * 256 * 512
    above, across = {0: mine}, {}
    own, crossed = {0: (mine, other)}, {}

    def descend(level):
        pairs = [(s, s - lines) for s in range(lines, segments - lines * (level - 1))]
        above[level] = lax.ppermute(above[level - 1], "segment", pairs)

    def cross(level):
        across[level] = lax.ppermute(above[level], "segment", swap)

    def fill_own(level):
        own[level] = (above[level], between_cores(above[level]))

    def fill_crossed(level):
        crossed[level] = (across[level], between_cores(across[level]))

    def after(value, *earlier):
        return lax.optimization_barrier((value, *earlier))[0]

    cross(0)
    descend(1)
    fill_crossed(0)
    fill_own(1)
    cross(1)
    kept = ()
    current = x
    for section in range(segments):
        level, turn = section // lines, section % lines
        operands = (ids, *own[level], *crossed[level], current, lift, proj, *kept)
        weights, rows, hidden, current = pl.pallas_call(
            functools.partial(section_kernel, section, turn, section == 0, section == segments - 1),
            out_shape=(w_shape, b_shape, h_shape, x_shape),
            in_specs=[smem] + [vmem] * 7 + ([vmem] + [anyspace] * 2 if kept else []),
            out_specs=(anyspace, anyspace, vmem, vmem),
            scratch_shapes=state_scratch()
            + [
                pltpu.VMEM((ROWS, 128), jnp.bfloat16),
                pltpu.VMEM((LAYERS, 4, 256, 384), jnp.bfloat16),
                pltpu.VMEM((LAYERS, 8, 128), jnp.float32),
                pltpu.SemaphoreType.DMA((LAYERS + 1,)),
            ],
            input_output_aliases={9: 0, 10: 1} if kept else {},
            compiler_params=params,
            cost_estimate=pl.CostEstimate(flops=LAYERS * layer_flops, bytes_accessed=4 << 20, transcendentals=0),
        )(*operands)
        kept = (hidden, weights, rows)
        if turn == 0 and level + 1 < levels:
            across[level + 1] = after(across[level + 1], hidden)
            fill_crossed(level + 1)
            if level + 2 < levels:
                above[level + 1] = after(above[level + 1], hidden)
                descend(level + 2)
        elif turn == 1 and level + 2 < levels:
            above[level + 2] = after(above[level + 2], hidden)
            fill_own(level + 2)
            cross(level + 2)
    first_result = current
    kept, given = pl.pallas_call(
        second_kernel,
        grid=(segments,),
        out_shape=(jax.ShapeDtypeStruct((128, 128), jnp.bfloat16),) * 2,
        in_specs=[smem]
        + [vmem] * 3
        + [
            pl.BlockSpec((1, LAYERS, 4, 256, 384), lambda s: (s, 0, 0, 0, 0)),
            pl.BlockSpec((1, LAYERS, 8, 128), lambda s: (s, 0, 0, 0)),
        ],
        out_specs=(vmem, vmem),
        scratch_shapes=state_scratch() + [pltpu.VMEM((16, 2048), jnp.float32)],
        compiler_params=params,
        cost_estimate=pl.CostEstimate(flops=segments * LAYERS * layer_flops, bytes_accessed=16 << 20, transcendentals=0),
    )(ids, first_result, lift, proj, weights, rows)

    got = between_cores(given)
    pair = jnp.where(slab_id == 0, jnp.stack([kept, got]), jnp.stack([got, kept]))
    got = lax.ppermute(pair, "segment", swap)
    crops = jnp.where(line == 0, jnp.concatenate([pair, got]), jnp.concatenate([got, pair]))
    share = z_cells // segments

    def part_for(target):
        return lax.dynamic_slice_in_dim(crops, target * share * 8, share * 8, 1)

    out = jnp.where(segment_id < lines, part_for(segment_id), 0)
    for level in range(1, levels):
        pairs = [(s, level * lines + s) for s in range(lines)]
        out = out + lax.ppermute(part_for(segment_id + level * lines), "segment", pairs)
    out = out.reshape(crop_count, share, 8, STEPS, 4, 2, 8)[..., : 2 * comps]
    out = out.reshape(crop_count, share, 8, STEPS, 4, 2, 2, comps).transpose(3, 0, 7, 6, 4, 5, 2, 1)
    return out.reshape(STEPS, crop_count, comps, slab_rows, y_cells, share).astype(jnp.float32)


def solution(mesh):
    in_specs = (
        P("groups", None, "slab", None, None),
        P("groups", None),
        P(),
        P("segment", None, None, None, None),
        P("segment", None, None),
        P(),
    )
    out_specs = P(None, "groups", None, "slab", None, "segment")
    return jax.shard_map(shards, mesh=mesh, in_specs=in_specs, out_specs=out_specs, check_vma=False)
```

```python
import functools

import jax
import jax.numpy as jnp
from jax import lax
from jax.experimental import pallas as pl
from jax.experimental.pallas import tpu as pltpu
from jax.sharding import PartitionSpec as P

STEPS = 2
FIELD = 4096
LAYERS = 3
CH = 64
ROWS = 896
VMEM_BYTES = 48 * 1024 * 1024

MOVES = (
    [(4 * b + m, 4 * b + 2 + m, 4 * m + b, 4 * m + 2 + b) for b in range(2) for m in range(2)],
    [(2 * m, 2 * m + 1, m, 4 + m) for m in range(4)],
    [(4 * p + 2 * m, 4 * p + 2 * m + 1, 2 * p + m, 2 * (2 + p) + m) for p in range(2) for m in range(2)],
)
CYCLES = (
    [list(range(8))],
    [list(range(4)), list(range(4, 8))],
    [[2 * r, 2 * r + 1] for r in range(4)],
)


def neighbour(layer, tile, step):
    cycle = next(cycle for cycle in CYCLES[layer] if tile in cycle)
    return cycle[(cycle.index(tile) + step) % len(cycle)]


def low_lanes(shape):
    return lax.broadcasted_iota(jnp.int32, shape, len(shape) - 1) < CH


def nt_dot(a, b):
    return lax.dot_general(a, b, (((1,), (1,)), ((), ())), preferred_element_type=jnp.float32)


def pack_kernel(raw_ref, bias_ref, eye_ref, packed):
    eye = eye_ref[...]
    low = low_lanes((CH, 128))
    for layer in range(LAYERS):
        for ty in range(3):
            pair = jnp.concatenate([raw_ref[layer, 3 + ty], raw_ref[layer, ty]], axis=0)
            packed[layer, ty * 192 : (ty + 1) * 192, :] = nt_dot(eye, pair).astype(jnp.bfloat16)
        pair = jnp.concatenate([raw_ref[layer, 6], raw_ref[layer, 7]], axis=0)
        packed[layer, 576:768, :] = nt_dot(eye, pair).astype(jnp.bfloat16)
        pair = jnp.concatenate([raw_ref[layer, 8], raw_ref[layer, 8]], axis=0)
        twice = nt_dot(eye, pair)
        packed[layer, 768:832, :] = jnp.where(low, twice[0:64], twice[64:128]).astype(jnp.bfloat16)
        terms = [term.astype(jnp.float32) for term in split_terms(bias_ref[layer : layer + 1, :])]
        terms = jnp.concatenate(terms + [jnp.zeros((CH - 3, CH), jnp.float32)], axis=0)
        terms = jnp.concatenate([terms, terms], axis=1)
        packed[layer, 832:896, :] = jnp.where(low, twice[128:192], terms).astype(jnp.bfloat16)


def combined(taps):
    before, here, behind = taps
    ends = 0.5 * (before + behind)
    return before, ends + 0.5 * here, ends - 0.5 * here, behind


def expand(packed, w_ref, bias_ref):
    low = low_lanes((192, 128))
    zero = jnp.zeros((192, 128), jnp.float32)
    mids = combined([packed[ty * 192 : (ty + 1) * 192, :].astype(jnp.float32) for ty in range(3)])
    both = packed[576:768, :].astype(jnp.float32)
    ends = packed[768:832, :].astype(jnp.float32)
    rest = packed[832:896, :].astype(jnp.float32)
    ends = jnp.concatenate([ends, pltpu.roll(ends, CH, 1), rest], axis=0)
    lasts = combined([both, pltpu.roll(both, CH, 1), ends])
    for index, (mid, last) in enumerate(zip(mids, lasts)):
        rolled = pltpu.roll(mid, CH, 1)
        blocks = (
            mid,
            jnp.where(low, last, rolled),
            jnp.where(low, zero, pltpu.roll(last, CH, 1)),
            jnp.where(low, rolled, zero),
        )
        for a, block in enumerate(blocks):
            block = block.astype(jnp.bfloat16)
            for tz in range(3):
                w_ref[index, a * CH : (a + 1) * CH, tz * 128 : (tz + 1) * 128] = block[tz * CH : (tz + 1) * CH]
    bias = rest[0:1] + rest[1:2] + rest[2:3]
    bias = jnp.where(low_lanes((1, 128)), pltpu.roll(bias, CH, 1), bias)
    bias_ref[...] = jnp.broadcast_to(bias, (8, 128))


def activate_into(v_ref, tile, value, layer):
    d = 2**layer
    activated = value * (0.5 * jnp.tanh(0.5 * value) + 0.5)
    pairs = activated.reshape(8 // d, 2, d, 16, 128)
    first, second = pairs[:, 0], pairs[:, 1]
    before = jnp.concatenate([second[-1:], second[:-1]], axis=0)
    behind = jnp.concatenate([first[1:], first[:1]], axis=0)
    mixed = (before - second, first + second, second - first, first - behind)
    for index, value in enumerate(mixed):
        v_ref[index, tile] = value.reshape(128, 128).astype(jnp.bfloat16)


def spread(move, u, v, state_out, v_ref, layer):
    low = low_lanes((16, 16, 128))
    for at, value in (
        (move[2], jnp.where(low, u, pltpu.roll(v, CH, 2))),
        (move[3], jnp.where(low, pltpu.roll(u, CH, 2), v)),
    ):
        state_out[at] = value
        activate_into(v_ref, at, value, layer)


def convolve(v_ref, w_ref, tiles, layer):
    d = 2**layer
    low = low_lanes((128, 128))
    products = []
    for index in range(4):
        rows = []
        for tile in tiles:
            after = v_ref[index, neighbour(layer, tile, 1)]
            before = v_ref[index, neighbour(layer, tile, -1)]
            rows.append(jnp.concatenate([v_ref[index, tile], jnp.where(low, after, before)], axis=1))
        rows = jnp.concatenate(rows, axis=0)
        products.append(jnp.dot(rows, w_ref[index], preferred_element_type=jnp.float32))
    first = products[0] + products[1] + products[2]
    second = products[1] - products[2] - products[3]
    results = []
    for at in range(len(tiles)):
        halves = []
        for half in (first, second):
            half = half[at * 128 : (at + 1) * 128].reshape(8, 16, 384)
            total = half[:, :, 128:256] + pltpu.roll(half[:, :, 0:128], d, 1) + pltpu.roll(half[:, :, 256:384], 16 - d, 1)
            halves.append(total.reshape(8 // d, 1, d, 16, 128))
        results.append(jnp.concatenate(halves, axis=1).reshape(16, 16, 128))
    return results


def run_section(state, v_refs, w_refs, bias_refs, prepare):
    s_a, s_b, s_c = state
    for move in MOVES[0]:
        spread(move, s_a[move[0]], s_a[move[1]], s_b, v_refs[0], 0)
    prepare(0)
    for layer in range(LAYERS):
        held, following = (s_b, s_c)[layer % 2], (s_c, s_b)[layer % 2]
        if layer + 1 < LAYERS:
            prepare(layer + 1)
        bias = bias_refs[layer][0:1][None]
        moves = MOVES[(layer + 1) % LAYERS]
        for chosen in (moves[0:2], moves[2:4]):
            tiles = [tile for move in chosen for tile in move[:2]]
            sums = convolve(v_refs[layer % 2], w_refs[layer], tiles, layer)
            sums = [held[tile] + bias + total for tile, total in zip(tiles, sums)]
            if layer + 1 < LAYERS:
                for at, move in enumerate(chosen):
                    spread(move, sums[2 * at], sums[2 * at + 1], following, v_refs[(layer + 1) % 2], layer + 1)
            else:
                for tile, total in zip(tiles, sums):
                    s_a[tile] = total.astype(jnp.bfloat16).astype(jnp.float32)


def lift_into(x, lift_ref, s_a):
    high = x.astype(jnp.bfloat16).astype(jnp.float32)
    columns = jnp.concatenate([high, x - high, high], axis=0).T.astype(jnp.bfloat16)
    hidden = jnp.dot(columns, lift_ref[...], preferred_element_type=jnp.float32)
    s_a[...] = hidden.astype(jnp.bfloat16).astype(jnp.float32).reshape(8, 16, 16, 128)


def renewed_fields(x, proj_ref, s_a):
    gain = nt_dot(proj_ref[...], s_a[...].reshape(2048, 128).astype(jnp.bfloat16))
    return x + gain[:16] + gain[16:32] + gain[32:48]


def section_kernel(section, turn, first, last, *refs):
    (ids_ref, own_0, own_1, far_0, far_1, x_ref, lift_ref, proj_ref) = refs[:8]
    (w_out, b_out, leaving, x_out, s_a, s_b, s_c, v_a, v_b, packed, w_all, b_all, sems) = refs[-13:]
    slab, line = ids_ref[0], ids_ref[1]
    if first:
        lift_into(x_ref[...], lift_ref, s_a)
    else:
        s_a[...] = refs[8][...].astype(jnp.float32)
    copies = [pltpu.make_async_copy(w_all.at[i], w_out.at[section, i], sems.at[i]) for i in range(LAYERS)]
    copies.append(pltpu.make_async_copy(b_all, b_out.at[section], sems.at[LAYERS]))

    def prepare(layer):
        for wanted, sources in ((True, (own_0, own_1)), (False, (far_0, far_1))):
            for core, source in enumerate(sources):

                @pl.when(((turn == line) == wanted) & (slab == core))
                def take(source=source):
                    packed[...] = source[layer]

        expand(packed, w_all.at[layer], b_all.at[layer])
        copies[layer].start()

    run_section((s_a, s_b, s_c), (v_a, v_b), [w_all.at[i] for i in range(LAYERS)], [b_all.at[i] for i in range(LAYERS)], prepare)
    copies[LAYERS].start()
    leaving[...] = s_a[...].astype(jnp.bfloat16)
    x_out[...] = renewed_fields(x_ref[...], proj_ref, s_a) if last else x_ref[...]
    for copy in copies:
        copy.wait()


def cells_in_rows(both, half):
    blocks = []
    for x_ref in both:
        for r in range(4):
            for upper in range(2):
                begin = pl.multiple_of(((2 * r + half) * 2 + upper) * 128, 128)
                blocks.append(x_ref[0:8, pl.ds(begin, 128)])
    row = lax.broadcasted_iota(jnp.int32, (128, 128), 0)
    lane = lax.broadcasted_iota(jnp.int32, (128, 128), 1)
    turned = ((row >> 3) == (lane & 15)) & ((row & 7) == (lane >> 4))
    turned = jnp.where(turned, 1.0, 0.0).astype(jnp.bfloat16)
    return nt_dot(turned, jnp.concatenate(blocks, axis=0).astype(jnp.bfloat16)).astype(jnp.bfloat16)


def second_kernel(ids_ref, x_ref, lift_ref, proj_ref, w_ref, b_ref, kept, given, s_a, s_b, s_c, v_a, v_b, x_new):
    s = pl.program_id(0)

    @pl.when(s == 0)
    def begin():
        lift_into(x_ref[...], lift_ref, s_a)

    run_section((s_a, s_b, s_c), (v_a, v_b), [w_ref.at[0, i] for i in range(LAYERS)], [b_ref.at[0, i] for i in range(LAYERS)], lambda layer: None)

    @pl.when(s == pl.num_programs(0) - 1)
    def finish():
        x_new[...] = renewed_fields(x_ref[...], proj_ref, s_a)
        kept[...] = cells_in_rows((x_ref, x_new), ids_ref[0])
        given[...] = cells_in_rows((x_ref, x_new), 1 - ids_ref[0])


def split_terms(matrix):
    first = matrix.astype(jnp.bfloat16)
    rest = matrix - first.astype(jnp.float32)
    second = rest.astype(jnp.bfloat16)
    third = (rest - second.astype(jnp.float32)).astype(jnp.bfloat16)
    return first, second, third


def state_scratch():
    return [pltpu.VMEM((8, 16, 16, 128), jnp.float32)] * 3 + [pltpu.VMEM((4, 8, 128, 128), jnp.bfloat16)] * 2


def shards(fields, anchors, lift_weight, conv_weight, conv_bias, proj_weight):
    segments = lax.axis_size("segment")
    slabs = lax.axis_size("slab")
    segment_id = lax.axis_index("segment")
    slab_id = lax.axis_index("slab")
    crop_count, comps, slab_rows, y_cells, z_cells = fields.shape
    lines = crop_count // slabs
    levels = segments // lines
    line = segment_id % lines
    slot = line * slabs + slab_id
    swap = [(0, 1), (1, 0)]
    vmem = pl.BlockSpec(memory_space=pltpu.VMEM)
    smem = pl.BlockSpec(memory_space=pltpu.SMEM)
    anyspace = pl.BlockSpec(memory_space=pl.ANY)
    params = pltpu.CompilerParams(vmem_limit_bytes=VMEM_BYTES)
    ids = jnp.stack([slab_id, line]).astype(jnp.int32)

    packed = pl.pallas_call(
        pack_kernel,
        out_shape=jax.ShapeDtypeStruct((LAYERS, ROWS, 128), jnp.bfloat16),
        in_specs=[vmem] * 3,
        out_specs=vmem,
        compiler_params=params,
    )(conv_weight[0], conv_bias[0], jnp.eye(192, dtype=jnp.bfloat16))

    def between_cores(value):
        return lax.ppermute(value, "slab", swap)

    kept = lax.dynamic_index_in_dim(fields, slot, 0, keepdims=False)
    given = lax.dynamic_index_in_dim(fields, line * slabs + (1 - slab_id), 0, keepdims=False)
    got = between_cores(given)
    halves = jnp.where(slab_id == 0, jnp.stack([kept, got]), jnp.stack([got, kept]))
    anchor = lax.dynamic_index_in_dim(anchors, slot, 0, keepdims=False)

    def wave(column, length):
        position = (anchor[column] + jnp.arange(length, dtype=jnp.int32)) % FIELD
        return jnp.sin(2.0 * jnp.pi * position.astype(jnp.float32) / FIELD)

    shape = (2, 2, 4, y_cells, z_cells)
    current = halves.reshape(2, comps, 2, 4, y_cells, z_cells).transpose(2, 1, 3, 0, 4, 5).reshape(6, 2048)
    wave_x = jnp.broadcast_to(wave(0, 2 * slab_rows).reshape(2, 2, 4, 1, 1), shape)
    wave_y = jnp.broadcast_to(wave(1, y_cells)[:, None], shape)
    wave_z = jnp.broadcast_to(wave(2, z_cells), shape)
    waves = jnp.stack([wave_x, wave_y, wave_z]).transpose(2, 0, 3, 1, 4, 5).reshape(6, 2048)
    x = jnp.concatenate([current, waves, jnp.zeros((4, 2048), jnp.float32)], axis=0)

    half = jnp.eye(2, dtype=jnp.float32)
    lift_cur = jnp.einsum("ab,of->afbo", half, lift_weight[:, :comps]).reshape(6, 128)
    lift_wave = jnp.einsum("ab,of->afbo", half, lift_weight[:, comps:]).reshape(6, 128)
    lift = jnp.concatenate([lift_cur, lift_wave, jnp.zeros((4, 128), jnp.float32)], axis=0)
    first, second, unused = split_terms(lift)
    lift = jnp.concatenate([first, first, second], axis=0)
    proj = jnp.einsum("ab,oc->aobc", half, proj_weight).reshape(6, 128)
    proj = jnp.concatenate([proj, jnp.zeros((10, 128), jnp.float32)], axis=0)
    proj = jnp.concatenate(split_terms(proj), axis=0)

    w_shape = jax.ShapeDtypeStruct((segments, LAYERS, 4, 256, 384), jnp.bfloat16)
    b_shape = jax.ShapeDtypeStruct((segments, LAYERS, 8, 128), jnp.float32)
    h_shape = jax.ShapeDtypeStruct((8, 16, 16, 128), jnp.bfloat16)
    x_shape = jax.ShapeDtypeStruct((16, 2048), jnp.float32)
    layer_flops = 2 * 4 * 1024 * 256 * 512
    def after(value, earlier):
        return lax.optimization_barrier((value, earlier))[0]

    def hand_on(value, level):
        pairs = [(s * slabs, (s - lines) * slabs) for s in range(lines, segments - lines * level)]
        pairs += [(0, slabs + 1), (slabs, 1)]
        return lax.ppermute(value, ("segment", "slab"), pairs)

    arrived = {0: hand_on(packed, 0)}
    swapped = {0: between_cores(arrived[0])}
    arrived[1] = hand_on(arrived[0], 1)
    kept = ()
    current = x
    for section in range(segments):
        level, turn = section // lines, section % lines
        own = (packed, packed) if level == 0 else (arrived[level - 1], swapped[level - 1])
        operands = (ids, *own, swapped[level], arrived[level], current, lift, proj, *kept)
        weights, rows, hidden, current = pl.pallas_call(
            functools.partial(section_kernel, section, turn, section == 0, section == segments - 1),
            out_shape=(w_shape, b_shape, h_shape, x_shape),
            in_specs=[smem] + [vmem] * 7 + ([vmem] + [anyspace] * 2 if kept else []),
            out_specs=(anyspace, anyspace, vmem, vmem),
            scratch_shapes=state_scratch()
            + [
                pltpu.VMEM((ROWS, 128), jnp.bfloat16),
                pltpu.VMEM((LAYERS, 4, 256, 384), jnp.bfloat16),
                pltpu.VMEM((LAYERS, 8, 128), jnp.float32),
                pltpu.SemaphoreType.DMA((LAYERS + 1,)),
            ],
            input_output_aliases={9: 0, 10: 1} if kept else {},
            compiler_params=params,
            cost_estimate=pl.CostEstimate(flops=LAYERS * layer_flops, bytes_accessed=4 << 20, transcendentals=0),
        )(*operands)
        kept = (hidden, weights, rows)
        if turn == 0 and level + 1 < levels:
            arrived[level + 1] = after(arrived[level + 1], hidden)
            swapped[level + 1] = between_cores(arrived[level + 1])
            if level + 2 < levels:
                arrived[level + 2] = hand_on(arrived[level + 1], level + 2)
    first_result = current
    kept, given = pl.pallas_call(
        second_kernel,
        grid=(segments,),
        out_shape=(jax.ShapeDtypeStruct((128, 128), jnp.bfloat16),) * 2,
        in_specs=[smem]
        + [vmem] * 3
        + [
            pl.BlockSpec((1, LAYERS, 4, 256, 384), lambda s: (s, 0, 0, 0, 0)),
            pl.BlockSpec((1, LAYERS, 8, 128), lambda s: (s, 0, 0, 0)),
        ],
        out_specs=(vmem, vmem),
        scratch_shapes=state_scratch() + [pltpu.VMEM((16, 2048), jnp.float32)],
        compiler_params=params,
        cost_estimate=pl.CostEstimate(flops=segments * LAYERS * layer_flops, bytes_accessed=16 << 20, transcendentals=0),
    )(ids, first_result, lift, proj, weights, rows)

    got = between_cores(given)
    pair = jnp.where(slab_id == 0, jnp.stack([kept, got]), jnp.stack([got, kept]))
    got = lax.ppermute(pair, "segment", swap)
    crops = jnp.where(line == 0, jnp.concatenate([pair, got]), jnp.concatenate([got, pair]))
    share = z_cells // segments

    def part_for(target):
        return lax.dynamic_slice_in_dim(crops, target * share * 8, share * 8, 1)

    out = jnp.where(segment_id < lines, part_for(segment_id), 0)
    for level in range(1, levels):
        pairs = [(s, level * lines + s) for s in range(lines)]
        out = out + lax.ppermute(part_for(segment_id + level * lines), "segment", pairs)
    out = out.reshape(crop_count, share, 8, STEPS, 4, 2, 8)[..., : 2 * comps]
    out = out.reshape(crop_count, share, 8, STEPS, 4, 2, 2, comps).transpose(3, 0, 7, 6, 4, 5, 2, 1)
    return out.reshape(STEPS, crop_count, comps, slab_rows, y_cells, share).astype(jnp.float32)


def solution(mesh):
    in_specs = (
        P("groups", None, "slab", None, None),
        P("groups", None),
        P(),
        P("segment", None, None, None, None),
        P("segment", None, None),
        P(),
    )
    out_specs = P(None, "groups", None, "slab", None, "segment")
    return jax.shard_map(shards, mesh=mesh, in_specs=in_specs, out_specs=out_specs, check_vma=False)
```

```python
import functools

import jax
import jax.numpy as jnp
from jax import lax
from jax.experimental import pallas as pl
from jax.experimental.pallas import tpu as pltpu
from jax.sharding import PartitionSpec as P

STEPS = 2
FIELD = 4096
LAYERS = 3
CH = 64
ROWS = 896
VMEM_BYTES = 48 * 1024 * 1024

MOVES = (
    [(4 * b + m, 4 * b + 2 + m, 4 * m + b, 4 * m + 2 + b) for b in range(2) for m in range(2)],
    [(2 * m, 2 * m + 1, m, 4 + m) for m in range(4)],
    [(4 * p + 2 * m, 4 * p + 2 * m + 1, 2 * p + m, 2 * (2 + p) + m) for p in range(2) for m in range(2)],
)
CYCLES = (
    [list(range(8))],
    [list(range(4)), list(range(4, 8))],
    [[2 * r, 2 * r + 1] for r in range(4)],
)


def neighbour(layer, tile, step):
    cycle = next(cycle for cycle in CYCLES[layer] if tile in cycle)
    return cycle[(cycle.index(tile) + step) % len(cycle)]


def low_lanes(shape):
    return lax.broadcasted_iota(jnp.int32, shape, len(shape) - 1) < CH


def nt_dot(a, b):
    return lax.dot_general(a, b, (((1,), (1,)), ((), ())), preferred_element_type=jnp.float32)


def pack_kernel(raw_ref, bias_ref, eye_ref, packed):
    eye = eye_ref[...]
    low = low_lanes((CH, 128))
    for layer in range(LAYERS):
        for ty in range(3):
            pair = jnp.concatenate([raw_ref[layer, 3 + ty], raw_ref[layer, ty]], axis=0)
            packed[layer, ty * 192 : (ty + 1) * 192, :] = nt_dot(eye, pair).astype(jnp.bfloat16)
        pair = jnp.concatenate([raw_ref[layer, 6], raw_ref[layer, 7]], axis=0)
        packed[layer, 576:768, :] = nt_dot(eye, pair).astype(jnp.bfloat16)
        pair = jnp.concatenate([raw_ref[layer, 8], raw_ref[layer, 8]], axis=0)
        twice = nt_dot(eye, pair)
        packed[layer, 768:832, :] = jnp.where(low, twice[0:64], twice[64:128]).astype(jnp.bfloat16)
        terms = [term.astype(jnp.float32) for term in split_terms(bias_ref[layer : layer + 1, :])]
        terms = jnp.concatenate(terms + [jnp.zeros((CH - 3, CH), jnp.float32)], axis=0)
        terms = jnp.concatenate([terms, terms], axis=1)
        packed[layer, 832:896, :] = jnp.where(low, twice[128:192], terms).astype(jnp.bfloat16)


def pair_forms(taps):
    before, here, behind = taps
    ends = 0.25 * (before + behind)
    here = 0.25 * here
    return 0.5 * before, ends + here, ends - here, 0.5 * behind


def cycle_forms(taps):
    before, here, behind = taps
    ends = 0.125 * (before + behind)
    near = 0.125 * here
    return near + ends, near - ends, 0.25 * here, 0.25 * (behind - before)


def expand(packed, w_ref, bias_ref, layer):
    low = low_lanes((192, 128))
    zero = jnp.zeros((192, 128), jnp.float32)
    forms = pair_forms if layer < 2 else cycle_forms
    mids = forms([packed[ty * 192 : (ty + 1) * 192, :].astype(jnp.float32) for ty in range(3)])
    both = packed[576:768, :].astype(jnp.float32)
    ends = packed[768:832, :].astype(jnp.float32)
    rest = packed[832:896, :].astype(jnp.float32)
    ends = jnp.concatenate([ends, pltpu.roll(ends, CH, 1), rest], axis=0)
    lasts = forms([both, pltpu.roll(both, CH, 1), ends])
    for index, (mid, last) in enumerate(zip(mids, lasts)):
        rolled = pltpu.roll(mid, CH, 1)
        blocks = (
            mid,
            jnp.where(low, last, rolled),
            jnp.where(low, zero, pltpu.roll(last, CH, 1)),
            jnp.where(low, rolled, zero),
        )
        blocks = [block.astype(jnp.bfloat16) for block in blocks]
        for tz in range(3):
            for a in range(4):
                if layer < 2:
                    w_ref[index, a * CH : (a + 1) * CH, tz * 128 : (tz + 1) * 128] = blocks[a][tz * CH : (tz + 1) * CH]
                else:
                    row = index * 256 + a * CH
                    for half in range(2):
                        chosen = blocks[((0, 2), (1, 3), (2, 0), (3, 1))[a][half]]
                        column = tz * 256 + half * 128
                        w_ref[row : row + CH, column : column + 128] = chosen[tz * CH : (tz + 1) * CH]
    bias = 0.5 * (rest[0:1] + rest[1:2] + rest[2:3])
    bias = jnp.where(low_lanes((1, 128)), pltpu.roll(bias, CH, 1), bias)
    bias_ref[...] = jnp.broadcast_to(bias, (8, 128))


def z_moved(values, tap, layer):
    even, odd = values[:, :8], values[:, 8:]
    if layer > 0:
        shift = -tap * 2 ** (layer - 1) % 8
        return pltpu.roll(even, shift, 1), pltpu.roll(odd, shift, 1)
    if tap > 0:
        return odd, pltpu.roll(even, 7, 1)
    return pltpu.roll(odd, 1, 1), even


def z_summed(products, width, layer):
    products = products.reshape(products.shape[0] // 16, 16, products.shape[1])
    here = products[:, :, width : 2 * width]
    before = z_moved(products[:, :, :width], -1, layer)
    behind = z_moved(products[:, :, 2 * width :], 1, layer)
    parts = [here[:, 8 * i : 8 * i + 8] + before[i] + behind[i] for i in range(2)]
    return jnp.concatenate(parts, axis=1)


def activate_into(v_ref, tile, value, layer):
    activated = value * jnp.tanh(value) + value
    if layer < 2:
        d = 2**layer
        pairs = activated.reshape(8 // d, 2, d, 16, 128)
        first, second = pairs[:, 0], pairs[:, 1]
        before = jnp.concatenate([second[-1:], second[:-1]], axis=0)
        behind = jnp.concatenate([first[1:], first[:1]], axis=0)
        mixed = (before - second, first + second, second - first, first - behind)
    else:
        cycle = activated.reshape(4, 4, 16, 128)
        even, odd = cycle[0] + cycle[2], cycle[1] + cycle[3]
        sine = cycle[3] - cycle[1]
        mixed = (even + odd, even - odd, cycle[0] - cycle[2], sine, -sine)
    for index, value in enumerate(mixed):
        v_ref[index, tile] = value.reshape(-1, 128).astype(jnp.bfloat16)


def spread(move, u, v, state_out, v_ref, layer):
    low = low_lanes((16, 16, 128))
    for at, value in (
        (move[2], jnp.where(low, u, pltpu.roll(v, CH, 2))),
        (move[3], jnp.where(low, pltpu.roll(u, CH, 2), v)),
    ):
        state_out[at] = value
        activate_into(v_ref, at, value, layer)


def convolve_pairs(v_ref, w_ref, tiles, layer):
    d = 2**layer
    low = low_lanes((128, 128))
    sums = []
    for index in range(4):
        rows = []
        for tile in tiles:
            after = v_ref[index, neighbour(layer, tile, 1)]
            before = v_ref[index, neighbour(layer, tile, -1)]
            rows.append(jnp.concatenate([v_ref[index, tile], jnp.where(low, after, before)], axis=1))
        rows = jnp.concatenate(rows, axis=0)
        sums.append(z_summed(jnp.dot(rows, w_ref[index], preferred_element_type=jnp.float32), 128, layer))
    first = sums[0] + sums[1] + sums[2]
    second = sums[1] - sums[2] - sums[3]
    results = []
    for at in range(len(tiles)):
        halves = [half[at * 8 : (at + 1) * 8].reshape(8 // d, 1, d, 16, 128) for half in (first, second)]
        results.append(jnp.concatenate(halves, axis=1).reshape(16, 16, 128))
    return results


def convolve_cycles(v_ref, w_ref, layer):
    def rows(left, right):
        parts = [jnp.concatenate([v_ref[left, t] for t in (2 * r, 2 * r + 1)] if right is None else
                 [v_ref[i, t] for i in (left, right) for t in (2 * r, 2 * r + 1)], axis=1) for r in range(4)]
        return jnp.concatenate(parts, axis=0)

    def summed(lhs, begin, end):
        return z_summed(jnp.dot(lhs, w_ref[begin:end, :], preferred_element_type=jnp.float32), 256, layer)

    flat = summed(rows(0, None), 0, 256)
    alternate = summed(rows(1, None), 256, 512)
    cosine = summed(rows(2, 4), 512, 1024)
    sine = summed(rows(3, 2), 512, 1024)
    even, odd = flat + alternate, flat - alternate
    cells = [value.reshape(4, 1, 4, 16, 256) for value in (even + cosine, odd - sine, even - cosine, odd + sine)]
    cells = jnp.concatenate(cells, axis=1).reshape(4, 16, 16, 256)
    return [cells[tile // 2, :, :, tile % 2 * 128 : tile % 2 * 128 + 128] for tile in range(8)]


def run_section(state, v_refs, w_refs, bias_refs, prepare):
    s_a, s_b, s_c = state
    for move in MOVES[0]:
        spread(move, s_a[move[0]], s_a[move[1]], s_b, v_refs[0], 0)
    prepare(0)
    for layer in range(LAYERS):
        held, following = (s_b, s_c)[layer % 2], (s_c, s_b)[layer % 2]
        if layer + 1 < LAYERS:
            prepare(layer + 1)
        bias = bias_refs[layer][0:1][None]
        if layer == LAYERS - 1:
            for tile, total in enumerate(convolve_cycles(v_refs[2], w_refs[layer], layer)):
                s_a[tile] = (held[tile] + bias + total).astype(jnp.bfloat16).astype(jnp.float32)
            break
        moves = MOVES[layer + 1]
        for chosen in (moves[0:2], moves[2:4]):
            tiles = [tile for move in chosen for tile in move[:2]]
            sums = convolve_pairs(v_refs[layer], w_refs[layer], tiles, layer)
            sums = [held[tile] + bias + total for tile, total in zip(tiles, sums)]
            for at, move in enumerate(chosen):
                spread(move, sums[2 * at], sums[2 * at + 1], following, v_refs[layer + 1], layer + 1)


def by_parity(x):
    row = lax.broadcasted_iota(jnp.int32, (128, 128), 0)
    lane = lax.broadcasted_iota(jnp.int32, (128, 128), 1)
    place = (row & 112) | ((row & 1) << 3) | ((row >> 1) & 7)
    turned = jnp.where(place == lane, 1.0, 0.0).astype(jnp.bfloat16)
    blocks = jnp.concatenate([x[:, at * 128 : (at + 1) * 128] for at in range(16)], axis=0)
    moved = sum(jnp.dot(term, turned, preferred_element_type=jnp.float32) for term in split_terms(blocks))
    return jnp.concatenate([moved[at * 16 : (at + 1) * 16] for at in range(16)], axis=1)


def lift_into(x, lift_ref, s_a):
    high = x.astype(jnp.bfloat16).astype(jnp.float32)
    columns = jnp.concatenate([high, x - high, high], axis=0).T.astype(jnp.bfloat16)
    hidden = jnp.dot(columns, lift_ref[...], preferred_element_type=jnp.float32)
    s_a[...] = hidden.astype(jnp.bfloat16).astype(jnp.float32).reshape(8, 16, 16, 128)


def renewed_fields(x, proj_ref, s_a):
    gain = nt_dot(proj_ref[...], s_a[...].reshape(2048, 128).astype(jnp.bfloat16))
    return x + gain[:16] + gain[16:32] + gain[32:48]


def section_kernel(section, turn, first, last, *refs):
    (ids_ref, own_0, own_1, far_0, far_1, x_ref, lift_ref, proj_ref) = refs[:8]
    (w_out, c_out, b_out, leaving, x_out, s_a, s_b, s_c, v_a, v_b, v_c, packed, w_pair, w_cycle, b_all, sems) = refs[-16:]
    slab, line = ids_ref[0], ids_ref[1]
    x = by_parity(x_ref[...]) if first else x_ref[...]
    if first:
        lift_into(x, lift_ref, s_a)
    else:
        s_a[...] = refs[8][...].astype(jnp.float32)
    w_refs = [w_pair.at[0], w_pair.at[1], w_cycle]
    copies = [pltpu.make_async_copy(w_pair.at[i], w_out.at[section, i], sems.at[i]) for i in range(2)]
    copies.append(pltpu.make_async_copy(w_cycle, c_out.at[section], sems.at[2]))
    copies.append(pltpu.make_async_copy(b_all, b_out.at[section], sems.at[LAYERS]))

    def prepare(layer):
        for wanted, sources in ((True, (own_0, own_1)), (False, (far_0, far_1))):
            for core, source in enumerate(sources):

                @pl.when(((turn == line) == wanted) & (slab == core))
                def take(source=source):
                    packed[...] = source[layer]

        expand(packed, w_refs[layer], b_all.at[layer], layer)
        copies[layer].start()

    run_section((s_a, s_b, s_c), (v_a, v_b, v_c), w_refs, [b_all.at[i] for i in range(LAYERS)], prepare)
    copies[LAYERS].start()
    leaving[...] = s_a[...].astype(jnp.bfloat16)
    x_out[...] = renewed_fields(x, proj_ref, s_a) if last else x
    for copy in copies:
        copy.wait()


def cells_in_rows(both, half):
    blocks = []
    for x_ref in both:
        for r in range(4):
            for upper in range(2):
                begin = pl.multiple_of(((2 * r + half) * 2 + upper) * 128, 128)
                blocks.append(x_ref[0:8, pl.ds(begin, 128)])
    row = lax.broadcasted_iota(jnp.int32, (128, 128), 0)
    lane = lax.broadcasted_iota(jnp.int32, (128, 128), 1)
    z = ((lane & 7) << 1) | ((lane >> 3) & 1)
    turned = ((row >> 3) == z) & ((row & 7) == (lane >> 4))
    turned = jnp.where(turned, 1.0, 0.0).astype(jnp.bfloat16)
    return nt_dot(turned, jnp.concatenate(blocks, axis=0).astype(jnp.bfloat16)).astype(jnp.bfloat16)


def second_kernel(ids_ref, x_ref, lift_ref, proj_ref, w_ref, c_ref, b_ref, kept, given, s_a, s_b, s_c, v_a, v_b, v_c, x_new):
    s = pl.program_id(0)

    @pl.when(s == 0)
    def begin():
        lift_into(x_ref[...], lift_ref, s_a)

    run_section((s_a, s_b, s_c), (v_a, v_b, v_c), [w_ref.at[0, 0], w_ref.at[0, 1], c_ref.at[0]], [b_ref.at[0, i] for i in range(LAYERS)], lambda layer: None)

    @pl.when(s == pl.num_programs(0) - 1)
    def finish():
        x_new[...] = renewed_fields(x_ref[...], proj_ref, s_a)
        kept[...] = cells_in_rows((x_ref, x_new), ids_ref[0])
        given[...] = cells_in_rows((x_ref, x_new), 1 - ids_ref[0])


def split_terms(matrix):
    first = matrix.astype(jnp.bfloat16)
    rest = matrix - first.astype(jnp.float32)
    second = rest.astype(jnp.bfloat16)
    third = (rest - second.astype(jnp.float32)).astype(jnp.bfloat16)
    return first, second, third


def state_scratch():
    return (
        [pltpu.VMEM((8, 16, 16, 128), jnp.float32)] * 3
        + [pltpu.VMEM((4, 8, 128, 128), jnp.bfloat16)] * 2
        + [pltpu.VMEM((5, 8, 64, 128), jnp.bfloat16)]
    )


def shards(fields, anchors, lift_weight, conv_weight, conv_bias, proj_weight):
    segments = lax.axis_size("segment")
    slabs = lax.axis_size("slab")
    segment_id = lax.axis_index("segment")
    slab_id = lax.axis_index("slab")
    crop_count, comps, slab_rows, y_cells, z_cells = fields.shape
    lines = crop_count // slabs
    levels = segments // lines
    line = segment_id % lines
    slot = line * slabs + slab_id
    swap = [(0, 1), (1, 0)]
    vmem = pl.BlockSpec(memory_space=pltpu.VMEM)
    smem = pl.BlockSpec(memory_space=pltpu.SMEM)
    anyspace = pl.BlockSpec(memory_space=pl.ANY)
    params = pltpu.CompilerParams(vmem_limit_bytes=VMEM_BYTES)
    ids = jnp.stack([slab_id, line]).astype(jnp.int32)

    packed = pl.pallas_call(
        pack_kernel,
        out_shape=jax.ShapeDtypeStruct((LAYERS, ROWS, 128), jnp.bfloat16),
        in_specs=[vmem] * 3,
        out_specs=vmem,
        compiler_params=params,
    )(conv_weight[0], conv_bias[0], jnp.eye(192, dtype=jnp.bfloat16))

    def between_cores(value):
        return lax.ppermute(value, "slab", swap)

    kept = lax.dynamic_index_in_dim(fields, slot, 0, keepdims=False)
    given = lax.dynamic_index_in_dim(fields, line * slabs + (1 - slab_id), 0, keepdims=False)
    got = between_cores(given)
    halves = jnp.where(slab_id == 0, jnp.stack([kept, got]), jnp.stack([got, kept]))
    anchor = lax.dynamic_index_in_dim(anchors, slot, 0, keepdims=False)

    def wave(column, length):
        position = (anchor[column] + jnp.arange(length, dtype=jnp.int32)) % FIELD
        return jnp.sin(2.0 * jnp.pi * position.astype(jnp.float32) / FIELD)

    shape = (2, 2, 4, y_cells, z_cells)
    current = halves.reshape(2, comps, 2, 4, y_cells, z_cells).transpose(2, 1, 3, 0, 4, 5).reshape(6, 2048)
    wave_x = jnp.broadcast_to(wave(0, 2 * slab_rows).reshape(2, 2, 4, 1, 1), shape)
    wave_y = jnp.broadcast_to(wave(1, y_cells)[:, None], shape)
    wave_z = jnp.broadcast_to(wave(2, z_cells), shape)
    waves = jnp.stack([wave_x, wave_y, wave_z]).transpose(2, 0, 3, 1, 4, 5).reshape(6, 2048)
    x = jnp.concatenate([current, waves, jnp.zeros((4, 2048), jnp.float32)], axis=0)

    half = jnp.eye(2, dtype=jnp.float32)
    lift_cur = jnp.einsum("ab,of->afbo", half, lift_weight[:, :comps]).reshape(6, 128)
    lift_wave = jnp.einsum("ab,of->afbo", half, lift_weight[:, comps:]).reshape(6, 128)
    lift = jnp.concatenate([lift_cur, lift_wave, jnp.zeros((4, 128), jnp.float32)], axis=0)
    first, second, unused = split_terms(0.5 * lift)
    lift = jnp.concatenate([first, first, second], axis=0)
    proj = jnp.einsum("ab,oc->aobc", half, proj_weight).reshape(6, 128)
    proj = jnp.concatenate([proj, jnp.zeros((10, 128), jnp.float32)], axis=0)
    proj = jnp.concatenate(split_terms(2.0 * proj), axis=0)

    w_shape = jax.ShapeDtypeStruct((segments, 2, 4, 256, 384), jnp.bfloat16)
    c_shape = jax.ShapeDtypeStruct((segments, 1024, 768), jnp.bfloat16)
    b_shape = jax.ShapeDtypeStruct((segments, LAYERS, 8, 128), jnp.float32)
    h_shape = jax.ShapeDtypeStruct((8, 16, 16, 128), jnp.bfloat16)
    x_shape = jax.ShapeDtypeStruct((16, 2048), jnp.float32)
    layer_flops = 2 * 4 * 1024 * 256 * 512
    def after(value, earlier):
        return lax.optimization_barrier((value, earlier))[0]

    def hand_on(value, level):
        pairs = [(s * slabs, (s - lines) * slabs) for s in range(lines, segments - lines * level)]
        pairs += [(0, slabs + 1), (slabs, 1)]
        return lax.ppermute(value, ("segment", "slab"), pairs)

    arrived = {0: hand_on(packed, 0)}
    swapped = {0: between_cores(arrived[0])}
    arrived[1] = hand_on(arrived[0], 1)
    kept = ()
    current = x
    for section in range(segments):
        level, turn = section // lines, section % lines
        own = (packed, packed) if level == 0 else (arrived[level - 1], swapped[level - 1])
        operands = (ids, *own, swapped[level], arrived[level], current, lift, proj, *kept)
        weights, cycles, rows, hidden, current = pl.pallas_call(
            functools.partial(section_kernel, section, turn, section == 0, section == segments - 1),
            out_shape=(w_shape, c_shape, b_shape, h_shape, x_shape),
            in_specs=[smem] + [vmem] * 7 + ([vmem] + [anyspace] * 3 if kept else []),
            out_specs=(anyspace, anyspace, anyspace, vmem, vmem),
            scratch_shapes=state_scratch()
            + [
                pltpu.VMEM((ROWS, 128), jnp.bfloat16),
                pltpu.VMEM((2, 4, 256, 384), jnp.bfloat16),
                pltpu.VMEM((1024, 768), jnp.bfloat16),
                pltpu.VMEM((LAYERS, 8, 128), jnp.float32),
                pltpu.SemaphoreType.DMA((LAYERS + 1,)),
            ],
            input_output_aliases={9: 0, 10: 1, 11: 2} if kept else {},
            compiler_params=params,
            cost_estimate=pl.CostEstimate(flops=LAYERS * layer_flops, bytes_accessed=4 << 20, transcendentals=0),
        )(*operands)
        kept = (hidden, weights, cycles, rows)
        if turn == 0 and level + 1 < levels:
            arrived[level + 1] = after(arrived[level + 1], hidden)
            swapped[level + 1] = between_cores(arrived[level + 1])
            if level + 2 < levels:
                arrived[level + 2] = hand_on(arrived[level + 1], level + 2)
    first_result = current
    kept, given = pl.pallas_call(
        second_kernel,
        grid=(segments,),
        out_shape=(jax.ShapeDtypeStruct((128, 128), jnp.bfloat16),) * 2,
        in_specs=[smem]
        + [vmem] * 3
        + [
            pl.BlockSpec((1, 2, 4, 256, 384), lambda s: (s, 0, 0, 0, 0)),
            pl.BlockSpec((1, 1024, 768), lambda s: (s, 0, 0)),
            pl.BlockSpec((1, LAYERS, 8, 128), lambda s: (s, 0, 0, 0)),
        ],
        out_specs=(vmem, vmem),
        scratch_shapes=state_scratch() + [pltpu.VMEM((16, 2048), jnp.float32)],
        compiler_params=params,
        cost_estimate=pl.CostEstimate(flops=segments * LAYERS * layer_flops, bytes_accessed=16 << 20, transcendentals=0),
    )(ids, first_result, lift, proj, weights, cycles, rows)

    got = between_cores(given)
    pair = jnp.where(slab_id == 0, jnp.stack([kept, got]), jnp.stack([got, kept]))
    got = lax.ppermute(pair, "segment", swap)
    crops = jnp.where(line == 0, jnp.concatenate([pair, got]), jnp.concatenate([got, pair]))
    share = z_cells // segments

    def part_for(target):
        return lax.dynamic_slice_in_dim(crops, target * share * 8, share * 8, 1)

    out = jnp.where(segment_id < lines, part_for(segment_id), 0)
    for level in range(1, levels):
        pairs = [(s, level * lines + s) for s in range(lines)]
        out = out + lax.ppermute(part_for(segment_id + level * lines), "segment", pairs)
    out = out.reshape(crop_count, share, 8, STEPS, 4, 2, 8)[..., : 2 * comps]
    out = out.reshape(crop_count, share, 8, STEPS, 4, 2, 2, comps).transpose(3, 0, 7, 6, 4, 5, 2, 1)
    return out.reshape(STEPS, crop_count, comps, slab_rows, y_cells, share).astype(jnp.float32)


def solution(mesh):
    in_specs = (
        P("groups", None, "slab", None, None),
        P("groups", None),
        P(),
        P("segment", None, None, None, None),
        P("segment", None, None),
        P(),
    )
    out_specs = P(None, "groups", None, "slab", None, "segment")
    return jax.shard_map(shards, mesh=mesh, in_specs=in_specs, out_specs=out_specs, check_vma=False)
```

```python
import functools

import jax
import jax.numpy as jnp
from jax import lax
from jax.experimental import pallas as pl
from jax.experimental.pallas import tpu as pltpu
from jax.sharding import PartitionSpec as P

STEPS = 2
FIELD = 4096
LAYERS = 3
CH = 64
ROWS = 896
VMEM_BYTES = 48 * 1024 * 1024

MOVES = (
    [(4 * b + m, 4 * b + 2 + m, 4 * m + b, 4 * m + 2 + b) for b in range(2) for m in range(2)],
    [(2 * m, 2 * m + 1, m, 4 + m) for m in range(4)],
    [(4 * p + 2 * m, 4 * p + 2 * m + 1, 2 * p + m, 2 * (2 + p) + m) for p in range(2) for m in range(2)],
)
CYCLES = (
    [list(range(8))],
    [list(range(4)), list(range(4, 8))],
    [[2 * r, 2 * r + 1] for r in range(4)],
)


GROUPS = ((0,), (1,), (2,), (3,))


def neighbour(layer, tile, step):
    cycle = next(cycle for cycle in CYCLES[layer] if tile in cycle)
    return cycle[(cycle.index(tile) + step) % len(cycle)]


def low_lanes(shape):
    return lax.broadcasted_iota(jnp.int32, shape, len(shape) - 1) < CH


def nt_dot(a, b):
    return lax.dot_general(a, b, (((1,), (1,)), ((), ())), preferred_element_type=jnp.float32)


def pack_kernel(raw_ref, bias_ref, eye_ref, packed):
    eye = eye_ref[...]
    low = low_lanes((CH, 128))
    for layer in range(LAYERS):
        for ty in range(3):
            pair = jnp.concatenate([raw_ref[layer, 3 + ty], raw_ref[layer, ty]], axis=0)
            packed[layer, ty * 192 : (ty + 1) * 192, :] = nt_dot(eye, pair).astype(jnp.bfloat16)
        pair = jnp.concatenate([raw_ref[layer, 6], raw_ref[layer, 7]], axis=0)
        packed[layer, 576:768, :] = nt_dot(eye, pair).astype(jnp.bfloat16)
        pair = jnp.concatenate([raw_ref[layer, 8], raw_ref[layer, 8]], axis=0)
        twice = nt_dot(eye, pair)
        packed[layer, 768:832, :] = jnp.where(low, twice[0:64], twice[64:128]).astype(jnp.bfloat16)
        terms = [term.astype(jnp.float32) for term in split_terms(bias_ref[layer : layer + 1, :])]
        terms = jnp.concatenate(terms + [jnp.zeros((CH - 3, CH), jnp.float32)], axis=0)
        terms = jnp.concatenate([terms, terms], axis=1)
        packed[layer, 832:896, :] = jnp.where(low, twice[128:192], terms).astype(jnp.bfloat16)


def pair_forms(taps):
    before, here, behind = taps
    ends = 0.25 * (before + behind)
    here = 0.25 * here
    return 0.5 * before, ends + here, ends - here, 0.5 * behind


def cycle_forms(taps):
    before, here, behind = taps
    ends = 0.125 * (before + behind)
    near = 0.125 * here
    return near + ends, near - ends, 0.25 * here, 0.25 * (behind - before)


def expand(packed, w_ref, bias_ref, layer):
    low = low_lanes((192, 128))
    zero = jnp.zeros((192, 128), jnp.float32)
    forms = pair_forms if layer < 2 else cycle_forms
    mids = forms([packed[ty * 192 : (ty + 1) * 192, :].astype(jnp.float32) for ty in range(3)])
    both = packed[576:768, :].astype(jnp.float32)
    ends = packed[768:832, :].astype(jnp.float32)
    rest = packed[832:896, :].astype(jnp.float32)
    ends = jnp.concatenate([ends, pltpu.roll(ends, CH, 1), rest], axis=0)
    lasts = forms([both, pltpu.roll(both, CH, 1), ends])
    for index, (mid, last) in enumerate(zip(mids, lasts)):
        rolled = pltpu.roll(mid, CH, 1)
        blocks = (
            mid,
            jnp.where(low, last, rolled),
            jnp.where(low, zero, pltpu.roll(last, CH, 1)),
            jnp.where(low, rolled, zero),
        )
        blocks = [block.astype(jnp.bfloat16) for block in blocks]
        for tz in range(3):
            for a in range(4):
                if layer < 2:
                    w_ref[index, a * CH : (a + 1) * CH, tz * 128 : (tz + 1) * 128] = blocks[a][tz * CH : (tz + 1) * CH]
                else:
                    row = index * 256 + a * CH
                    for half in range(2):
                        chosen = blocks[((0, 2), (1, 3), (2, 0), (3, 1))[a][half]]
                        column = tz * 256 + half * 128
                        w_ref[row : row + CH, column : column + 128] = chosen[tz * CH : (tz + 1) * CH]
    bias = 0.5 * (rest[0:1] + rest[1:2] + rest[2:3])
    bias = jnp.where(low_lanes((1, 128)), pltpu.roll(bias, CH, 1), bias)
    bias_ref[...] = jnp.broadcast_to(bias, (8, 128))


def z_moved(values, tap, layer):
    even, odd = values[:, :8], values[:, 8:]
    if layer > 0:
        shift = -tap * 2 ** (layer - 1) % 8
        return pltpu.roll(even, shift, 1), pltpu.roll(odd, shift, 1)
    if tap > 0:
        return odd, pltpu.roll(even, 7, 1)
    return pltpu.roll(odd, 1, 1), even


def z_summed(products, width, layer):
    products = products.reshape(products.shape[0] // 16, 16, products.shape[1])
    here = products[:, :, width : 2 * width]
    before = z_moved(products[:, :, :width], -1, layer)
    behind = z_moved(products[:, :, 2 * width :], 1, layer)
    parts = [here[:, 8 * i : 8 * i + 8] + before[i] + behind[i] for i in range(2)]
    return jnp.concatenate(parts, axis=1)


def activate_into(v_ref, tile, value, layer):
    activated = value * jnp.tanh(value) + value
    if layer < 2:
        d = 2**layer
        pairs = activated.reshape(8 // d, 2, d, 16, 128)
        first, second = pairs[:, 0], pairs[:, 1]
        before = jnp.concatenate([second[-1:], second[:-1]], axis=0)
        behind = jnp.concatenate([first[1:], first[:1]], axis=0)
        mixed = (before - second, first + second, second - first, first - behind)
    else:
        cycle = activated.reshape(4, 4, 16, 128)
        even, odd = cycle[0] + cycle[2], cycle[1] + cycle[3]
        sine = cycle[3] - cycle[1]
        mixed = (even + odd, even - odd, cycle[0] - cycle[2], sine, -sine)
    for index, value in enumerate(mixed):
        v_ref[index, tile] = value.reshape(-1, 128).astype(jnp.bfloat16)


def spread(move, u, v, state_out, v_ref, layer):
    low = low_lanes((16, 16, 128))
    for at, value in (
        (move[2], jnp.where(low, u, pltpu.roll(v, CH, 2))),
        (move[3], jnp.where(low, pltpu.roll(u, CH, 2), v)),
    ):
        state_out[at] = value
        activate_into(v_ref, at, value, layer)


def convolve_pairs(v_ref, w_ref, tiles, layer):
    d = 2**layer
    low = low_lanes((128, 128))
    sums = []
    for index in range(4):
        rows = []
        for tile in tiles:
            after = v_ref[index, neighbour(layer, tile, 1)]
            before = v_ref[index, neighbour(layer, tile, -1)]
            rows.append(jnp.concatenate([v_ref[index, tile], jnp.where(low, after, before)], axis=1))
        rows = jnp.concatenate(rows, axis=0)
        sums.append(z_summed(jnp.dot(rows, w_ref[index], preferred_element_type=jnp.float32), 128, layer))
    first = sums[0] + sums[1] + sums[2]
    second = sums[1] - sums[2] - sums[3]
    results = []
    for at in range(len(tiles)):
        halves = [half[at * 8 : (at + 1) * 8].reshape(8 // d, 1, d, 16, 128) for half in (first, second)]
        results.append(jnp.concatenate(halves, axis=1).reshape(16, 16, 128))
    return results


def convolve_cycles(v_ref, w_ref, units, layer):
    def rows(*forms):
        parts = [jnp.concatenate([v_ref[form, 2 * r + m] for form in forms for m in range(2)], axis=1) for r in units]
        return jnp.concatenate(parts, axis=0)

    def summed(lhs, begin, end):
        return z_summed(jnp.dot(lhs, w_ref[begin:end, :], preferred_element_type=jnp.float32), 256, layer)

    flat = summed(rows(0), 0, 256)
    alternate = summed(rows(1), 256, 512)
    waves = summed(jnp.concatenate([rows(2, 4), rows(3, 2)], axis=0), 512, 1024)
    count = 4 * len(units)
    cosine, sine = waves[:count], waves[count:]
    even, odd = flat + alternate, flat - alternate
    cells = [value.reshape(len(units), 1, 4, 16, 256) for value in (even + cosine, odd - sine, even - cosine, odd + sine)]
    cells = jnp.concatenate(cells, axis=1).reshape(len(units), 16, 16, 256)
    return [cells[at, :, :, m * 128 : m * 128 + 128] for at in range(len(units)) for m in range(2)]


def begin_section(state, v_refs):
    for move in MOVES[0]:
        spread(move, state[0][move[0]], state[0][move[1]], state[1], v_refs[0], 0)


def run_section(state, v_refs, w_refs, bias_refs, prepare, go_on):
    s_a, *held_in = state
    prepare(0)
    for layer in range(LAYERS):
        held, following = held_in[layer], held_in[(layer + 1) % LAYERS]
        if layer + 1 < LAYERS:
            prepare(layer + 1)
        bias = bias_refs[layer][0:1][None]
        if layer == LAYERS - 1:
            for at in range(2):
                tiles = range(4 * at, 4 * at + 4)
                sums = convolve_cycles(v_refs[2], w_refs[layer], (2 * at, 2 * at + 1), layer)
                ends = {}
                for tile, total in zip(tiles, sums):
                    ends[tile] = (held[tile] + bias + total).astype(jnp.bfloat16).astype(jnp.float32)
                    s_a[tile] = ends[tile]
                if go_on:
                    for move in MOVES[0][2 * at : 2 * at + 2]:
                        spread(move, ends[move[0]], ends[move[1]], following, v_refs[0], 0)
            break
        for chosen in GROUPS:
            moves = [MOVES[layer + 1][at] for at in chosen]
            tiles = [tile for move in moves for tile in move[:2]]
            sums = convolve_pairs(v_refs[layer], w_refs[layer], tiles, layer)
            sums = [held[tile] + bias + total for tile, total in zip(tiles, sums)]
            for at, move in enumerate(moves):
                spread(move, sums[2 * at], sums[2 * at + 1], following, v_refs[layer + 1], layer + 1)


def by_parity(x):
    row = lax.broadcasted_iota(jnp.int32, (128, 128), 0)
    lane = lax.broadcasted_iota(jnp.int32, (128, 128), 1)
    place = (row & 112) | ((row & 1) << 3) | ((row >> 1) & 7)
    turned = jnp.where(place == lane, 1.0, 0.0).astype(jnp.bfloat16)
    blocks = jnp.concatenate([x[:, at * 128 : (at + 1) * 128] for at in range(16)], axis=0)
    moved = sum(jnp.dot(term, turned, preferred_element_type=jnp.float32) for term in split_terms(blocks))
    return jnp.concatenate([moved[at * 16 : (at + 1) * 16] for at in range(16)], axis=1)


def lift_into(x, lift_ref, s_a):
    high = x.astype(jnp.bfloat16).astype(jnp.float32)
    columns = jnp.concatenate([high, x - high, high], axis=0).T.astype(jnp.bfloat16)
    hidden = jnp.dot(columns, lift_ref[...], preferred_element_type=jnp.float32)
    s_a[...] = hidden.astype(jnp.bfloat16).astype(jnp.float32).reshape(8, 16, 16, 128)


def renewed_fields(x, proj_ref, s_a):
    gain = nt_dot(proj_ref[...], s_a[...].reshape(2048, 128).astype(jnp.bfloat16))
    return x + gain[:16] + gain[16:32] + gain[32:48]


def section_kernel(section, turn, first, last, *refs):
    (ids_ref, own_0, own_1, far_0, far_1, x_ref, lift_ref, proj_ref) = refs[:8]
    (w_out, c_out, b_out, leaving, x_out, s_a, s_b, s_c, s_d, v_a, v_b, v_c, packed, w_pair, w_cycle, b_all, sems) = refs[-17:]
    slab, line = ids_ref[0], ids_ref[1]
    x = by_parity(x_ref[...]) if first else x_ref[...]
    if first:
        lift_into(x, lift_ref, s_a)
    else:
        s_a[...] = refs[8][...].astype(jnp.float32)
    w_refs = [w_pair.at[0], w_pair.at[1], w_cycle]
    copies = [pltpu.make_async_copy(w_pair.at[i], w_out.at[section, i], sems.at[i]) for i in range(2)]
    copies.append(pltpu.make_async_copy(w_cycle, c_out.at[section], sems.at[2]))
    copies.append(pltpu.make_async_copy(b_all, b_out.at[section], sems.at[LAYERS]))

    for wanted, sources in ((True, (own_0, own_1)), (False, (far_0, far_1))):
        for core, source in enumerate(sources):

            @pl.when(((turn == line) == wanted) & (slab == core))
            def take(source=source):
                packed[...] = source[...]

    def prepare(layer):
        expand(packed.at[layer], w_refs[layer], b_all.at[layer], layer)
        copies[layer].start()

    state, v_refs = (s_a, s_b, s_c, s_d), (v_a, v_b, v_c)
    begin_section(state, v_refs)
    run_section(state, v_refs, w_refs, [b_all.at[i] for i in range(LAYERS)], prepare, False)
    copies[LAYERS].start()
    leaving[...] = s_a[...].astype(jnp.bfloat16)
    x_out[...] = renewed_fields(x, proj_ref, s_a) if last else x
    for copy in copies:
        copy.wait()


def cells_in_rows(both, half):
    blocks = []
    for x_ref in both:
        for r in range(4):
            for upper in range(2):
                begin = pl.multiple_of(((2 * r + half) * 2 + upper) * 128, 128)
                blocks.append(x_ref[0:8, pl.ds(begin, 128)])
    row = lax.broadcasted_iota(jnp.int32, (128, 128), 0)
    lane = lax.broadcasted_iota(jnp.int32, (128, 128), 1)
    z = ((lane & 7) << 1) | ((lane >> 3) & 1)
    turned = ((row >> 3) == z) & ((row & 7) == (lane >> 4))
    turned = jnp.where(turned, 1.0, 0.0).astype(jnp.bfloat16)
    return nt_dot(turned, jnp.concatenate(blocks, axis=0).astype(jnp.bfloat16)).astype(jnp.bfloat16)


def second_kernel(ids_ref, x_ref, lift_ref, proj_ref, w_ref, c_ref, b_ref, kept, given, s_a, s_b, s_c, s_d, v_a, v_b, v_c, x_new):
    s = pl.program_id(0)

    state, v_refs = (s_a, s_b, s_c, s_d), (v_a, v_b, v_c)

    @pl.when(s == 0)
    def begin():
        lift_into(x_ref[...], lift_ref, s_a)
        begin_section(state, v_refs)

    w_refs = [w_ref.at[0, 0], w_ref.at[0, 1], c_ref.at[0]]
    run_section(state, v_refs, w_refs, [b_ref.at[0, i] for i in range(LAYERS)], lambda layer: None, True)

    @pl.when(s == pl.num_programs(0) - 1)
    def finish():
        x_new[...] = renewed_fields(x_ref[...], proj_ref, s_a)
        kept[...] = cells_in_rows((x_ref, x_new), ids_ref[0])
        given[...] = cells_in_rows((x_ref, x_new), 1 - ids_ref[0])


def split_terms(matrix):
    first = matrix.astype(jnp.bfloat16)
    rest = matrix - first.astype(jnp.float32)
    second = rest.astype(jnp.bfloat16)
    third = (rest - second.astype(jnp.float32)).astype(jnp.bfloat16)
    return first, second, third


def state_scratch():
    return (
        [pltpu.VMEM((8, 16, 16, 128), jnp.float32)] * 4
        + [pltpu.VMEM((4, 8, 128, 128), jnp.bfloat16)] * 2
        + [pltpu.VMEM((5, 8, 64, 128), jnp.bfloat16)]
    )


def shards(fields, anchors, lift_weight, conv_weight, conv_bias, proj_weight):
    segments = lax.axis_size("segment")
    slabs = lax.axis_size("slab")
    segment_id = lax.axis_index("segment")
    slab_id = lax.axis_index("slab")
    crop_count, comps, slab_rows, y_cells, z_cells = fields.shape
    lines = crop_count // slabs
    levels = segments // lines
    line = segment_id % lines
    slot = line * slabs + slab_id
    swap = [(0, 1), (1, 0)]
    vmem = pl.BlockSpec(memory_space=pltpu.VMEM)
    smem = pl.BlockSpec(memory_space=pltpu.SMEM)
    anyspace = pl.BlockSpec(memory_space=pl.ANY)
    params = pltpu.CompilerParams(vmem_limit_bytes=VMEM_BYTES)
    ids = jnp.stack([slab_id, line]).astype(jnp.int32)

    packed = pl.pallas_call(
        pack_kernel,
        out_shape=jax.ShapeDtypeStruct((LAYERS, ROWS, 128), jnp.bfloat16),
        in_specs=[vmem] * 3,
        out_specs=vmem,
        compiler_params=params,
    )(conv_weight[0], conv_bias[0], jnp.eye(192, dtype=jnp.bfloat16))

    def between_cores(value):
        return lax.ppermute(value, "slab", swap)

    kept = lax.dynamic_index_in_dim(fields, slot, 0, keepdims=False)
    given = lax.dynamic_index_in_dim(fields, line * slabs + (1 - slab_id), 0, keepdims=False)
    got = between_cores(given)
    halves = jnp.where(slab_id == 0, jnp.stack([kept, got]), jnp.stack([got, kept]))
    anchor = lax.dynamic_index_in_dim(anchors, slot, 0, keepdims=False)

    def wave(column, length):
        position = (anchor[column] + jnp.arange(length, dtype=jnp.int32)) % FIELD
        return jnp.sin(2.0 * jnp.pi * position.astype(jnp.float32) / FIELD)

    shape = (2, 2, 4, y_cells, z_cells)
    current = halves.reshape(2, comps, 2, 4, y_cells, z_cells).transpose(2, 1, 3, 0, 4, 5).reshape(6, 2048)
    wave_x = jnp.broadcast_to(wave(0, 2 * slab_rows).reshape(2, 2, 4, 1, 1), shape)
    wave_y = jnp.broadcast_to(wave(1, y_cells)[:, None], shape)
    wave_z = jnp.broadcast_to(wave(2, z_cells), shape)
    waves = jnp.stack([wave_x, wave_y, wave_z]).transpose(2, 0, 3, 1, 4, 5).reshape(6, 2048)
    x = jnp.concatenate([current, waves, jnp.zeros((4, 2048), jnp.float32)], axis=0)

    half = jnp.eye(2, dtype=jnp.float32)
    lift_cur = jnp.einsum("ab,of->afbo", half, lift_weight[:, :comps]).reshape(6, 128)
    lift_wave = jnp.einsum("ab,of->afbo", half, lift_weight[:, comps:]).reshape(6, 128)
    lift = jnp.concatenate([lift_cur, lift_wave, jnp.zeros((4, 128), jnp.float32)], axis=0)
    first, second, unused = split_terms(0.5 * lift)
    lift = jnp.concatenate([first, first, second], axis=0)
    proj = jnp.einsum("ab,oc->aobc", half, proj_weight).reshape(6, 128)
    proj = jnp.concatenate([proj, jnp.zeros((10, 128), jnp.float32)], axis=0)
    proj = jnp.concatenate(split_terms(2.0 * proj), axis=0)

    w_shape = jax.ShapeDtypeStruct((segments, 2, 4, 256, 384), jnp.bfloat16)
    c_shape = jax.ShapeDtypeStruct((segments, 1024, 768), jnp.bfloat16)
    b_shape = jax.ShapeDtypeStruct((segments, LAYERS, 8, 128), jnp.float32)
    h_shape = jax.ShapeDtypeStruct((8, 16, 16, 128), jnp.bfloat16)
    x_shape = jax.ShapeDtypeStruct((16, 2048), jnp.float32)
    layer_flops = 2 * 4 * 1024 * 256 * 512
    def after(value, earlier):
        return lax.optimization_barrier((value, earlier))[0]

    def hand_on(value, level):
        pairs = [(s * slabs, (s - lines) * slabs) for s in range(lines, segments - lines * level)]
        pairs += [(0, slabs + 1), (slabs, 1)]
        return lax.ppermute(value, ("segment", "slab"), pairs)

    arrived = {0: hand_on(packed, 0)}
    swapped = {0: between_cores(arrived[0])}
    arrived[1] = hand_on(arrived[0], 1)
    kept = ()
    current = x
    for section in range(segments):
        level, turn = section // lines, section % lines
        own = (packed, packed) if level == 0 else (arrived[level - 1], swapped[level - 1])
        operands = (ids, *own, swapped[level], arrived[level], current, lift, proj, *kept)
        weights, cycles, rows, hidden, current = pl.pallas_call(
            functools.partial(section_kernel, section, turn, section == 0, section == segments - 1),
            out_shape=(w_shape, c_shape, b_shape, h_shape, x_shape),
            in_specs=[smem] + [vmem] * 7 + ([vmem] + [anyspace] * 3 if kept else []),
            out_specs=(anyspace, anyspace, anyspace, vmem, vmem),
            scratch_shapes=state_scratch()
            + [
                pltpu.VMEM((LAYERS, ROWS, 128), jnp.bfloat16),
                pltpu.VMEM((2, 4, 256, 384), jnp.bfloat16),
                pltpu.VMEM((1024, 768), jnp.bfloat16),
                pltpu.VMEM((LAYERS, 8, 128), jnp.float32),
                pltpu.SemaphoreType.DMA((LAYERS + 1,)),
            ],
            input_output_aliases={9: 0, 10: 1, 11: 2} if kept else {},
            compiler_params=params,
            cost_estimate=pl.CostEstimate(flops=LAYERS * layer_flops, bytes_accessed=4 << 20, transcendentals=0),
        )(*operands)
        kept = (hidden, weights, cycles, rows)
        if turn == 0 and level + 1 < levels:
            arrived[level + 1] = after(arrived[level + 1], hidden)
            swapped[level + 1] = between_cores(arrived[level + 1])
            if level + 2 < levels:
                arrived[level + 2] = hand_on(arrived[level + 1], level + 2)
    first_result = current
    kept, given = pl.pallas_call(
        second_kernel,
        grid=(segments,),
        out_shape=(jax.ShapeDtypeStruct((128, 128), jnp.bfloat16),) * 2,
        in_specs=[smem]
        + [vmem] * 3
        + [
            pl.BlockSpec((1, 2, 4, 256, 384), lambda s: (s, 0, 0, 0, 0)),
            pl.BlockSpec((1, 1024, 768), lambda s: (s, 0, 0)),
            pl.BlockSpec((1, LAYERS, 8, 128), lambda s: (s, 0, 0, 0)),
        ],
        out_specs=(vmem, vmem),
        scratch_shapes=state_scratch() + [pltpu.VMEM((16, 2048), jnp.float32)],
        compiler_params=params,
        cost_estimate=pl.CostEstimate(flops=segments * LAYERS * layer_flops, bytes_accessed=16 << 20, transcendentals=0),
    )(ids, first_result, lift, proj, weights, cycles, rows)

    got = between_cores(given)
    pair = jnp.where(slab_id == 0, jnp.stack([kept, got]), jnp.stack([got, kept]))
    got = lax.ppermute(pair, "segment", swap)
    crops = jnp.where(line == 0, jnp.concatenate([pair, got]), jnp.concatenate([got, pair]))
    share = z_cells // segments

    def part_for(target):
        return lax.dynamic_slice_in_dim(crops, target * share * 8, share * 8, 1)

    out = jnp.where(segment_id < lines, part_for(segment_id), 0)
    for level in range(1, levels):
        pairs = [(s, level * lines + s) for s in range(lines)]
        out = out + lax.ppermute(part_for(segment_id + level * lines), "segment", pairs)
    out = out.reshape(crop_count, share, 8, STEPS, 4, 2, 8)[..., : 2 * comps]
    out = out.reshape(crop_count, share, 8, STEPS, 4, 2, 2, comps).transpose(3, 0, 7, 6, 4, 5, 2, 1)
    return out.reshape(STEPS, crop_count, comps, slab_rows, y_cells, share).astype(jnp.float32)


def solution(mesh):
    in_specs = (
        P("groups", None, "slab", None, None),
        P("groups", None),
        P(),
        P("segment", None, None, None, None),
        P("segment", None, None),
        P(),
    )
    out_specs = P(None, "groups", None, "slab", None, "segment")
    return jax.shard_map(shards, mesh=mesh, in_specs=in_specs, out_specs=out_specs, check_vma=False)
```

```python
import functools

import jax
import jax.numpy as jnp
from jax import lax
from jax.experimental import pallas as pl
from jax.experimental.pallas import tpu as pltpu
from jax.sharding import PartitionSpec as P

STEPS = 2
FIELD = 4096
LAYERS = 3
CH = 64
ROWS = 896
VMEM_BYTES = 48 * 1024 * 1024

MOVES = (
    [(4 * b + m, 4 * b + 2 + m, 4 * m + b, 4 * m + 2 + b) for b in range(2) for m in range(2)],
    [(2 * m, 2 * m + 1, m, 4 + m) for m in range(4)],
    [(4 * p + 2 * m, 4 * p + 2 * m + 1, 2 * p + m, 2 * (2 + p) + m) for p in range(2) for m in range(2)],
)
CYCLES = (
    [list(range(8))],
    [list(range(4)), list(range(4, 8))],
    [[2 * r, 2 * r + 1] for r in range(4)],
)


GROUPS = ((0, 1), (2, 3))


def neighbour(layer, tile, step):
    cycle = next(cycle for cycle in CYCLES[layer] if tile in cycle)
    return cycle[(cycle.index(tile) + step) % len(cycle)]


def low_lanes(shape):
    return lax.broadcasted_iota(jnp.int32, shape, len(shape) - 1) < CH


def nt_dot(a, b):
    return lax.dot_general(a, b, (((1,), (1,)), ((), ())), preferred_element_type=jnp.float32)


def pack_kernel(raw_ref, bias_ref, eye_ref, packed, *single):
    eye = eye_ref[...]
    low = low_lanes((CH, 128))
    for layer in range(LAYERS):
        for ty in range(3):
            pair = jnp.concatenate([raw_ref[layer, 3 + ty], raw_ref[layer, ty]], axis=0)
            packed[layer, ty * 192 : (ty + 1) * 192, :] = nt_dot(eye, pair).astype(jnp.bfloat16)
        pair = jnp.concatenate([raw_ref[layer, 6], raw_ref[layer, 7]], axis=0)
        packed[layer, 576:768, :] = nt_dot(eye, pair).astype(jnp.bfloat16)
        pair = jnp.concatenate([raw_ref[layer, 8], raw_ref[layer, 8]], axis=0)
        twice = nt_dot(eye, pair)
        packed[layer, 768:832, :] = jnp.where(low, twice[0:64], twice[64:128]).astype(jnp.bfloat16)
        terms = [term.astype(jnp.float32) for term in split_terms(bias_ref[layer : layer + 1, :])]
        terms = jnp.concatenate(terms + [jnp.zeros((CH - 3, CH), jnp.float32)], axis=0)
        terms = jnp.concatenate([terms, terms], axis=1)
        packed[layer, 832:896, :] = jnp.where(low, twice[128:192], terms).astype(jnp.bfloat16)
        single[layer][...] = packed[layer]


def pair_forms(taps):
    before, here, behind = taps
    ends = 0.25 * (before + behind)
    here = 0.25 * here
    return 0.5 * before, ends + here, ends - here, 0.5 * behind


def cycle_forms(taps):
    before, here, behind = taps
    ends = 0.125 * (before + behind)
    near = 0.125 * here
    return near + ends, near - ends, 0.25 * here, 0.25 * (behind - before)


def expand(packed, w_ref, bias_ref, layer):
    low = low_lanes((192, 128))
    zero = jnp.zeros((192, 128), jnp.float32)
    forms = pair_forms if layer < 2 else cycle_forms
    mids = forms([packed[ty * 192 : (ty + 1) * 192, :].astype(jnp.float32) for ty in range(3)])
    both = packed[576:768, :].astype(jnp.float32)
    ends = packed[768:832, :].astype(jnp.float32)
    rest = packed[832:896, :].astype(jnp.float32)
    ends = jnp.concatenate([ends, pltpu.roll(ends, CH, 1), rest], axis=0)
    lasts = forms([both, pltpu.roll(both, CH, 1), ends])
    for index, (mid, last) in enumerate(zip(mids, lasts)):
        rolled = pltpu.roll(mid, CH, 1)
        blocks = (
            mid,
            jnp.where(low, last, rolled),
            jnp.where(low, zero, pltpu.roll(last, CH, 1)),
            jnp.where(low, rolled, zero),
        )
        blocks = [block.astype(jnp.bfloat16) for block in blocks]
        for tz in range(3):
            for a in range(4):
                if layer < 2:
                    w_ref[index, a * CH : (a + 1) * CH, tz * 128 : (tz + 1) * 128] = blocks[a][tz * CH : (tz + 1) * CH]
                else:
                    row = index * 256 + a * CH
                    for half in range(2):
                        chosen = blocks[((0, 2), (1, 3), (2, 0), (3, 1))[a][half]]
                        column = tz * 256 + half * 128
                        w_ref[row : row + CH, column : column + 128] = chosen[tz * CH : (tz + 1) * CH]
    bias = 0.5 * (rest[0:1] + rest[1:2] + rest[2:3])
    bias = jnp.where(low_lanes((1, 128)), pltpu.roll(bias, CH, 1), bias)
    bias_ref[...] = jnp.broadcast_to(bias, (8, 128))


def z_moved(values, tap, layer):
    even, odd = values[:, :8], values[:, 8:]
    if layer > 0:
        shift = -tap * 2 ** (layer - 1) % 8
        return pltpu.roll(even, shift, 1), pltpu.roll(odd, shift, 1)
    if tap > 0:
        return odd, pltpu.roll(even, 7, 1)
    return pltpu.roll(odd, 1, 1), even


def z_summed(products, width, layer):
    products = products.reshape(products.shape[0] // 16, 16, products.shape[1])
    here = products[:, :, width : 2 * width]
    before = z_moved(products[:, :, :width], -1, layer)
    behind = z_moved(products[:, :, 2 * width :], 1, layer)
    parts = [here[:, 8 * i : 8 * i + 8] + before[i] + behind[i] for i in range(2)]
    return jnp.concatenate(parts, axis=1)


def activate_into(v_ref, tile, value, layer):
    activated = value * jnp.tanh(value) + value
    if layer < 2:
        d = 2**layer
        pairs = activated.reshape(8 // d, 2, d, 16, 128)
        first, second = pairs[:, 0], pairs[:, 1]
        before = jnp.concatenate([second[-1:], second[:-1]], axis=0)
        behind = jnp.concatenate([first[1:], first[:1]], axis=0)
        mixed = (before - second, first + second, second - first, first - behind)
    else:
        cycle = activated.reshape(4, 4, 16, 128)
        even, odd = cycle[0] + cycle[2], cycle[1] + cycle[3]
        sine = cycle[3] - cycle[1]
        mixed = (even + odd, even - odd, cycle[0] - cycle[2], sine, -sine)
    for index, value in enumerate(mixed):
        v_ref[index, tile] = value.reshape(-1, 128).astype(jnp.bfloat16)


def spread(move, u, v, state_out, v_ref, layer):
    low = low_lanes((16, 16, 128))
    for at, value in (
        (move[2], jnp.where(low, u, pltpu.roll(v, CH, 2))),
        (move[3], jnp.where(low, pltpu.roll(u, CH, 2), v)),
    ):
        state_out[at] = value
        activate_into(v_ref, at, value, layer)


def convolve_pairs(v_ref, w_ref, tiles, layer):
    d = 2**layer
    low = low_lanes((128, 128))
    sums = []
    for index in range(4):
        rows = []
        for tile in tiles:
            after = v_ref[index, neighbour(layer, tile, 1)]
            before = v_ref[index, neighbour(layer, tile, -1)]
            rows.append(jnp.concatenate([v_ref[index, tile], jnp.where(low, after, before)], axis=1))
        rows = jnp.concatenate(rows, axis=0)
        sums.append(z_summed(jnp.dot(rows, w_ref[index], preferred_element_type=jnp.float32), 128, layer))
    first = sums[0] + sums[1] + sums[2]
    second = sums[1] - sums[2] - sums[3]
    results = []
    for at in range(len(tiles)):
        halves = [half[at * 8 : (at + 1) * 8].reshape(8 // d, 1, d, 16, 128) for half in (first, second)]
        results.append(jnp.concatenate(halves, axis=1).reshape(16, 16, 128))
    return results


def convolve_cycles(v_ref, w_ref, units, layer):
    def rows(*forms):
        parts = [jnp.concatenate([v_ref[form, 2 * r + m] for form in forms for m in range(2)], axis=1) for r in units]
        return jnp.concatenate(parts, axis=0)

    def summed(lhs, begin, end):
        return z_summed(jnp.dot(lhs, w_ref[begin:end, :], preferred_element_type=jnp.float32), 256, layer)

    flat = summed(rows(0), 0, 256)
    alternate = summed(rows(1), 256, 512)
    waves = summed(jnp.concatenate([rows(2, 4), rows(3, 2)], axis=0), 512, 1024)
    count = 4 * len(units)
    cosine, sine = waves[:count], waves[count:]
    even, odd = flat + alternate, flat - alternate
    cells = [value.reshape(len(units), 1, 4, 16, 256) for value in (even + cosine, odd - sine, even - cosine, odd + sine)]
    cells = jnp.concatenate(cells, axis=1).reshape(len(units), 16, 16, 256)
    return [cells[at, :, :, m * 128 : m * 128 + 128] for at in range(len(units)) for m in range(2)]


def begin_section(state, v_refs):
    for move in MOVES[0]:
        spread(move, state[0][move[0]], state[0][move[1]], state[1], v_refs[0], 0)


def run_section(state, v_refs, w_refs, bias_refs, prepare, go_on, layers=range(LAYERS)):
    s_a, *held_in = state
    prepare(layers[0])
    for layer in layers:
        held, following = held_in[layer], held_in[(layer + 1) % LAYERS]
        if layer + 1 in layers:
            prepare(layer + 1)
        bias = bias_refs[layer][0:1][None]
        if layer == LAYERS - 1:
            for at in range(2):
                tiles = range(4 * at, 4 * at + 4)
                sums = convolve_cycles(v_refs[2], w_refs[layer], (2 * at, 2 * at + 1), layer)
                ends = {}
                for tile, total in zip(tiles, sums):
                    ends[tile] = (held[tile] + bias + total).astype(jnp.bfloat16).astype(jnp.float32)
                    s_a[tile] = ends[tile]
                if go_on:
                    for move in MOVES[0][2 * at : 2 * at + 2]:
                        spread(move, ends[move[0]], ends[move[1]], following, v_refs[0], 0)
            break
        for chosen in GROUPS:
            moves = [MOVES[layer + 1][at] for at in chosen]
            tiles = [tile for move in moves for tile in move[:2]]
            sums = convolve_pairs(v_refs[layer], w_refs[layer], tiles, layer)
            sums = [held[tile] + bias + total for tile, total in zip(tiles, sums)]
            for at, move in enumerate(moves):
                spread(move, sums[2 * at], sums[2 * at + 1], following, v_refs[layer + 1], layer + 1)


def by_parity(x):
    row = lax.broadcasted_iota(jnp.int32, (128, 128), 0)
    lane = lax.broadcasted_iota(jnp.int32, (128, 128), 1)
    place = (row & 112) | ((row & 1) << 3) | ((row >> 1) & 7)
    turned = jnp.where(place == lane, 1.0, 0.0).astype(jnp.bfloat16)
    blocks = jnp.concatenate([x[:, at * 128 : (at + 1) * 128] for at in range(16)], axis=0)
    moved = sum(jnp.dot(term, turned, preferred_element_type=jnp.float32) for term in split_terms(blocks))
    return jnp.concatenate([moved[at * 16 : (at + 1) * 16] for at in range(16)], axis=1)


def lift_into(x, lift_ref, s_a):
    high = x.astype(jnp.bfloat16).astype(jnp.float32)
    columns = jnp.concatenate([high, x - high, high], axis=0).T.astype(jnp.bfloat16)
    hidden = jnp.dot(columns, lift_ref[...], preferred_element_type=jnp.float32)
    s_a[...] = hidden.astype(jnp.bfloat16).astype(jnp.float32).reshape(8, 16, 16, 128)


def renewed_fields(x, proj_ref, s_a):
    gain = nt_dot(proj_ref[...], s_a[...].reshape(2048, 128).astype(jnp.bfloat16))
    return x + gain[:16] + gain[16:32] + gain[32:48]


def section_kernel(section, turn, last, *refs):
    (ids_ref, own_0, own_1, far_0, far_1, x_ref, lift_ref, proj_ref) = refs[:8]
    (w_out, c_out, b_out, leaving, x_out, s_a, s_b, s_c, s_d, v_a, v_b, v_c, packed, w_pair, w_cycle, b_all, sems) = refs[-17:]
    slab, line = ids_ref[0], ids_ref[1]
    x = x_ref[...]
    s_a[...] = refs[8][...].astype(jnp.float32)
    w_refs = [w_pair.at[0], w_pair.at[1], w_cycle]
    copies = [pltpu.make_async_copy(w_pair.at[i], w_out.at[section, i], sems.at[i]) for i in range(2)]
    copies.append(pltpu.make_async_copy(w_cycle, c_out.at[section], sems.at[2]))
    copies.append(pltpu.make_async_copy(b_all, b_out.at[section], sems.at[LAYERS]))

    for wanted, sources in ((True, (own_0, own_1)), (False, (far_0, far_1))):
        for core, source in enumerate(sources):

            @pl.when(((turn == line) == wanted) & (slab == core))
            def take(source=source):
                packed[...] = source[...]

    def prepare(layer):
        expand(packed.at[layer], w_refs[layer], b_all.at[layer], layer)
        copies[layer].start()

    state, v_refs = (s_a, s_b, s_c, s_d), (v_a, v_b, v_c)
    begin_section(state, v_refs)
    run_section(state, v_refs, w_refs, [b_all.at[i] for i in range(LAYERS)], prepare, False)
    copies[LAYERS].start()
    leaving[...] = s_a[...].astype(jnp.bfloat16)
    x_out[...] = renewed_fields(x, proj_ref, s_a) if last else x
    for copy in copies:
        copy.wait()


def layer_kernel(layer, *refs):
    ids_ref, own, far_0, far_1 = refs[:4]
    slab, line = ids_ref[0], ids_ref[1]
    scratch = refs[-7:]
    packed, w_pair, w_cycle, b_all, s_end, x_scratch, sems = scratch
    outs = refs[:-7]
    for chosen, source in ((line == 0, own), ((line != 0) & (slab == 0), far_0), ((line != 0) & (slab != 0), far_1)):

        @pl.when(chosen)
        def take(source=source):
            packed[...] = source[...]

    w_refs = [w_pair, w_pair, w_cycle]
    states = [s_end, None, None, None]
    v_refs = [None, None, None]
    if layer == 0:
        x_ref, lift_ref, w_out, c_out, b_out, x_out, s_next, v_next, s_now, v_now = refs[4:14]
        x = by_parity(x_ref[...])
        x_out[...] = x
        lift_into(x, lift_ref, s_end)
        begin_section([s_end, s_now], [v_now])
    elif layer == 1:
        s_now, v_now, w_in, c_in, b_in, w_out, c_out, b_out, s_next, v_next = refs[4:14]
    else:
        s_now, v_now, w_in, c_in, b_in, w_out, c_out, b_out, leaving = refs[4:13]
        s_next = v_next = None
    states[1 + layer] = s_now
    states[1 + (layer + 1) % LAYERS] = s_next
    v_refs[layer] = v_now
    v_refs[(layer + 1) % LAYERS] = v_next
    target = c_out.at[0] if layer == 2 else w_out.at[0, layer]
    copies = [pltpu.make_async_copy(w_refs[layer], target, sems.at[0]), pltpu.make_async_copy(b_all, b_out.at[0, layer], sems.at[1])]

    def prepare(layer):
        expand(packed, w_refs[layer], b_all, layer)
        for copy in copies:
            copy.start()

    run_section(states, v_refs, w_refs, [b_all] * LAYERS, prepare, False, range(layer, layer + 1))
    if layer == 2:
        leaving[...] = s_end[...].astype(jnp.bfloat16)
    for copy in copies:
        copy.wait()


def feature_kernel(ids_ref, anchor_ref, kept_ref, got_ref, lift_ref, proj_ref, x_ref, lift_out, proj_out):
    slab, slot = ids_ref[0], ids_ref[2]
    kept, got = kept_ref[slot], got_ref[slot]
    halves = (jnp.where(slab == 0, kept, got), jnp.where(slab == 0, got, kept))
    columns = []
    for r in range(4):
        for m in range(2):
            columns.append(jnp.concatenate([halves[m][:, r], halves[m][:, 4 + r]], axis=0))
    current = jnp.concatenate([jnp.concatenate(columns, axis=1), jnp.zeros((10, 2048), jnp.float32)], axis=0)
    row = lax.broadcasted_iota(jnp.int32, (16, 2048), 0)
    column = lax.broadcasted_iota(jnp.int32, (16, 2048), 1)
    along_x = ((column >> 8) & 1) * 8 + (column >> 9) + jnp.where(row >= 9, 4, 0)
    along_x = along_x + anchor_ref[slot, 0]
    along_y = ((column >> 4) & 15) + anchor_ref[slot, 1]
    along_z = (column & 15) + anchor_ref[slot, 2]
    axis = jnp.where(row >= 9, row - 9, row - 6)
    position = jnp.where(axis == 0, along_x, jnp.where(axis == 1, along_y, along_z)) & (FIELD - 1)
    waves = jnp.sin(2.0 * jnp.pi * position.astype(jnp.float32) / FIELD)
    x_ref[...] = jnp.where(row < 6, current, jnp.where(row < 12, waves, 0.0))

    def two_halves(part):
        blank = jnp.zeros(part.shape, jnp.float32)
        return [jnp.concatenate([part, blank], axis=1), jnp.concatenate([blank, part], axis=1)]

    lift = 0.5 * lift_ref[...]
    lift = two_halves(lift[0:3]) + two_halves(lift[3:6]) + [jnp.zeros((4, 128), jnp.float32)]
    first, second, unused = [term.astype(jnp.float32) for term in split_terms(jnp.concatenate(lift, axis=0))]
    lift_out[...] = jnp.concatenate([first, first, second], axis=0).astype(jnp.bfloat16)
    proj = two_halves(2.0 * proj_ref[...]) + [jnp.zeros((10, 128), jnp.float32)]
    proj = [term.astype(jnp.float32) for term in split_terms(jnp.concatenate(proj, axis=0))]
    proj_out[...] = jnp.concatenate(proj, axis=0).astype(jnp.bfloat16)


def cells_in_rows(both, half):
    blocks = []
    for x_ref in both:
        for r in range(4):
            for upper in range(2):
                begin = pl.multiple_of(((2 * r + half) * 2 + upper) * 128, 128)
                blocks.append(x_ref[0:8, pl.ds(begin, 128)])
    row = lax.broadcasted_iota(jnp.int32, (128, 128), 0)
    lane = lax.broadcasted_iota(jnp.int32, (128, 128), 1)
    z = ((lane & 7) << 1) | ((lane >> 3) & 1)
    turned = ((row >> 3) == z) & ((row & 7) == (lane >> 4))
    turned = jnp.where(turned, 1.0, 0.0).astype(jnp.bfloat16)
    return nt_dot(turned, jnp.concatenate(blocks, axis=0).astype(jnp.bfloat16)).astype(jnp.bfloat16)


def second_kernel(ids_ref, x_ref, lift_ref, proj_ref, w_ref, c_ref, b_ref, kept, given, s_a, s_b, s_c, s_d, v_a, v_b, v_c, x_new):
    s = pl.program_id(0)

    state, v_refs = (s_a, s_b, s_c, s_d), (v_a, v_b, v_c)

    @pl.when(s == 0)
    def begin():
        lift_into(x_ref[...], lift_ref, s_a)
        begin_section(state, v_refs)

    w_refs = [w_ref.at[0, 0], w_ref.at[0, 1], c_ref.at[0]]
    run_section(state, v_refs, w_refs, [b_ref.at[0, i] for i in range(LAYERS)], lambda layer: None, True)

    @pl.when(s == pl.num_programs(0) - 1)
    def finish():
        x_new[...] = renewed_fields(x_ref[...], proj_ref, s_a)
        kept[...] = cells_in_rows((x_ref, x_new), ids_ref[0])
        given[...] = cells_in_rows((x_ref, x_new), 1 - ids_ref[0])


def split_terms(matrix):
    first = matrix.astype(jnp.bfloat16)
    rest = matrix - first.astype(jnp.float32)
    second = rest.astype(jnp.bfloat16)
    third = (rest - second.astype(jnp.float32)).astype(jnp.bfloat16)
    return first, second, third


def state_scratch():
    return (
        [pltpu.VMEM((8, 16, 16, 128), jnp.float32)] * 4
        + [pltpu.VMEM((4, 8, 128, 128), jnp.bfloat16)] * 2
        + [pltpu.VMEM((5, 8, 64, 128), jnp.bfloat16)]
    )


def shards(fields, anchors, lift_weight, conv_weight, conv_bias, proj_weight):
    segments = lax.axis_size("segment")
    slabs = lax.axis_size("slab")
    segment_id = lax.axis_index("segment")
    slab_id = lax.axis_index("slab")
    crop_count, comps, slab_rows, y_cells, z_cells = fields.shape
    lines = crop_count // slabs
    levels = segments // lines
    line = segment_id % lines
    slot = line * slabs + slab_id
    swap = [(0, 1), (1, 0)]
    vmem = pl.BlockSpec(memory_space=pltpu.VMEM)
    smem = pl.BlockSpec(memory_space=pltpu.SMEM)
    anyspace = pl.BlockSpec(memory_space=pl.ANY)
    params = pltpu.CompilerParams(vmem_limit_bytes=VMEM_BYTES)
    ids = jnp.stack([slab_id, line, slot]).astype(jnp.int32)

    def after(value, earlier):
        return lax.optimization_barrier((value, earlier))[0]

    def between_cores(value):
        return lax.ppermute(value, "slab", swap)

    packed, *single = pl.pallas_call(
        pack_kernel,
        out_shape=[jax.ShapeDtypeStruct((LAYERS, ROWS, 128), jnp.bfloat16)]
        + [jax.ShapeDtypeStruct((ROWS, 128), jnp.bfloat16)] * LAYERS,
        in_specs=[vmem] * 3,
        out_specs=[vmem] * 4,
        compiler_params=params,
    )(conv_weight[0], conv_bias[0], jnp.eye(192, dtype=jnp.bfloat16))

    flat = after(fields, single[0]).reshape(crop_count, comps, slab_rows, y_cells * z_cells)
    x, lift, proj = pl.pallas_call(
        feature_kernel,
        out_shape=(
            jax.ShapeDtypeStruct((16, 2048), jnp.float32),
            jax.ShapeDtypeStruct((48, 128), jnp.bfloat16),
            jax.ShapeDtypeStruct((48, 128), jnp.bfloat16),
        ),
        in_specs=[smem, smem] + [vmem] * 4,
        out_specs=(vmem, vmem, vmem),
        compiler_params=params,
    )(ids, anchors, flat, between_cores(flat), lift_weight.T, proj_weight)

    w_shape = jax.ShapeDtypeStruct((segments, 2, 4, 256, 384), jnp.bfloat16)
    c_shape = jax.ShapeDtypeStruct((segments, 1024, 768), jnp.bfloat16)
    b_shape = jax.ShapeDtypeStruct((segments, LAYERS, 8, 128), jnp.float32)
    h_shape = jax.ShapeDtypeStruct((8, 16, 16, 128), jnp.bfloat16)
    x_shape = jax.ShapeDtypeStruct((16, 2048), jnp.float32)
    layer_flops = 2 * 4 * 1024 * 256 * 512
    def hand_on(value, level):
        pairs = [(s * slabs, (s - lines) * slabs) for s in range(lines, segments - lines * level)]
        pairs += [(0, slabs + 1), (slabs, 1)]
        return lax.ppermute(value, ("segment", "slab"), pairs)

    s_shape = jax.ShapeDtypeStruct((8, 16, 16, 128), jnp.float32)
    v_shapes = [jax.ShapeDtypeStruct((4, 8, 128, 128), jnp.bfloat16)] * 2 + [jax.ShapeDtypeStruct((5, 8, 64, 128), jnp.bfloat16)]
    parts = [hand_on(part, 0) for part in single]
    swaps, carried, current = [], (), None
    for layer in range(LAYERS):
        swaps.append(between_cores(parts[layer]))
        operands = (ids, single[layer], swaps[layer], parts[layer]) + ((x, lift) if layer == 0 else carried)
        outputs = [w_shape, c_shape, b_shape]
        if layer == 0:
            outputs += [x_shape]
        outputs += [s_shape, v_shapes[layer + 1]] if layer < 2 else [h_shape]
        results = pl.pallas_call(
            functools.partial(layer_kernel, layer),
            out_shape=outputs,
            in_specs=[smem] + [vmem] * 5 + ([anyspace] * 3 if layer > 0 else []),
            out_specs=[anyspace] * 3 + [vmem] * (len(outputs) - 3),
            scratch_shapes=([pltpu.VMEM(s_shape.shape, jnp.float32), pltpu.VMEM(v_shapes[0].shape, jnp.bfloat16)] if layer == 0 else [])
            + [
                pltpu.VMEM((ROWS, 128), jnp.bfloat16),
                pltpu.VMEM((4, 256, 384), jnp.bfloat16),
                pltpu.VMEM((1024, 768), jnp.bfloat16),
                pltpu.VMEM((8, 128), jnp.float32),
                pltpu.VMEM(s_shape.shape, jnp.float32),
                pltpu.VMEM((8, 128), jnp.float32),
                pltpu.SemaphoreType.DMA((2,)),
            ],
            input_output_aliases={6: 0, 7: 1, 8: 2} if layer > 0 else {},
            compiler_params=params,
            cost_estimate=pl.CostEstimate(flops=layer_flops, bytes_accessed=4 << 20, transcendentals=0),
        )(*operands)
        if layer == 0:
            current = results[3]
        carried = (*results[-2:], *results[:3]) if layer < 2 else (results[3], *results[:3])
        if layer < 2:
            parts[layer + 1] = after(parts[layer + 1], results[-1])
    kept = carried
    arrived, swapped = {0: jnp.stack(parts)}, {0: jnp.stack(swaps)}
    arrived[1] = hand_on(arrived[0], 1)
    for section in range(1, segments):
        level, turn = section // lines, section % lines
        own = (packed, packed) if level == 0 else (arrived[level - 1], swapped[level - 1])
        operands = (ids, *own, swapped[level], arrived[level], current, lift, proj, *kept)
        weights, cycles, rows, hidden, current = pl.pallas_call(
            functools.partial(section_kernel, section, turn, section == segments - 1),
            out_shape=(w_shape, c_shape, b_shape, h_shape, x_shape),
            in_specs=[smem] + [vmem] * 8 + [anyspace] * 3,
            out_specs=(anyspace, anyspace, anyspace, vmem, vmem),
            scratch_shapes=state_scratch()
            + [
                pltpu.VMEM((LAYERS, ROWS, 128), jnp.bfloat16),
                pltpu.VMEM((2, 4, 256, 384), jnp.bfloat16),
                pltpu.VMEM((1024, 768), jnp.bfloat16),
                pltpu.VMEM((LAYERS, 8, 128), jnp.float32),
                pltpu.SemaphoreType.DMA((LAYERS + 1,)),
            ],
            input_output_aliases={9: 0, 10: 1, 11: 2},
            compiler_params=params,
            cost_estimate=pl.CostEstimate(flops=LAYERS * layer_flops, bytes_accessed=4 << 20, transcendentals=0),
        )(*operands)
        kept = (hidden, weights, cycles, rows)
        if turn == lines - 1 and level + 1 < levels:
            arrived[level + 1] = after(arrived[level + 1], hidden)
            swapped[level + 1] = between_cores(arrived[level + 1])
            if level + 2 < levels:
                arrived[level + 2] = hand_on(arrived[level + 1], level + 2)
    first_result = current
    kept, given = pl.pallas_call(
        second_kernel,
        grid=(segments,),
        out_shape=(jax.ShapeDtypeStruct((128, 128), jnp.bfloat16),) * 2,
        in_specs=[smem]
        + [vmem] * 3
        + [
            pl.BlockSpec((1, 2, 4, 256, 384), lambda s: (s, 0, 0, 0, 0)),
            pl.BlockSpec((1, 1024, 768), lambda s: (s, 0, 0)),
            pl.BlockSpec((1, LAYERS, 8, 128), lambda s: (s, 0, 0, 0)),
        ],
        out_specs=(vmem, vmem),
        scratch_shapes=state_scratch() + [pltpu.VMEM((16, 2048), jnp.float32)],
        compiler_params=params,
        cost_estimate=pl.CostEstimate(flops=segments * LAYERS * layer_flops, bytes_accessed=16 << 20, transcendentals=0),
    )(ids, first_result, lift, proj, weights, cycles, rows)

    share = z_cells // segments
    got = between_cores(given)
    pair = jnp.where(slab_id == 0, jnp.stack([kept, got]), jnp.stack([got, kept]))
    pair = pair.reshape(slabs, levels, lines, share * 8, 128)
    mine = lax.dynamic_index_in_dim(pair, line, 2, keepdims=False)
    got = lax.ppermute(lax.dynamic_index_in_dim(pair, 1 - line, 2, keepdims=False), "segment", swap)
    crops = jnp.where(line == 0, jnp.concatenate([mine, got]), jnp.concatenate([got, mine]))
    out = jnp.where(segment_id < lines, crops[:, 0], 0)
    for level in range(1, levels):
        pairs = [(s, level * lines + s) for s in range(lines)]
        out = out + lax.ppermute(crops[:, level], "segment", pairs)
    out = out.reshape(crop_count, share, 8, STEPS, 4, 2, 8)[..., : 2 * comps]
    out = out.reshape(crop_count, share, 8, STEPS, 4, 2, 2, comps).transpose(3, 0, 7, 6, 4, 5, 2, 1)
    return out.reshape(STEPS, crop_count, comps, slab_rows, y_cells, share).astype(jnp.float32)


def solution(mesh):
    in_specs = (
        P("groups", None, "slab", None, None),
        P("groups", None),
        P(),
        P("segment", None, None, None, None),
        P("segment", None, None),
        P(),
    )
    out_specs = P(None, "groups", None, "slab", None, "segment")
    return jax.shard_map(shards, mesh=mesh, in_specs=in_specs, out_specs=out_specs, check_vma=False)
```

```python
import functools

import jax
import jax.numpy as jnp
from jax import lax
from jax.experimental import pallas as pl
from jax.experimental.pallas import tpu as pltpu
from jax.sharding import PartitionSpec as P

STEPS = 2
FIELD = 4096
LAYERS = 3
CH = 64
ROWS = 896
VMEM_BYTES = 48 * 1024 * 1024

MOVES = (
    [(4 * b + m, 4 * b + 2 + m, 4 * m + b, 4 * m + 2 + b) for b in range(2) for m in range(2)],
    [(2 * m, 2 * m + 1, m, 4 + m) for m in range(4)],
    [(4 * p + 2 * m, 4 * p + 2 * m + 1, 2 * p + m, 2 * (2 + p) + m) for p in range(2) for m in range(2)],
)
CYCLES = (
    [list(range(8))],
    [list(range(4)), list(range(4, 8))],
    [[2 * r, 2 * r + 1] for r in range(4)],
)


GROUPS = ((0,), (1,), (2,), (3,))


def neighbour(layer, tile, step):
    cycle = next(cycle for cycle in CYCLES[layer] if tile in cycle)
    return cycle[(cycle.index(tile) + step) % len(cycle)]


def low_lanes(shape):
    return lax.broadcasted_iota(jnp.int32, shape, len(shape) - 1) < CH


def nt_dot(a, b):
    return lax.dot_general(a, b, (((1,), (1,)), ((), ())), preferred_element_type=jnp.float32)


def pack_kernel(raw_ref, bias_ref, eye_ref, packed):
    eye = eye_ref[...]
    low = low_lanes((CH, 128))
    for layer in range(LAYERS):
        for ty in range(3):
            pair = jnp.concatenate([raw_ref[layer, 3 + ty], raw_ref[layer, ty]], axis=0)
            packed[layer, ty * 192 : (ty + 1) * 192, :] = nt_dot(eye, pair).astype(jnp.bfloat16)
        pair = jnp.concatenate([raw_ref[layer, 6], raw_ref[layer, 7]], axis=0)
        packed[layer, 576:768, :] = nt_dot(eye, pair).astype(jnp.bfloat16)
        pair = jnp.concatenate([raw_ref[layer, 8], raw_ref[layer, 8]], axis=0)
        twice = nt_dot(eye, pair)
        packed[layer, 768:832, :] = jnp.where(low, twice[0:64], twice[64:128]).astype(jnp.bfloat16)
        terms = [term.astype(jnp.float32) for term in split_terms(bias_ref[layer : layer + 1, :])]
        terms = jnp.concatenate(terms + [jnp.zeros((CH - 3, CH), jnp.float32)], axis=0)
        terms = jnp.concatenate([terms, terms], axis=1)
        packed[layer, 832:896, :] = jnp.where(low, twice[128:192], terms).astype(jnp.bfloat16)


def pair_forms(taps):
    before, here, behind = taps
    ends = 0.25 * (before + behind)
    here = 0.25 * here
    return 0.5 * before, ends + here, ends - here, 0.5 * behind


def cycle_forms(taps):
    before, here, behind = taps
    ends = 0.125 * (before + behind)
    near = 0.125 * here
    return near + ends, near - ends, 0.25 * here, 0.25 * (behind - before)


def expand(packed, w_ref, bias_ref, layer):
    low = low_lanes((192, 128))
    zero = jnp.zeros((192, 128), jnp.float32)
    forms = pair_forms if layer < 2 else cycle_forms
    mids = forms([packed[ty * 192 : (ty + 1) * 192, :].astype(jnp.float32) for ty in range(3)])
    both = packed[576:768, :].astype(jnp.float32)
    ends = packed[768:832, :].astype(jnp.float32)
    rest = packed[832:896, :].astype(jnp.float32)
    ends = jnp.concatenate([ends, pltpu.roll(ends, CH, 1), rest], axis=0)
    lasts = forms([both, pltpu.roll(both, CH, 1), ends])
    for index, (mid, last) in enumerate(zip(mids, lasts)):
        rolled = pltpu.roll(mid, CH, 1)
        blocks = (
            mid,
            jnp.where(low, last, rolled),
            jnp.where(low, zero, pltpu.roll(last, CH, 1)),
            jnp.where(low, rolled, zero),
        )
        blocks = [block.astype(jnp.bfloat16) for block in blocks]
        for tz in range(3):
            for a in range(4):
                if layer < 2:
                    w_ref[index, a * CH : (a + 1) * CH, tz * 128 : (tz + 1) * 128] = blocks[a][tz * CH : (tz + 1) * CH]
                else:
                    row = index * 256 + a * CH
                    for half in range(2):
                        chosen = blocks[((0, 2), (1, 3), (2, 0), (3, 1))[a][half]]
                        column = tz * 256 + half * 128
                        w_ref[row : row + CH, column : column + 128] = chosen[tz * CH : (tz + 1) * CH]
    bias = 0.5 * (rest[0:1] + rest[1:2] + rest[2:3])
    bias = jnp.where(low_lanes((1, 128)), pltpu.roll(bias, CH, 1), bias)
    bias_ref[...] = jnp.broadcast_to(bias, (8, 128))


def z_moved(values, tap, layer):
    even, odd = values[:, :8], values[:, 8:]
    if layer > 0:
        shift = -tap * 2 ** (layer - 1) % 8
        return pltpu.roll(even, shift, 1), pltpu.roll(odd, shift, 1)
    if tap > 0:
        return odd, pltpu.roll(even, 7, 1)
    return pltpu.roll(odd, 1, 1), even


def z_summed(products, width, layer):
    products = products.reshape(products.shape[0] // 16, 16, products.shape[1])
    here = products[:, :, width : 2 * width]
    before = z_moved(products[:, :, :width], -1, layer)
    behind = z_moved(products[:, :, 2 * width :], 1, layer)
    parts = [here[:, 8 * i : 8 * i + 8] + before[i] + behind[i] for i in range(2)]
    return jnp.concatenate(parts, axis=1)


def activate_into(v_ref, tile, value, layer):
    activated = value * jnp.tanh(value) + value
    if layer < 2:
        d = 2**layer
        pairs = activated.reshape(8 // d, 2, d, 16, 128)
        first, second = pairs[:, 0], pairs[:, 1]
        before = jnp.concatenate([second[-1:], second[:-1]], axis=0)
        behind = jnp.concatenate([first[1:], first[:1]], axis=0)
        mixed = (before - second, first + second, second - first, first - behind)
    else:
        cycle = activated.reshape(4, 4, 16, 128)
        even, odd = cycle[0] + cycle[2], cycle[1] + cycle[3]
        sine = cycle[3] - cycle[1]
        mixed = (even + odd, even - odd, cycle[0] - cycle[2], sine, -sine)
    for index, value in enumerate(mixed):
        v_ref[index, tile] = value.reshape(-1, 128).astype(jnp.bfloat16)


def spread(move, u, v, state_out, v_ref, layer):
    low = low_lanes((16, 16, 128))
    for at, value in (
        (move[2], jnp.where(low, u, pltpu.roll(v, CH, 2))),
        (move[3], jnp.where(low, pltpu.roll(u, CH, 2), v)),
    ):
        state_out[at] = value
        activate_into(v_ref, at, value, layer)


def convolve_pairs(v_ref, w_ref, tiles, layer):
    d = 2**layer
    low = low_lanes((128, 128))
    sums = []
    for index in range(4):
        rows = []
        for tile in tiles:
            after = v_ref[index, neighbour(layer, tile, 1)]
            before = v_ref[index, neighbour(layer, tile, -1)]
            rows.append(jnp.concatenate([v_ref[index, tile], jnp.where(low, after, before)], axis=1))
        rows = jnp.concatenate(rows, axis=0)
        sums.append(z_summed(jnp.dot(rows, w_ref[index], preferred_element_type=jnp.float32), 128, layer))
    first = sums[0] + sums[1] + sums[2]
    second = sums[1] - sums[2] - sums[3]
    results = []
    for at in range(len(tiles)):
        halves = [half[at * 8 : (at + 1) * 8].reshape(8 // d, 1, d, 16, 128) for half in (first, second)]
        results.append(jnp.concatenate(halves, axis=1).reshape(16, 16, 128))
    return results


def convolve_cycles(v_ref, w_ref, units, layer):
    def rows(*forms):
        parts = [jnp.concatenate([v_ref[form, 2 * r + m] for form in forms for m in range(2)], axis=1) for r in units]
        return jnp.concatenate(parts, axis=0)

    def summed(lhs, begin, end):
        return z_summed(jnp.dot(lhs, w_ref[begin:end, :], preferred_element_type=jnp.float32), 256, layer)

    flat = summed(rows(0), 0, 256)
    alternate = summed(rows(1), 256, 512)
    waves = summed(jnp.concatenate([rows(2, 4), rows(3, 2)], axis=0), 512, 1024)
    count = 4 * len(units)
    cosine, sine = waves[:count], waves[count:]
    even, odd = flat + alternate, flat - alternate
    cells = [value.reshape(len(units), 1, 4, 16, 256) for value in (even + cosine, odd - sine, even - cosine, odd + sine)]
    cells = jnp.concatenate(cells, axis=1).reshape(len(units), 16, 16, 256)
    return [cells[at, :, :, m * 128 : m * 128 + 128] for at in range(len(units)) for m in range(2)]


def begin_section(state, v_refs):
    for move in MOVES[0]:
        spread(move, state[0][move[0]], state[0][move[1]], state[1], v_refs[0], 0)


def run_section(state, v_refs, w_refs, bias_refs, prepare):
    s_a, *held_in = state
    begin_section(state, v_refs)
    prepare(0)
    for layer in range(LAYERS):
        held, following = held_in[layer], held_in[(layer + 1) % LAYERS]
        if layer + 1 < LAYERS:
            prepare(layer + 1)
        bias = bias_refs[layer][0:1][None]
        if layer == LAYERS - 1:
            for tile, total in enumerate(convolve_cycles(v_refs[2], w_refs[layer], range(4), layer)):
                s_a[tile] = (held[tile] + bias + total).astype(jnp.bfloat16).astype(jnp.float32)
            break
        for chosen in GROUPS:
            moves = [MOVES[layer + 1][at] for at in chosen]
            tiles = [tile for move in moves for tile in move[:2]]
            sums = convolve_pairs(v_refs[layer], w_refs[layer], tiles, layer)
            sums = [held[tile] + bias + total for tile, total in zip(tiles, sums)]
            for at, move in enumerate(moves):
                spread(move, sums[2 * at], sums[2 * at + 1], following, v_refs[layer + 1], layer + 1)


def by_parity(x):
    row = lax.broadcasted_iota(jnp.int32, (128, 128), 0)
    lane = lax.broadcasted_iota(jnp.int32, (128, 128), 1)
    place = (row & 112) | ((row & 1) << 3) | ((row >> 1) & 7)
    turned = jnp.where(place == lane, 1.0, 0.0).astype(jnp.bfloat16)
    blocks = jnp.concatenate([x[:, at * 128 : (at + 1) * 128] for at in range(16)], axis=0)
    moved = sum(jnp.dot(term, turned, preferred_element_type=jnp.float32) for term in split_terms(blocks))
    return jnp.concatenate([moved[at * 16 : (at + 1) * 16] for at in range(16)], axis=1)


def lift_into(x, lift_ref, s_a):
    high = x.astype(jnp.bfloat16).astype(jnp.float32)
    columns = jnp.concatenate([high, x - high, high], axis=0).T.astype(jnp.bfloat16)
    hidden = jnp.dot(columns, lift_ref[...], preferred_element_type=jnp.float32)
    s_a[...] = hidden.astype(jnp.bfloat16).astype(jnp.float32).reshape(8, 16, 16, 128)


def renewed_fields(x, proj_ref, s_a):
    gain = nt_dot(proj_ref[...], s_a[...].reshape(2048, 128).astype(jnp.bfloat16))
    return x + gain[:16] + gain[16:32] + gain[32:48]


def level_kernel(level, first, last, *refs):
    (ids_ref, own_0, own_1, far_0, far_1, x_ref, lift_ref, proj_ref) = refs[:8]
    (w_out, c_out, b_out, leaving, x_out, s_a, s_b, s_c, s_d, v_a, v_b, v_c) = refs[-17:-5]
    (packed, w_pair, w_cycle, b_all, sems) = refs[-5:]
    slab, line = ids_ref[0], ids_ref[1]
    x = by_parity(x_ref[...]) if first else x_ref[...]
    if first:
        lift_into(x, lift_ref, s_a)
    else:
        s_a[...] = refs[8][...].astype(jnp.float32)
    state, v_refs = (s_a, s_b, s_c, s_d), (v_a, v_b, v_c)

    def copies(turn):
        at = 2 * level + turn
        pairs = [pltpu.make_async_copy(w_pair.at[turn, i], w_out.at[at, i], sems.at[turn, i]) for i in range(2)]
        cycle = pltpu.make_async_copy(w_cycle.at[turn], c_out.at[at], sems.at[turn, 2])
        return pairs + [cycle, pltpu.make_async_copy(b_all.at[turn], b_out.at[at], sems.at[turn, 3])]

    def section(turn, unused):
        for wanted, sources in ((True, (own_0, own_1)), (False, (far_0, far_1))):
            for core, source in enumerate(sources):

                @pl.when(((turn == line) == wanted) & (slab == core))
                def take(source=source):
                    packed[...] = source[...]

        w_refs = [w_pair.at[turn, 0], w_pair.at[turn, 1], w_cycle.at[turn]]

        def prepare(layer):
            expand(packed.at[layer], w_refs[layer], b_all.at[turn, layer], layer)
            copies(turn)[layer].start()

        run_section(state, v_refs, w_refs, [b_all.at[turn, i] for i in range(LAYERS)], prepare)
        copies(turn)[LAYERS].start()
        return 0

    lax.fori_loop(0, 2, section, 0)
    leaving[...] = s_a[...].astype(jnp.bfloat16)
    x_out[...] = renewed_fields(x, proj_ref, s_a) if last else x
    for turn in range(2):
        for copy in copies(turn):
            copy.wait()


def feature_kernel(ids_ref, anchor_ref, kept_ref, got_ref, lift_ref, proj_ref, x_ref, lift_out, proj_out):
    slab, slot = ids_ref[0], ids_ref[2]
    kept, got = kept_ref[slot], got_ref[slot]
    halves = (jnp.where(slab == 0, kept, got), jnp.where(slab == 0, got, kept))
    columns = []
    for r in range(4):
        for m in range(2):
            columns.append(jnp.concatenate([halves[m][:, r], halves[m][:, 4 + r]], axis=0))
    current = jnp.concatenate([jnp.concatenate(columns, axis=1), jnp.zeros((10, 2048), jnp.float32)], axis=0)
    row = lax.broadcasted_iota(jnp.int32, (16, 2048), 0)
    column = lax.broadcasted_iota(jnp.int32, (16, 2048), 1)
    along_x = ((column >> 8) & 1) * 8 + (column >> 9) + jnp.where(row >= 9, 4, 0)
    along_x = along_x + anchor_ref[slot, 0]
    along_y = ((column >> 4) & 15) + anchor_ref[slot, 1]
    along_z = (column & 15) + anchor_ref[slot, 2]
    axis = jnp.where(row >= 9, row - 9, row - 6)
    position = jnp.where(axis == 0, along_x, jnp.where(axis == 1, along_y, along_z)) & (FIELD - 1)
    waves = jnp.sin(2.0 * jnp.pi * position.astype(jnp.float32) / FIELD)
    x_ref[...] = jnp.where(row < 6, current, jnp.where(row < 12, waves, 0.0))

    def two_halves(part):
        blank = jnp.zeros(part.shape, jnp.float32)
        return [jnp.concatenate([part, blank], axis=1), jnp.concatenate([blank, part], axis=1)]

    lift = 0.5 * lift_ref[...]
    lift = two_halves(lift[0:3]) + two_halves(lift[3:6]) + [jnp.zeros((4, 128), jnp.float32)]
    first, second, unused = [term.astype(jnp.float32) for term in split_terms(jnp.concatenate(lift, axis=0))]
    lift_out[...] = jnp.concatenate([first, first, second], axis=0).astype(jnp.bfloat16)
    proj = two_halves(2.0 * proj_ref[...]) + [jnp.zeros((10, 128), jnp.float32)]
    proj = [term.astype(jnp.float32) for term in split_terms(jnp.concatenate(proj, axis=0))]
    proj_out[...] = jnp.concatenate(proj, axis=0).astype(jnp.bfloat16)


def cells_in_rows(both, half):
    blocks = []
    for x_ref in both:
        for r in range(4):
            for upper in range(2):
                begin = pl.multiple_of(((2 * r + half) * 2 + upper) * 128, 128)
                blocks.append(x_ref[0:8, pl.ds(begin, 128)])
    row = lax.broadcasted_iota(jnp.int32, (128, 128), 0)
    lane = lax.broadcasted_iota(jnp.int32, (128, 128), 1)
    z = ((lane & 7) << 1) | ((lane >> 3) & 1)
    turned = ((row >> 3) == z) & ((row & 7) == (lane >> 4))
    turned = jnp.where(turned, 1.0, 0.0).astype(jnp.bfloat16)
    return nt_dot(turned, jnp.concatenate(blocks, axis=0).astype(jnp.bfloat16)).astype(jnp.bfloat16)


def second_kernel(ids_ref, x_ref, lift_ref, proj_ref, w_ref, c_ref, b_ref, kept, given, s_a, s_b, s_c, s_d, v_a, v_b, v_c, x_new):
    s = pl.program_id(0)

    state, v_refs = (s_a, s_b, s_c, s_d), (v_a, v_b, v_c)

    @pl.when(s == 0)
    def begin():
        lift_into(x_ref[...], lift_ref, s_a)

    w_refs = [w_ref.at[0, 0], w_ref.at[0, 1], c_ref.at[0]]
    run_section(state, v_refs, w_refs, [b_ref.at[0, i] for i in range(LAYERS)], lambda layer: None)

    @pl.when(s == pl.num_programs(0) - 1)
    def finish():
        x_new[...] = renewed_fields(x_ref[...], proj_ref, s_a)
        kept[...] = cells_in_rows((x_ref, x_new), ids_ref[0])
        given[...] = cells_in_rows((x_ref, x_new), 1 - ids_ref[0])


def split_terms(matrix):
    first = matrix.astype(jnp.bfloat16)
    rest = matrix - first.astype(jnp.float32)
    second = rest.astype(jnp.bfloat16)
    third = (rest - second.astype(jnp.float32)).astype(jnp.bfloat16)
    return first, second, third


def state_scratch():
    return (
        [pltpu.VMEM((8, 16, 16, 128), jnp.float32)] * 4
        + [pltpu.VMEM((4, 8, 128, 128), jnp.bfloat16)] * 2
        + [pltpu.VMEM((5, 8, 64, 128), jnp.bfloat16)]
    )


def shards(fields, anchors, lift_weight, conv_weight, conv_bias, proj_weight):
    segments = lax.axis_size("segment")
    slabs = lax.axis_size("slab")
    segment_id = lax.axis_index("segment")
    slab_id = lax.axis_index("slab")
    crop_count, comps, slab_rows, y_cells, z_cells = fields.shape
    lines = crop_count // slabs
    levels = segments // lines
    line = segment_id % lines
    slot = line * slabs + slab_id
    swap = [(0, 1), (1, 0)]
    vmem = pl.BlockSpec(memory_space=pltpu.VMEM)
    smem = pl.BlockSpec(memory_space=pltpu.SMEM)
    anyspace = pl.BlockSpec(memory_space=pl.ANY)
    params = pltpu.CompilerParams(vmem_limit_bytes=VMEM_BYTES)
    ids = jnp.stack([slab_id, line, slot]).astype(jnp.int32)

    def after(value, earlier):
        return lax.optimization_barrier((value, earlier))[0]

    def between_cores(value):
        return lax.ppermute(value, "slab", swap)

    packed = pl.pallas_call(
        pack_kernel,
        out_shape=jax.ShapeDtypeStruct((LAYERS, ROWS, 128), jnp.bfloat16),
        in_specs=[vmem] * 3,
        out_specs=vmem,
        compiler_params=params,
    )(conv_weight[0], conv_bias[0], jnp.eye(192, dtype=jnp.bfloat16))

    flat = after(fields, packed).reshape(crop_count, comps, slab_rows, y_cells * z_cells)
    x, lift, proj = pl.pallas_call(
        feature_kernel,
        out_shape=(
            jax.ShapeDtypeStruct((16, 2048), jnp.float32),
            jax.ShapeDtypeStruct((48, 128), jnp.bfloat16),
            jax.ShapeDtypeStruct((48, 128), jnp.bfloat16),
        ),
        in_specs=[smem, smem] + [vmem] * 4,
        out_specs=(vmem, vmem, vmem),
        compiler_params=params,
    )(ids, anchors, flat, between_cores(flat), lift_weight.T, proj_weight)

    w_shape = jax.ShapeDtypeStruct((segments, 2, 4, 256, 384), jnp.bfloat16)
    c_shape = jax.ShapeDtypeStruct((segments, 1024, 768), jnp.bfloat16)
    b_shape = jax.ShapeDtypeStruct((segments, LAYERS, 8, 128), jnp.float32)
    h_shape = jax.ShapeDtypeStruct((8, 16, 16, 128), jnp.bfloat16)
    x_shape = jax.ShapeDtypeStruct((16, 2048), jnp.float32)
    layer_flops = 2 * 4 * 1024 * 256 * 512
    def hand_on(value, level):
        pairs = [(s * slabs, (s - lines) * slabs) for s in range(lines, segments - lines * level)]
        pairs += [(0, slabs + 1), (slabs, 1)]
        return lax.ppermute(value, ("segment", "slab"), pairs)

    arrived = {0: after(hand_on(packed, 0), x)}
    swapped = {0: between_cores(arrived[0])}
    arrived[1] = hand_on(arrived[0], 1)
    kept = ()
    current = x
    for level in range(levels):
        own = (packed, packed) if level == 0 else (arrived[level - 1], swapped[level - 1])
        operands = (ids, *own, swapped[level], arrived[level], current, lift, proj, *kept)
        weights, cycles, rows, hidden, current = pl.pallas_call(
            functools.partial(level_kernel, level, level == 0, level == levels - 1),
            out_shape=(w_shape, c_shape, b_shape, h_shape, x_shape),
            in_specs=[smem] + [vmem] * 7 + ([vmem] + [anyspace] * 3 if kept else []),
            out_specs=(anyspace, anyspace, anyspace, vmem, vmem),
            scratch_shapes=state_scratch()
            + [
                pltpu.VMEM((LAYERS, ROWS, 128), jnp.bfloat16),
                pltpu.VMEM((2, 2, 4, 256, 384), jnp.bfloat16),
                pltpu.VMEM((2, 1024, 768), jnp.bfloat16),
                pltpu.VMEM((2, LAYERS, 8, 128), jnp.float32),
                pltpu.SemaphoreType.DMA((2, LAYERS + 1)),
            ],
            input_output_aliases={9: 0, 10: 1, 11: 2} if kept else {},
            compiler_params=params,
            cost_estimate=pl.CostEstimate(flops=2 * LAYERS * layer_flops, bytes_accessed=4 << 20, transcendentals=0),
        )(*operands)
        kept = (hidden, weights, cycles, rows)
        if level + 1 < levels:
            arrived[level + 1] = after(arrived[level + 1], hidden)
            swapped[level + 1] = between_cores(arrived[level + 1])
            if level + 2 < levels:
                arrived[level + 2] = hand_on(arrived[level + 1], level + 2)
    first_result = current
    kept, given = pl.pallas_call(
        second_kernel,
        grid=(segments,),
        out_shape=(jax.ShapeDtypeStruct((128, 128), jnp.bfloat16),) * 2,
        in_specs=[smem]
        + [vmem] * 3
        + [
            pl.BlockSpec((1, 2, 4, 256, 384), lambda s: (s, 0, 0, 0, 0)),
            pl.BlockSpec((1, 1024, 768), lambda s: (s, 0, 0)),
            pl.BlockSpec((1, LAYERS, 8, 128), lambda s: (s, 0, 0, 0)),
        ],
        out_specs=(vmem, vmem),
        scratch_shapes=state_scratch() + [pltpu.VMEM((16, 2048), jnp.float32)],
        compiler_params=params,
        cost_estimate=pl.CostEstimate(flops=segments * LAYERS * layer_flops, bytes_accessed=16 << 20, transcendentals=0),
    )(ids, first_result, lift, proj, weights, cycles, rows)

    share = z_cells // segments
    got = between_cores(given)
    pair = jnp.where(slab_id == 0, jnp.stack([kept, got]), jnp.stack([got, kept]))
    pair = pair.reshape(slabs, levels, lines, share * 8, 128)
    mine = lax.dynamic_index_in_dim(pair, line, 2, keepdims=False)
    got = lax.ppermute(lax.dynamic_index_in_dim(pair, 1 - line, 2, keepdims=False), "segment", swap)
    crops = jnp.where(line == 0, jnp.concatenate([mine, got]), jnp.concatenate([got, mine]))
    out = jnp.where(segment_id < lines, crops[:, 0], 0)
    for level in range(1, levels):
        pairs = [(s, level * lines + s) for s in range(lines)]
        out = out + lax.ppermute(crops[:, level], "segment", pairs)
    out = out.reshape(crop_count, share, 8, STEPS, 4, 2, 8)[..., : 2 * comps]
    out = out.reshape(crop_count, share, 8, STEPS, 4, 2, 2, comps).transpose(3, 0, 7, 6, 4, 5, 2, 1)
    return out.reshape(STEPS, crop_count, comps, slab_rows, y_cells, share).astype(jnp.float32)


def solution(mesh):
    in_specs = (
        P("groups", None, "slab", None, None),
        P("groups", None),
        P(),
        P("segment", None, None, None, None),
        P("segment", None, None),
        P(),
    )
    out_specs = P(None, "groups", None, "slab", None, "segment")
    return jax.shard_map(shards, mesh=mesh, in_specs=in_specs, out_specs=out_specs, check_vma=False)
```

```python
import functools

import jax
import jax.numpy as jnp
from jax import lax
from jax.experimental import pallas as pl
from jax.experimental.pallas import tpu as pltpu
from jax.sharding import PartitionSpec as P

STEPS = 2
FIELD = 4096
LAYERS = 3
CH = 64
ROWS = 896
SLOTS = 16
VMEM_BYTES = 48 * 1024 * 1024

MOVES = (
    [(4 * b + m, 4 * b + 2 + m, 4 * m + b, 4 * m + 2 + b) for b in range(2) for m in range(2)],
    [(2 * m, 2 * m + 1, m, 4 + m) for m in range(4)],
    [(4 * p + 2 * m, 4 * p + 2 * m + 1, 2 * p + m, 2 * (2 + p) + m) for p in range(2) for m in range(2)],
)
CYCLES = (
    [list(range(8))],
    [list(range(4)), list(range(4, 8))],
    [[2 * r, 2 * r + 1] for r in range(4)],
)


def neighbour(layer, tile, step):
    cycle = next(cycle for cycle in CYCLES[layer] if tile in cycle)
    return cycle[(cycle.index(tile) + step) % len(cycle)]


def low_lanes(shape):
    return lax.broadcasted_iota(jnp.int32, shape, len(shape) - 1) < CH


def nt_dot(a, b):
    return lax.dot_general(a, b, (((1,), (1,)), ((), ())), preferred_element_type=jnp.float32)


def pack_kernel(raw_ref, bias_ref, eye_ref, packed):
    eye = eye_ref[...]
    low = low_lanes((CH, 128))
    for layer in range(LAYERS):
        for ty in range(3):
            pair = jnp.concatenate([raw_ref[layer, 3 + ty], raw_ref[layer, ty]], axis=0)
            packed[layer, ty * 192 : (ty + 1) * 192, :] = nt_dot(eye, pair).astype(jnp.bfloat16)
        pair = jnp.concatenate([raw_ref[layer, 6], raw_ref[layer, 7]], axis=0)
        packed[layer, 576:768, :] = nt_dot(eye, pair).astype(jnp.bfloat16)
        pair = jnp.concatenate([raw_ref[layer, 8], raw_ref[layer, 8]], axis=0)
        twice = nt_dot(eye, pair)
        packed[layer, 768:832, :] = jnp.where(low, twice[0:64], twice[64:128]).astype(jnp.bfloat16)
        terms = [term.astype(jnp.float32) for term in split_terms(bias_ref[layer : layer + 1, :])]
        terms = jnp.concatenate(terms + [jnp.zeros((CH - 3, CH), jnp.float32)], axis=0)
        terms = jnp.concatenate([terms, terms], axis=1)
        packed[layer, 832:896, :] = jnp.where(low, twice[128:192], terms).astype(jnp.bfloat16)


def pair_forms(taps):
    before, here, behind = taps
    ends = 0.25 * (before + behind)
    here = 0.25 * here
    return 0.5 * before, ends + here, ends - here, 0.5 * behind


def cycle_forms(taps):
    before, here, behind = taps
    ends = 0.125 * (before + behind)
    near = 0.125 * here
    return near + ends, near - ends, 0.25 * here, 0.25 * (behind - before)


def expand(packed, w_ref, bias_ref, layer):
    low = low_lanes((192, 128))
    zero = jnp.zeros((192, 128), jnp.float32)
    forms = pair_forms if layer < 2 else cycle_forms
    mids = forms([packed[ty * 192 : (ty + 1) * 192, :].astype(jnp.float32) for ty in range(3)])
    both = packed[576:768, :].astype(jnp.float32)
    ends = packed[768:832, :].astype(jnp.float32)
    rest = packed[832:896, :].astype(jnp.float32)
    ends = jnp.concatenate([ends, pltpu.roll(ends, CH, 1), rest], axis=0)
    lasts = forms([both, pltpu.roll(both, CH, 1), ends])
    for index, (mid, last) in enumerate(zip(mids, lasts)):
        rolled = pltpu.roll(mid, CH, 1)
        blocks = (
            mid,
            jnp.where(low, last, rolled),
            jnp.where(low, zero, pltpu.roll(last, CH, 1)),
            jnp.where(low, rolled, zero),
        )
        blocks = [block.astype(jnp.bfloat16) for block in blocks]
        for tz in range(3):
            for a in range(4):
                if layer < 2:
                    w_ref[index, a * CH : (a + 1) * CH, tz * 128 : (tz + 1) * 128] = blocks[a][tz * CH : (tz + 1) * CH]
                else:
                    row = index * 256 + a * CH
                    for half in range(2):
                        chosen = blocks[((0, 2), (1, 3), (2, 0), (3, 1))[a][half]]
                        column = tz * 256 + half * 128
                        w_ref[row : row + CH, column : column + 128] = chosen[tz * CH : (tz + 1) * CH]
    bias = 0.5 * (rest[0:1] + rest[1:2] + rest[2:3])
    bias = jnp.where(low_lanes((1, 128)), pltpu.roll(bias, CH, 1), bias)
    bias_ref[...] = jnp.broadcast_to(bias, (8, 128))


def z_moved(values, tap, layer):
    even, odd = values[:, :8], values[:, 8:]
    if layer > 0:
        shift = -tap * 2 ** (layer - 1) % 8
        return pltpu.roll(even, shift, 1), pltpu.roll(odd, shift, 1)
    if tap > 0:
        return odd, pltpu.roll(even, 7, 1)
    return pltpu.roll(odd, 1, 1), even


def z_summed(products, width, layer):
    products = products.reshape(products.shape[0] // 16, 16, products.shape[1])
    here = products[:, :, width : 2 * width]
    before = z_moved(products[:, :, :width], -1, layer)
    behind = z_moved(products[:, :, 2 * width :], 1, layer)
    parts = [here[:, 8 * i : 8 * i + 8] + before[i] + behind[i] for i in range(2)]
    return jnp.concatenate(parts, axis=1)


def activate_into(v_ref, tile, value, layer):
    activated = value * jnp.tanh(value) + value
    if layer < 2:
        d = 2**layer
        pairs = activated.reshape(8 // d, 2, d, 16, 128)
        first, second = pairs[:, 0], pairs[:, 1]
        before = jnp.concatenate([second[-1:], second[:-1]], axis=0)
        behind = jnp.concatenate([first[1:], first[:1]], axis=0)
        mixed = (before - second, first + second, second - first, first - behind)
    else:
        cycle = activated.reshape(4, 4, 16, 128)
        even, odd = cycle[0] + cycle[2], cycle[1] + cycle[3]
        sine = cycle[3] - cycle[1]
        mixed = (even + odd, even - odd, cycle[0] - cycle[2], sine, -sine)
    for index, value in enumerate(mixed):
        v_ref[index, tile] = value.reshape(-1, 128).astype(jnp.bfloat16)


def spread(move, u, v, state_out, v_ref, layer):
    low = low_lanes((16, 16, 128))
    for at, value in (
        (move[2], jnp.where(low, u, pltpu.roll(v, CH, 2))),
        (move[3], jnp.where(low, pltpu.roll(u, CH, 2), v)),
    ):
        state_out[at] = value
        activate_into(v_ref, at, value, layer)


def stream(accs, unit, steps):
    def push(at):
        pltpu.matmul_push_rhs(steps[at][0](), at % 2, unit)

    def take(results):
        for slot, use in results:
            use(pltpu.matmul_pop(accs[unit][slot]))

    push(0)
    waiting = ()
    for at, (weights, rows, results) in enumerate(steps):
        for index, (slot, value) in enumerate(rows):
            pltpu.matmul_acc_lhs(accs[unit][slot], value(), load_staged_rhs=at % 2 if index == 0 else None)
            if index == 0 and at + 1 < len(steps):
                push(at + 1)
        take(waiting)
        waiting = results
        yield
    take(waiting)


def convolve_pairs(v_ref, w_ref, layer, accs, finish):
    d = 2**layer
    low = low_lanes((128, 128))
    order = [tile for move in MOVES[layer + 1] for tile in move[:2]]

    def push(index):
        pltpu.matmul_push_rhs(w_ref[index, :, 0:256], index % 2, 0)
        last = w_ref[index, :, 256:384]
        pltpu.matmul_push_rhs(jnp.concatenate([last, last], axis=1), index % 2, 1)

    def taken(slot):
        both = pltpu.matmul_pop(accs[0][slot]).reshape(4, 16, 256)
        last = pltpu.matmul_pop(accs[1][slot]).reshape(4, 16, 256)
        before = z_moved(both[:, :, :128], -1, layer)
        behind = z_moved(last[:, :, :128], 1, layer)
        here = both[:, :, 128:]
        return jnp.concatenate([here[:, 8 * i : 8 * i + 8] + before[i] + behind[i] for i in range(2)], axis=1)

    first, second, waiting = {}, {}, []

    def take():
        index, tile, slots = waiting.pop(0)
        total = jnp.concatenate([taken(slot) for slot in slots], axis=0)
        if index == 0:
            first[tile] = total
        elif index == 1:
            first[tile], second[tile] = first[tile] + total, total
        elif index == 2:
            first[tile], second[tile] = first[tile] + total, second[tile] - total
        else:
            second[tile] = second[tile] - total
            halves = [half.reshape(8 // d, 1, d, 16, 128) for half in (first.pop(tile), second.pop(tile))]
            finish(tile, jnp.concatenate(halves, axis=1).reshape(16, 16, 128))

    push(0)
    for index in range(4):
        for at, tile in enumerate(order):
            after = v_ref[index, neighbour(layer, tile, 1)]
            before = v_ref[index, neighbour(layer, tile, -1)]
            rows = jnp.concatenate([v_ref[index, tile], jnp.where(low, after, before)], axis=1)
            base = 2 * ((8 * index + at) % (SLOTS // 2))
            for half in range(2):
                for acc in accs:
                    staged = index % 2 if at == 0 and half == 0 else None
                    pltpu.matmul_acc_lhs(acc[base + half], rows[64 * half : 64 * half + 64], load_staged_rhs=staged)
            waiting.append((index, tile, (base, base + 1)))
            if at == 2 and index < 3:
                push(index + 1)
            if len(waiting) == 3:
                take()
    while waiting:
        take()


def convolve_cycles(v_ref, w_ref, layer, accs, finish):
    sums = {}

    def rows(form, r):
        return lambda: jnp.concatenate([v_ref[form, 2 * r], v_ref[form, 2 * r + 1]], axis=1)

    def weights(row, tz):
        return lambda: w_ref[row * 256 : row * 256 + 256, tz * 256 : tz * 256 + 256]

    def adding(name, r, tz):
        def use(product):
            product = product.reshape(4, 16, 256)
            if tz != 1:
                product = jnp.concatenate(z_moved(product, tz - 1, layer), axis=1)
            sums[name, r] = sums[name, r] + product if (name, r) in sums else product

        return use

    def plain(form, tz, base):
        fed = [(base + r, rows(form, r)) for r in range(4)]
        return [(weights(form, tz), fed, [(base + r, adding(form, r, tz)) for r in range(4)])]

    def paired(tz, base):
        ends = [(base + r, adding(2, r, tz)) for r in range(4)] + [(base + 4 + r, adding(3, r, tz)) for r in range(4)]
        real = [(base + r, rows(2, r)) for r in range(4)] + [(base + 4 + r, rows(3, r)) for r in range(4)]
        other = [(base + r, rows(4, r)) for r in range(4)] + [(base + 4 + r, rows(2, r)) for r in range(4)]
        return [(weights(2, tz), real, ()), (weights(3, tz), other, ends)]

    ways = (
        paired(0, 0) + paired(1, 8) + plain(0, 0, 0),
        paired(2, 0) + plain(0, 1, 8) + plain(0, 2, 0) + plain(1, 0, 8) + plain(1, 1, 0) + plain(1, 2, 8),
    )
    streams = [stream(accs, unit, steps) for unit, steps in enumerate(ways)]
    while streams:
        streams = [one for one in streams if next(one, True) is None]
    for r in range(4):
        even, odd = sums[0, r] + sums[1, r], sums[0, r] - sums[1, r]
        cosine, sine = sums[2, r], sums[3, r]
        cells = jnp.stack([even + cosine, odd - sine, even - cosine, odd + sine]).reshape(16, 16, 256)
        for m in range(2):
            finish(2 * r + m, cells[:, :, m * 128 : m * 128 + 128])


def begin_section(state, v_refs):
    for move in MOVES[0]:
        spread(move, state[0][move[0]], state[0][move[1]], state[1], v_refs[0], 0)


def run_section(state, v_refs, w_refs, bias_refs, prepare):
    s_a, *held_in = state
    begin_section(state, v_refs)
    prepare(0)

    def layers(*accs):
        accs = accs[:SLOTS], accs[SLOTS:]
        for layer in range(LAYERS):
            held, following = held_in[layer], held_in[(layer + 1) % LAYERS]
            if layer + 1 < LAYERS:
                prepare(layer + 1)
            bias = bias_refs[layer][0:1][None]
            done = {}

            def finish(tile, total, layer=layer, held=held, following=following, bias=bias, done=done):
                total = held[tile] + bias + total
                if layer == LAYERS - 1:
                    s_a[tile] = total.astype(jnp.bfloat16).astype(jnp.float32)
                    return
                done[tile] = total
                for move in MOVES[layer + 1]:
                    if tile == move[1]:
                        spread(move, done.pop(move[0]), done.pop(tile), following, v_refs[layer + 1], layer + 1)

            convolve = convolve_cycles if layer == LAYERS - 1 else convolve_pairs
            convolve(v_refs[layer], w_refs[layer], layer, accs, finish)

    pl.run_scoped(layers, *[pltpu.ACC(unit)((64, 256), jnp.float32) for unit in range(2) for slot in range(SLOTS)])


def by_parity(x):
    row = lax.broadcasted_iota(jnp.int32, (128, 128), 0)
    lane = lax.broadcasted_iota(jnp.int32, (128, 128), 1)
    place = (row & 112) | ((row & 1) << 3) | ((row >> 1) & 7)
    turned = jnp.where(place == lane, 1.0, 0.0).astype(jnp.bfloat16)
    blocks = jnp.concatenate([x[:, at * 128 : (at + 1) * 128] for at in range(16)], axis=0)
    moved = sum(jnp.dot(term, turned, preferred_element_type=jnp.float32) for term in split_terms(blocks))
    return jnp.concatenate([moved[at * 16 : (at + 1) * 16] for at in range(16)], axis=1)


def lifted(x, lift):
    high = x.astype(jnp.bfloat16).astype(jnp.float32)
    columns = jnp.concatenate([high, x - high, high], axis=0).T.astype(jnp.bfloat16)
    hidden = jnp.dot(columns, lift, preferred_element_type=jnp.float32)
    return hidden.astype(jnp.bfloat16).reshape(8, 16, 16, 128)


def renewed_fields(x, proj_ref, hidden_ref):
    gain = nt_dot(proj_ref[...], hidden_ref[...].reshape(2048, 128))
    return x + gain[:16] + gain[16:32] + gain[32:48]


def renew_kernel(x_ref, hidden_ref, lift_ref, proj_ref, x_out, hidden_out):
    x = renewed_fields(x_ref[...], proj_ref, hidden_ref)
    x_out[...] = x
    hidden_out[...] = lifted(x, lift_ref[...])


def result_kernel(ids_ref, x_ref, hidden_ref, proj_ref, kept, given, x_new):
    x_new[...] = renewed_fields(x_ref[...], proj_ref, hidden_ref)
    kept[...] = cells_in_rows((x_ref, x_new), ids_ref[0])
    given[...] = cells_in_rows((x_ref, x_new), 1 - ids_ref[0])


def level_kernel(level, *refs):
    (ids_ref, own_0, own_1, far_0, far_1, entry) = refs[:6]
    (w_out, c_out, b_out, leaving, s_a, s_b, s_c, s_d, v_a, v_b, v_c) = refs[-16:-5]
    (packed, w_pair, w_cycle, b_all, sems) = refs[-5:]
    slab, line = ids_ref[0], ids_ref[1]
    s_a[...] = entry[...].astype(jnp.float32)
    state, v_refs = (s_a, s_b, s_c, s_d), (v_a, v_b, v_c)

    def copy(turn, part):
        at = 2 * level + turn
        source = (w_pair.at[turn, 0], w_pair.at[turn, 1], w_cycle.at[turn], b_all.at[turn])[part]
        target = (w_out.at[at, 0], w_out.at[at, 1], c_out.at[at], b_out.at[at])[part]
        return pltpu.make_async_copy(source, target, sems.at[turn, part])

    def section(turn, unused):
        for wanted, sources in ((True, (own_0, own_1)), (False, (far_0, far_1))):
            for core, source in enumerate(sources):

                @pl.when(((turn == line) == wanted) & (slab == core))
                def take(source=source):
                    packed[...] = source[...]

        w_refs = [w_pair.at[turn, 0], w_pair.at[turn, 1], w_cycle.at[turn]]

        def prepare(layer):
            expand(packed.at[layer], w_refs[layer], b_all.at[turn, layer], layer)
            copy(turn, layer).start()

        run_section(state, v_refs, w_refs, [b_all.at[turn, i] for i in range(LAYERS)], prepare)
        copy(turn, LAYERS).start()
        return 0

    lax.fori_loop(0, 2, section, 0)
    leaving[...] = s_a[...].astype(jnp.bfloat16)
    for turn in range(2):
        for part in range(LAYERS + 1):
            copy(turn, part).wait()


def feature_kernel(ids_ref, anchor_ref, kept_ref, got_ref, lift_ref, proj_ref, x_ref, lift_out, proj_out, hidden_out):
    slab, slot = ids_ref[0], ids_ref[2]
    kept, got = kept_ref[slot], got_ref[slot]
    halves = (jnp.where(slab == 0, kept, got), jnp.where(slab == 0, got, kept))
    columns = []
    for r in range(4):
        for m in range(2):
            columns.append(jnp.concatenate([halves[m][:, r], halves[m][:, 4 + r]], axis=0))
    current = jnp.concatenate([jnp.concatenate(columns, axis=1), jnp.zeros((10, 2048), jnp.float32)], axis=0)
    row = lax.broadcasted_iota(jnp.int32, (16, 2048), 0)
    column = lax.broadcasted_iota(jnp.int32, (16, 2048), 1)
    along_x = ((column >> 8) & 1) * 8 + (column >> 9) + jnp.where(row >= 9, 4, 0)
    along_x = along_x + anchor_ref[slot, 0]
    along_y = ((column >> 4) & 15) + anchor_ref[slot, 1]
    along_z = (column & 15) + anchor_ref[slot, 2]
    axis = jnp.where(row >= 9, row - 9, row - 6)
    position = jnp.where(axis == 0, along_x, jnp.where(axis == 1, along_y, along_z)) & (FIELD - 1)
    waves = jnp.sin(2.0 * jnp.pi * position.astype(jnp.float32) / FIELD)
    x = by_parity(jnp.where(row < 6, current, jnp.where(row < 12, waves, 0.0)))
    x_ref[...] = x

    def two_halves(part):
        blank = jnp.zeros(part.shape, jnp.float32)
        return [jnp.concatenate([part, blank], axis=1), jnp.concatenate([blank, part], axis=1)]

    lift = 0.5 * lift_ref[...]
    lift = two_halves(lift[0:3]) + two_halves(lift[3:6]) + [jnp.zeros((4, 128), jnp.float32)]
    first, second, unused = [term.astype(jnp.float32) for term in split_terms(jnp.concatenate(lift, axis=0))]
    lift = jnp.concatenate([first, first, second], axis=0).astype(jnp.bfloat16)
    lift_out[...] = lift
    hidden_out[...] = lifted(x, lift)
    proj = two_halves(2.0 * proj_ref[...]) + [jnp.zeros((10, 128), jnp.float32)]
    proj = [term.astype(jnp.float32) for term in split_terms(jnp.concatenate(proj, axis=0))]
    proj_out[...] = jnp.concatenate(proj, axis=0).astype(jnp.bfloat16)


def cells_in_rows(both, half):
    blocks = []
    for x_ref in both:
        for r in range(4):
            for upper in range(2):
                begin = pl.multiple_of(((2 * r + half) * 2 + upper) * 128, 128)
                blocks.append(x_ref[0:8, pl.ds(begin, 128)])
    row = lax.broadcasted_iota(jnp.int32, (128, 128), 0)
    lane = lax.broadcasted_iota(jnp.int32, (128, 128), 1)
    z = ((lane & 7) << 1) | ((lane >> 3) & 1)
    turned = ((row >> 3) == z) & ((row & 7) == (lane >> 4))
    turned = jnp.where(turned, 1.0, 0.0).astype(jnp.bfloat16)
    return nt_dot(turned, jnp.concatenate(blocks, axis=0).astype(jnp.bfloat16)).astype(jnp.bfloat16)


def second_kernel(entry, w_ref, c_ref, b_ref, leaving, s_a, s_b, s_c, s_d, v_a, v_b, v_c):
    s = pl.program_id(0)

    @pl.when(s == 0)
    def begin():
        s_a[...] = entry[...].astype(jnp.float32)

    w_refs = [w_ref.at[0, 0], w_ref.at[0, 1], c_ref.at[0]]
    biases = [b_ref.at[0, i] for i in range(LAYERS)]
    run_section((s_a, s_b, s_c, s_d), (v_a, v_b, v_c), w_refs, biases, lambda layer: None)

    @pl.when(s == pl.num_programs(0) - 1)
    def finish():
        leaving[...] = s_a[...].astype(jnp.bfloat16)


def split_terms(matrix):
    first = matrix.astype(jnp.bfloat16)
    rest = matrix - first.astype(jnp.float32)
    second = rest.astype(jnp.bfloat16)
    third = (rest - second.astype(jnp.float32)).astype(jnp.bfloat16)
    return first, second, third


def state_scratch():
    return (
        [pltpu.VMEM((8, 16, 16, 128), jnp.float32)] * 4
        + [pltpu.VMEM((4, 8, 128, 128), jnp.bfloat16)] * 2
        + [pltpu.VMEM((5, 8, 64, 128), jnp.bfloat16)]
    )


def shards(fields, anchors, lift_weight, conv_weight, conv_bias, proj_weight):
    segments = lax.axis_size("segment")
    slabs = lax.axis_size("slab")
    segment_id = lax.axis_index("segment")
    slab_id = lax.axis_index("slab")
    crop_count, comps, slab_rows, y_cells, z_cells = fields.shape
    lines = crop_count // slabs
    levels = segments // lines
    line = segment_id % lines
    slot = line * slabs + slab_id
    swap = [(0, 1), (1, 0)]
    vmem = pl.BlockSpec(memory_space=pltpu.VMEM)
    smem = pl.BlockSpec(memory_space=pltpu.SMEM)
    anyspace = pl.BlockSpec(memory_space=pl.ANY)
    params = pltpu.CompilerParams(vmem_limit_bytes=VMEM_BYTES)
    ids = jnp.stack([slab_id, line, slot]).astype(jnp.int32)

    def after(value, earlier):
        return lax.optimization_barrier((value, earlier))[0]

    def between_cores(value):
        return lax.ppermute(value, "slab", swap)

    packed = pl.pallas_call(
        pack_kernel,
        out_shape=jax.ShapeDtypeStruct((LAYERS, ROWS, 128), jnp.bfloat16),
        in_specs=[vmem] * 3,
        out_specs=vmem,
        compiler_params=params,
    )(conv_weight[0], conv_bias[0], jnp.eye(192, dtype=jnp.bfloat16))

    flat = after(fields, packed).reshape(crop_count, comps, slab_rows, y_cells * z_cells)
    h_shape = jax.ShapeDtypeStruct((8, 16, 16, 128), jnp.bfloat16)
    x_shape = jax.ShapeDtypeStruct((16, 2048), jnp.float32)
    x, lift, proj, hidden = pl.pallas_call(
        feature_kernel,
        out_shape=(
            x_shape,
            jax.ShapeDtypeStruct((48, 128), jnp.bfloat16),
            jax.ShapeDtypeStruct((48, 128), jnp.bfloat16),
            h_shape,
        ),
        in_specs=[smem, smem] + [vmem] * 4,
        out_specs=(vmem, vmem, vmem, vmem),
        compiler_params=params,
    )(ids, anchors, flat, between_cores(flat), lift_weight.T, proj_weight)

    w_shape = jax.ShapeDtypeStruct((segments, 2, 4, 256, 384), jnp.bfloat16)
    c_shape = jax.ShapeDtypeStruct((segments, 1024, 768), jnp.bfloat16)
    b_shape = jax.ShapeDtypeStruct((segments, LAYERS, 8, 128), jnp.float32)
    layer_flops = 2 * 4 * 1024 * 256 * 512
    def hand_on(value, level):
        pairs = [(s * slabs, (s - lines) * slabs) for s in range(lines, segments - lines * level)]
        pairs += [(0, slabs + 1), (slabs, 1)]
        return lax.ppermute(value, ("segment", "slab"), pairs)

    arrived = {0: after(hand_on(packed, 0), x)}
    swapped = {0: between_cores(arrived[0])}
    arrived[1] = hand_on(arrived[0], 1)
    kept = ()
    for level in range(levels):
        own = (packed, packed) if level == 0 else (arrived[level - 1], swapped[level - 1])
        operands = (ids, *own, swapped[level], arrived[level], hidden, *kept)
        weights, cycles, rows, hidden = pl.pallas_call(
            functools.partial(level_kernel, level),
            out_shape=(w_shape, c_shape, b_shape, h_shape),
            in_specs=[smem] + [vmem] * 5 + ([anyspace] * 3 if kept else []),
            out_specs=(anyspace, anyspace, anyspace, vmem),
            scratch_shapes=state_scratch()
            + [
                pltpu.VMEM((LAYERS, ROWS, 128), jnp.bfloat16),
                pltpu.VMEM((2, 2, 4, 256, 384), jnp.bfloat16),
                pltpu.VMEM((2, 1024, 768), jnp.bfloat16),
                pltpu.VMEM((2, LAYERS, 8, 128), jnp.float32),
                pltpu.SemaphoreType.DMA((2, LAYERS + 1)),
            ],
            input_output_aliases={6: 0, 7: 1, 8: 2} if kept else {},
            compiler_params=params,
            cost_estimate=pl.CostEstimate(flops=2 * LAYERS * layer_flops, bytes_accessed=4 << 20, transcendentals=0),
        )(*operands)
        kept = (weights, cycles, rows)
        if level + 1 < levels:
            arrived[level + 1] = after(arrived[level + 1], hidden)
            swapped[level + 1] = between_cores(arrived[level + 1])
            if level + 2 < levels:
                arrived[level + 2] = hand_on(arrived[level + 1], level + 2)
    x, hidden = pl.pallas_call(
        renew_kernel,
        out_shape=(x_shape, h_shape),
        in_specs=[vmem] * 4,
        out_specs=(vmem, vmem),
        compiler_params=params,
    )(x, hidden, lift, proj)
    hidden = pl.pallas_call(
        second_kernel,
        grid=(segments,),
        out_shape=h_shape,
        in_specs=[
            vmem,
            pl.BlockSpec((1, 2, 4, 256, 384), lambda s: (s, 0, 0, 0, 0)),
            pl.BlockSpec((1, 1024, 768), lambda s: (s, 0, 0)),
            pl.BlockSpec((1, LAYERS, 8, 128), lambda s: (s, 0, 0, 0)),
        ],
        out_specs=vmem,
        scratch_shapes=state_scratch(),
        compiler_params=params,
        cost_estimate=pl.CostEstimate(flops=segments * LAYERS * layer_flops, bytes_accessed=16 << 20, transcendentals=0),
    )(hidden, weights, cycles, rows)
    kept, given = pl.pallas_call(
        result_kernel,
        out_shape=(jax.ShapeDtypeStruct((128, 128), jnp.bfloat16),) * 2,
        in_specs=[smem] + [vmem] * 3,
        out_specs=(vmem, vmem),
        scratch_shapes=[pltpu.VMEM((16, 2048), jnp.float32)],
        compiler_params=params,
    )(ids, x, hidden, proj)

    share = z_cells // segments
    got = between_cores(given)
    pair = jnp.where(slab_id == 0, jnp.stack([kept, got]), jnp.stack([got, kept]))
    pair = pair.reshape(slabs, levels, lines, share * 8, 128)
    mine = lax.dynamic_index_in_dim(pair, line, 2, keepdims=False)
    got = lax.ppermute(lax.dynamic_index_in_dim(pair, 1 - line, 2, keepdims=False), "segment", swap)
    crops = jnp.where(line == 0, jnp.concatenate([mine, got]), jnp.concatenate([got, mine]))
    out = jnp.where(segment_id < lines, crops[:, 0], 0)
    for level in range(1, levels):
        pairs = [(s, level * lines + s) for s in range(lines)]
        out = out + lax.ppermute(crops[:, level], "segment", pairs)
    out = out.reshape(crop_count, share, 8, STEPS, 4, 2, 8)[..., : 2 * comps]
    out = out.reshape(crop_count, share, 8, STEPS, 4, 2, 2, comps).transpose(3, 0, 7, 6, 4, 5, 2, 1)
    return out.reshape(STEPS, crop_count, comps, slab_rows, y_cells, share).astype(jnp.float32)


def solution(mesh):
    in_specs = (
        P("groups", None, "slab", None, None),
        P("groups", None),
        P(),
        P("segment", None, None, None, None),
        P("segment", None, None),
        P(),
    )
    out_specs = P(None, "groups", None, "slab", None, "segment")
    return jax.shard_map(shards, mesh=mesh, in_specs=in_specs, out_specs=out_specs, check_vma=False)
```

```python
import functools

import jax
import jax.numpy as jnp
from jax import lax
from jax.experimental import pallas as pl
from jax.experimental.pallas import tpu as pltpu
from jax.sharding import PartitionSpec as P

STEPS = 2
FIELD = 4096
LAYERS = 3
CH = 64
ROWS = 896
SLOTS = 16
VMEM_BYTES = 48 * 1024 * 1024

MOVES = (
    [(4 * b + m, 4 * b + 2 + m, 4 * m + b, 4 * m + 2 + b) for b in range(2) for m in range(2)],
    [(2 * m, 2 * m + 1, m, 4 + m) for m in range(4)],
    [(4 * p + 2 * m, 4 * p + 2 * m + 1, 2 * p + m, 2 * (2 + p) + m) for p in range(2) for m in range(2)],
)
CYCLES = (
    [list(range(8))],
    [list(range(4)), list(range(4, 8))],
    [[2 * r, 2 * r + 1] for r in range(4)],
)


def neighbour(layer, tile, step):
    cycle = next(cycle for cycle in CYCLES[layer] if tile in cycle)
    return cycle[(cycle.index(tile) + step) % len(cycle)]


def low_lanes(shape):
    return lax.broadcasted_iota(jnp.int32, shape, len(shape) - 1) < CH


def nt_dot(a, b):
    return lax.dot_general(a, b, (((1,), (1,)), ((), ())), preferred_element_type=jnp.float32)


def pack_kernel(raw_ref, bias_ref, eye_ref, packed):
    eye = eye_ref[...]
    low = low_lanes((CH, 128))
    for layer in range(LAYERS):
        for ty in range(3):
            pair = jnp.concatenate([raw_ref[layer, 3 + ty], raw_ref[layer, ty]], axis=0)
            packed[layer, ty * 192 : (ty + 1) * 192, :] = nt_dot(eye, pair).astype(jnp.bfloat16)
        pair = jnp.concatenate([raw_ref[layer, 6], raw_ref[layer, 7]], axis=0)
        packed[layer, 576:768, :] = nt_dot(eye, pair).astype(jnp.bfloat16)
        pair = jnp.concatenate([raw_ref[layer, 8], raw_ref[layer, 8]], axis=0)
        twice = nt_dot(eye, pair)
        packed[layer, 768:832, :] = jnp.where(low, twice[0:64], twice[64:128]).astype(jnp.bfloat16)
        terms = [term.astype(jnp.float32) for term in split_terms(bias_ref[layer : layer + 1, :])]
        terms = jnp.concatenate(terms + [jnp.zeros((CH - 3, CH), jnp.float32)], axis=0)
        terms = jnp.concatenate([terms, terms], axis=1)
        packed[layer, 832:896, :] = jnp.where(low, twice[128:192], terms).astype(jnp.bfloat16)


def pair_forms(taps):
    before, here, behind = taps
    ends = 0.25 * (before + behind)
    here = 0.25 * here
    return 0.5 * before, ends + here, ends - here, 0.5 * behind


def cycle_forms(taps):
    before, here, behind = taps
    ends = 0.125 * (before + behind)
    near = 0.125 * here
    return near + ends, near - ends, 0.25 * here, 0.25 * (behind - before)


def expand(packed, w_ref, bias_ref, layer):
    low = low_lanes((192, 128))
    zero = jnp.zeros((192, 128), jnp.float32)
    forms = pair_forms if layer < 2 else cycle_forms
    mids = forms([packed[ty * 192 : (ty + 1) * 192, :].astype(jnp.float32) for ty in range(3)])
    both = packed[576:768, :].astype(jnp.float32)
    ends = packed[768:832, :].astype(jnp.float32)
    rest = packed[832:896, :].astype(jnp.float32)
    ends = jnp.concatenate([ends, pltpu.roll(ends, CH, 1), rest], axis=0)
    lasts = forms([both, pltpu.roll(both, CH, 1), ends])
    for index, (mid, last) in enumerate(zip(mids, lasts)):
        rolled = pltpu.roll(mid, CH, 1)
        blocks = (
            mid,
            jnp.where(low, last, rolled),
            jnp.where(low, zero, pltpu.roll(last, CH, 1)),
            jnp.where(low, rolled, zero),
        )
        blocks = [block.astype(jnp.bfloat16) for block in blocks]
        for tz in range(3):
            for a in range(4):
                if layer < 2:
                    w_ref[index, a * CH : (a + 1) * CH, tz * 128 : (tz + 1) * 128] = blocks[a][tz * CH : (tz + 1) * CH]
                else:
                    row = index * 256 + a * CH
                    for half in range(2):
                        chosen = blocks[((0, 2), (1, 3), (2, 0), (3, 1))[a][half]]
                        column = tz * 256 + half * 128
                        w_ref[row : row + CH, column : column + 128] = chosen[tz * CH : (tz + 1) * CH]
    bias = 0.5 * (rest[0:1] + rest[1:2] + rest[2:3])
    bias = jnp.where(low_lanes((1, 128)), pltpu.roll(bias, CH, 1), bias)
    bias_ref[...] = jnp.broadcast_to(bias, (8, 128))


def z_moved(values, tap, layer):
    even, odd = values[:, :8], values[:, 8:]
    if layer > 0:
        shift = -tap * 2 ** (layer - 1) % 8
        return pltpu.roll(even, shift, 1), pltpu.roll(odd, shift, 1)
    if tap > 0:
        return odd, pltpu.roll(even, 7, 1)
    return pltpu.roll(odd, 1, 1), even


def z_summed(products, width, layer):
    products = products.reshape(products.shape[0] // 16, 16, products.shape[1])
    here = products[:, :, width : 2 * width]
    before = z_moved(products[:, :, :width], -1, layer)
    behind = z_moved(products[:, :, 2 * width :], 1, layer)
    parts = [here[:, 8 * i : 8 * i + 8] + before[i] + behind[i] for i in range(2)]
    return jnp.concatenate(parts, axis=1)


def activate_into(v_ref, tile, value, layer):
    activated = value * jnp.tanh(value) + value
    if layer < 2:
        d = 2**layer
        pairs = activated.reshape(8 // d, 2, d, 16, 128)
        first, second = pairs[:, 0], pairs[:, 1]
        before = jnp.concatenate([second[-1:], second[:-1]], axis=0)
        behind = jnp.concatenate([first[1:], first[:1]], axis=0)
        mixed = (before - second, first + second, second - first, first - behind)
    else:
        cycle = activated.reshape(4, 4, 16, 128)
        even, odd = cycle[0] + cycle[2], cycle[1] + cycle[3]
        sine = cycle[3] - cycle[1]
        mixed = (even + odd, even - odd, cycle[0] - cycle[2], sine, -sine)
    for index, value in enumerate(mixed):
        v_ref[index, tile] = value.reshape(-1, 128).astype(jnp.bfloat16)


def spread(move, u, v, state_out, v_ref, layer):
    low = low_lanes((16, 16, 128))
    for at, value in (
        (move[2], jnp.where(low, u, pltpu.roll(v, CH, 2))),
        (move[3], jnp.where(low, pltpu.roll(u, CH, 2), v)),
    ):
        state_out[at] = value
        activate_into(v_ref, at, value, layer)


def stream(accs, unit, steps):
    def push(at):
        pltpu.matmul_push_rhs(steps[at][0](), at % 2, unit)

    def take(results):
        for slot, use in results:
            use(pltpu.matmul_pop(accs[unit][slot]))

    push(0)
    waiting = ()
    for at, (weights, rows, results) in enumerate(steps):
        for index, (slot, value) in enumerate(rows):
            pltpu.matmul_acc_lhs(accs[unit][slot], value(), load_staged_rhs=at % 2 if index == 0 else None)
            if index == 0 and at + 1 < len(steps):
                push(at + 1)
        take(waiting)
        waiting = results
        yield
    take(waiting)


def convolve_pairs(v_ref, w_ref, layer, accs, finish):
    d = 2**layer
    low = low_lanes((128, 128))
    order = [tile for move in MOVES[layer + 1] for tile in move[:2]]

    def push(index):
        pltpu.matmul_push_rhs(w_ref[index, :, 0:256], index % 2, 0)
        last = w_ref[index, :, 256:384]
        pltpu.matmul_push_rhs(jnp.concatenate([last, last], axis=1), index % 2, 1)

    def taken(slot):
        both = pltpu.matmul_pop(accs[0][slot]).reshape(4, 16, 256)
        last = pltpu.matmul_pop(accs[1][slot]).reshape(4, 16, 256)
        before = z_moved(both[:, :, :128], -1, layer)
        behind = z_moved(last[:, :, :128], 1, layer)
        here = both[:, :, 128:]
        return jnp.concatenate([here[:, 8 * i : 8 * i + 8] + before[i] + behind[i] for i in range(2)], axis=1)

    first, second, waiting = {}, {}, []

    def take():
        index, tile, slots = waiting.pop(0)
        total = jnp.concatenate([taken(slot) for slot in slots], axis=0)
        if index == 0:
            first[tile] = total
        elif index == 1:
            first[tile], second[tile] = first[tile] + total, total
        elif index == 2:
            first[tile], second[tile] = first[tile] + total, second[tile] - total
        else:
            second[tile] = second[tile] - total
            halves = [half.reshape(8 // d, 1, d, 16, 128) for half in (first.pop(tile), second.pop(tile))]
            finish(tile, jnp.concatenate(halves, axis=1).reshape(16, 16, 128))

    push(0)
    for index in range(4):
        for at, tile in enumerate(order):
            after = v_ref[index, neighbour(layer, tile, 1)]
            before = v_ref[index, neighbour(layer, tile, -1)]
            rows = jnp.concatenate([v_ref[index, tile], jnp.where(low, after, before)], axis=1)
            base = 2 * ((8 * index + at) % (SLOTS // 2))
            for half in range(2):
                for acc in accs:
                    staged = index % 2 if at == 0 and half == 0 else None
                    pltpu.matmul_acc_lhs(acc[base + half], rows[64 * half : 64 * half + 64], load_staged_rhs=staged)
            waiting.append((index, tile, (base, base + 1)))
            if at == 2 and index < 3:
                push(index + 1)
            if len(waiting) == 7:
                take()
    while waiting:
        take()


def convolve_cycles(v_ref, w_ref, layer, accs, finish):
    sums = {}

    def rows(form, r):
        return lambda: jnp.concatenate([v_ref[form, 2 * r], v_ref[form, 2 * r + 1]], axis=1)

    def weights(row, tz):
        return lambda: w_ref[row * 256 : row * 256 + 256, tz * 256 : tz * 256 + 256]

    def adding(name, r, tz):
        def use(product):
            product = product.reshape(4, 16, 256)
            if tz != 1:
                product = jnp.concatenate(z_moved(product, tz - 1, layer), axis=1)
            sums[name, r] = sums[name, r] + product if (name, r) in sums else product

        return use

    def plain(form, tz, base):
        fed = [(base + r, rows(form, r)) for r in range(4)]
        return [(weights(form, tz), fed, [(base + r, adding(form, r, tz)) for r in range(4)])]

    def paired(tz, base):
        ends = [(base + r, adding(2, r, tz)) for r in range(4)] + [(base + 4 + r, adding(3, r, tz)) for r in range(4)]
        real = [(base + r, rows(2, r)) for r in range(4)] + [(base + 4 + r, rows(3, r)) for r in range(4)]
        other = [(base + r, rows(4, r)) for r in range(4)] + [(base + 4 + r, rows(2, r)) for r in range(4)]
        return [(weights(2, tz), real, ()), (weights(3, tz), other, ends)]

    ways = (
        paired(0, 0) + paired(1, 8) + plain(0, 0, 0),
        paired(2, 0) + plain(0, 1, 8) + plain(0, 2, 0) + plain(1, 0, 8) + plain(1, 1, 0) + plain(1, 2, 8),
    )
    streams = [stream(accs, unit, steps) for unit, steps in enumerate(ways)]
    while streams:
        streams = [one for one in streams if next(one, True) is None]
    for r in range(4):
        even, odd = sums[0, r] + sums[1, r], sums[0, r] - sums[1, r]
        cosine, sine = sums[2, r], sums[3, r]
        cells = jnp.stack([even + cosine, odd - sine, even - cosine, odd + sine]).reshape(16, 16, 256)
        for m in range(2):
            finish(2 * r + m, cells[:, :, m * 128 : m * 128 + 128])


def begin_section(state, v_refs):
    for move in MOVES[0]:
        spread(move, state[0][move[0]], state[0][move[1]], state[1], v_refs[0], 0)


def run_section(state, v_refs, w_refs, bias_refs, prepare):
    s_a, *held_in = state
    begin_section(state, v_refs)
    prepare(0)

    def layers(*accs):
        accs = accs[:SLOTS], accs[SLOTS:]
        for layer in range(LAYERS):
            held, following = held_in[layer], held_in[(layer + 1) % LAYERS]
            if layer + 1 < LAYERS:
                prepare(layer + 1)
            bias = bias_refs[layer][0:1][None]
            done = {}

            def finish(tile, total, layer=layer, held=held, following=following, bias=bias, done=done):
                total = held[tile] + bias + total
                if layer == LAYERS - 1:
                    s_a[tile] = total.astype(jnp.bfloat16).astype(jnp.float32)
                    return
                done[tile] = total
                for move in MOVES[layer + 1]:
                    if tile == move[1]:
                        spread(move, done.pop(move[0]), done.pop(tile), following, v_refs[layer + 1], layer + 1)

            convolve = convolve_cycles if layer == LAYERS - 1 else convolve_pairs
            convolve(v_refs[layer], w_refs[layer], layer, accs, finish)

    pl.run_scoped(layers, *[pltpu.ACC(unit)((64, 256), jnp.float32) for unit in range(2) for slot in range(SLOTS)])


def by_parity(x):
    row = lax.broadcasted_iota(jnp.int32, (128, 128), 0)
    lane = lax.broadcasted_iota(jnp.int32, (128, 128), 1)
    place = (row & 112) | ((row & 1) << 3) | ((row >> 1) & 7)
    turned = jnp.where(place == lane, 1.0, 0.0).astype(jnp.bfloat16)
    blocks = jnp.concatenate([x[:, at * 128 : (at + 1) * 128] for at in range(16)], axis=0)
    moved = sum(jnp.dot(term, turned, preferred_element_type=jnp.float32) for term in split_terms(blocks))
    return jnp.concatenate([moved[at * 16 : (at + 1) * 16] for at in range(16)], axis=1)


def lifted(x, lift):
    high = x.astype(jnp.bfloat16).astype(jnp.float32)
    columns = jnp.concatenate([high, x - high, high], axis=0).T.astype(jnp.bfloat16)
    hidden = jnp.dot(columns, lift, preferred_element_type=jnp.float32)
    return hidden.astype(jnp.bfloat16).reshape(8, 16, 16, 128)


def renewed_fields(x, proj_ref, hidden_ref):
    gain = nt_dot(proj_ref[...], hidden_ref[...].reshape(2048, 128))
    return x + gain[:16] + gain[16:32] + gain[32:48]


def renew_kernel(x_ref, hidden_ref, lift_ref, proj_ref, x_out, hidden_out):
    x = renewed_fields(x_ref[...], proj_ref, hidden_ref)
    x_out[...] = x
    hidden_out[...] = lifted(x, lift_ref[...])


def result_kernel(ids_ref, x_ref, hidden_ref, proj_ref, kept, given, x_new):
    x_new[...] = renewed_fields(x_ref[...], proj_ref, hidden_ref)
    kept[...] = cells_in_rows((x_ref, x_new), ids_ref[0])
    given[...] = cells_in_rows((x_ref, x_new), 1 - ids_ref[0])


def level_kernel(level, *refs):
    (ids_ref, own_0, own_1, far_0, far_1, entry) = refs[:6]
    (w_out, c_out, b_out, leaving, s_a, s_b, s_c, s_d, v_a, v_b, v_c) = refs[-16:-5]
    (packed, w_pair, w_cycle, b_all, sems) = refs[-5:]
    slab, line = ids_ref[0], ids_ref[1]
    s_a[...] = entry[...].astype(jnp.float32)
    state, v_refs = (s_a, s_b, s_c, s_d), (v_a, v_b, v_c)

    def copy(turn, part):
        at = 2 * level + turn
        source = (w_pair.at[turn, 0], w_pair.at[turn, 1], w_cycle.at[turn], b_all.at[turn])[part]
        target = (w_out.at[at, 0], w_out.at[at, 1], c_out.at[at], b_out.at[at])[part]
        return pltpu.make_async_copy(source, target, sems.at[turn, part])

    def section(turn, unused):
        for wanted, sources in ((True, (own_0, own_1)), (False, (far_0, far_1))):
            for core, source in enumerate(sources):

                @pl.when(((turn == line) == wanted) & (slab == core))
                def take(source=source):
                    packed[...] = source[...]

        w_refs = [w_pair.at[turn, 0], w_pair.at[turn, 1], w_cycle.at[turn]]

        def prepare(layer):
            expand(packed.at[layer], w_refs[layer], b_all.at[turn, layer], layer)
            copy(turn, layer).start()

        run_section(state, v_refs, w_refs, [b_all.at[turn, i] for i in range(LAYERS)], prepare)
        copy(turn, LAYERS).start()
        return 0

    lax.fori_loop(0, 2, section, 0)
    leaving[...] = s_a[...].astype(jnp.bfloat16)
    for turn in range(2):
        for part in range(LAYERS + 1):
            copy(turn, part).wait()


def feature_kernel(ids_ref, anchor_ref, kept_ref, got_ref, lift_ref, proj_ref, x_ref, lift_out, proj_out, hidden_out):
    slab, slot = ids_ref[0], ids_ref[2]
    kept, got = kept_ref[slot], got_ref[slot]
    halves = (jnp.where(slab == 0, kept, got), jnp.where(slab == 0, got, kept))
    columns = []
    for r in range(4):
        for m in range(2):
            columns.append(jnp.concatenate([halves[m][:, r], halves[m][:, 4 + r]], axis=0))
    current = jnp.concatenate([jnp.concatenate(columns, axis=1), jnp.zeros((10, 2048), jnp.float32)], axis=0)
    row = lax.broadcasted_iota(jnp.int32, (16, 2048), 0)
    column = lax.broadcasted_iota(jnp.int32, (16, 2048), 1)
    along_x = ((column >> 8) & 1) * 8 + (column >> 9) + jnp.where(row >= 9, 4, 0)
    along_x = along_x + anchor_ref[slot, 0]
    along_y = ((column >> 4) & 15) + anchor_ref[slot, 1]
    along_z = (column & 15) + anchor_ref[slot, 2]
    axis = jnp.where(row >= 9, row - 9, row - 6)
    position = jnp.where(axis == 0, along_x, jnp.where(axis == 1, along_y, along_z)) & (FIELD - 1)
    waves = jnp.sin(2.0 * jnp.pi * position.astype(jnp.float32) / FIELD)
    x = by_parity(jnp.where(row < 6, current, jnp.where(row < 12, waves, 0.0)))
    x_ref[...] = x

    def two_halves(part):
        blank = jnp.zeros(part.shape, jnp.float32)
        return [jnp.concatenate([part, blank], axis=1), jnp.concatenate([blank, part], axis=1)]

    lift = 0.5 * lift_ref[...]
    lift = two_halves(lift[0:3]) + two_halves(lift[3:6]) + [jnp.zeros((4, 128), jnp.float32)]
    first, second, unused = [term.astype(jnp.float32) for term in split_terms(jnp.concatenate(lift, axis=0))]
    lift = jnp.concatenate([first, first, second], axis=0).astype(jnp.bfloat16)
    lift_out[...] = lift
    hidden_out[...] = lifted(x, lift)
    proj = two_halves(2.0 * proj_ref[...]) + [jnp.zeros((10, 128), jnp.float32)]
    proj = [term.astype(jnp.float32) for term in split_terms(jnp.concatenate(proj, axis=0))]
    proj_out[...] = jnp.concatenate(proj, axis=0).astype(jnp.bfloat16)


def cells_in_rows(both, half):
    blocks = []
    for x_ref in both:
        for r in range(4):
            for upper in range(2):
                begin = pl.multiple_of(((2 * r + half) * 2 + upper) * 128, 128)
                blocks.append(x_ref[0:8, pl.ds(begin, 128)])
    row = lax.broadcasted_iota(jnp.int32, (128, 128), 0)
    lane = lax.broadcasted_iota(jnp.int32, (128, 128), 1)
    z = ((lane & 7) << 1) | ((lane >> 3) & 1)
    turned = ((row >> 3) == z) & ((row & 7) == (lane >> 4))
    turned = jnp.where(turned, 1.0, 0.0).astype(jnp.bfloat16)
    return nt_dot(turned, jnp.concatenate(blocks, axis=0).astype(jnp.bfloat16)).astype(jnp.bfloat16)


def second_kernel(entry, w_ref, c_ref, b_ref, leaving, s_a, s_b, s_c, s_d, v_a, v_b, v_c):
    s = pl.program_id(0)

    @pl.when(s == 0)
    def begin():
        s_a[...] = entry[...].astype(jnp.float32)

    w_refs = [w_ref.at[0, 0], w_ref.at[0, 1], c_ref.at[0]]
    biases = [b_ref.at[0, i] for i in range(LAYERS)]
    run_section((s_a, s_b, s_c, s_d), (v_a, v_b, v_c), w_refs, biases, lambda layer: None)

    @pl.when(s == pl.num_programs(0) - 1)
    def finish():
        leaving[...] = s_a[...].astype(jnp.bfloat16)


def split_terms(matrix):
    first = matrix.astype(jnp.bfloat16)
    rest = matrix - first.astype(jnp.float32)
    second = rest.astype(jnp.bfloat16)
    third = (rest - second.astype(jnp.float32)).astype(jnp.bfloat16)
    return first, second, third


def state_scratch():
    return (
        [pltpu.VMEM((8, 16, 16, 128), jnp.float32)] * 4
        + [pltpu.VMEM((4, 8, 128, 128), jnp.bfloat16)] * 2
        + [pltpu.VMEM((5, 8, 64, 128), jnp.bfloat16)]
    )


def shards(fields, anchors, lift_weight, conv_weight, conv_bias, proj_weight):
    segments = lax.axis_size("segment")
    slabs = lax.axis_size("slab")
    segment_id = lax.axis_index("segment")
    slab_id = lax.axis_index("slab")
    crop_count, comps, slab_rows, y_cells, z_cells = fields.shape
    lines = crop_count // slabs
    levels = segments // lines
    line = segment_id % lines
    slot = line * slabs + slab_id
    swap = [(0, 1), (1, 0)]
    vmem = pl.BlockSpec(memory_space=pltpu.VMEM)
    smem = pl.BlockSpec(memory_space=pltpu.SMEM)
    anyspace = pl.BlockSpec(memory_space=pl.ANY)
    params = pltpu.CompilerParams(vmem_limit_bytes=VMEM_BYTES)
    ids = jnp.stack([slab_id, line, slot]).astype(jnp.int32)

    def after(value, earlier):
        return lax.optimization_barrier((value, earlier))[0]

    def between_cores(value):
        return lax.ppermute(value, "slab", swap)

    packed = pl.pallas_call(
        pack_kernel,
        out_shape=jax.ShapeDtypeStruct((LAYERS, ROWS, 128), jnp.bfloat16),
        in_specs=[vmem] * 3,
        out_specs=vmem,
        compiler_params=params,
    )(conv_weight[0], conv_bias[0], jnp.eye(192, dtype=jnp.bfloat16))

    flat = after(fields, packed).reshape(crop_count, comps, slab_rows, y_cells * z_cells)
    h_shape = jax.ShapeDtypeStruct((8, 16, 16, 128), jnp.bfloat16)
    x_shape = jax.ShapeDtypeStruct((16, 2048), jnp.float32)
    x, lift, proj, hidden = pl.pallas_call(
        feature_kernel,
        out_shape=(
            x_shape,
            jax.ShapeDtypeStruct((48, 128), jnp.bfloat16),
            jax.ShapeDtypeStruct((48, 128), jnp.bfloat16),
            h_shape,
        ),
        in_specs=[smem, smem] + [vmem] * 4,
        out_specs=(vmem, vmem, vmem, vmem),
        compiler_params=params,
    )(ids, anchors, flat, between_cores(flat), lift_weight.T, proj_weight)

    w_shape = jax.ShapeDtypeStruct((segments, 2, 4, 256, 384), jnp.bfloat16)
    c_shape = jax.ShapeDtypeStruct((segments, 1024, 768), jnp.bfloat16)
    b_shape = jax.ShapeDtypeStruct((segments, LAYERS, 8, 128), jnp.float32)
    layer_flops = 2 * 4 * 1024 * 256 * 512
    def hand_on(value, level):
        pairs = [(s * slabs, (s - lines) * slabs) for s in range(lines, segments - lines * level)]
        pairs += [(0, slabs + 1), (slabs, 1)]
        return lax.ppermute(value, ("segment", "slab"), pairs)

    arrived = {0: after(hand_on(packed, 0), x)}
    swapped = {0: between_cores(arrived[0])}
    arrived[1] = hand_on(arrived[0], 1)
    kept = ()
    for level in range(levels):
        own = (packed, packed) if level == 0 else (arrived[level - 1], swapped[level - 1])
        operands = (ids, *own, swapped[level], arrived[level], hidden, *kept)
        weights, cycles, rows, hidden = pl.pallas_call(
            functools.partial(level_kernel, level),
            out_shape=(w_shape, c_shape, b_shape, h_shape),
            in_specs=[smem] + [vmem] * 5 + ([anyspace] * 3 if kept else []),
            out_specs=(anyspace, anyspace, anyspace, vmem),
            scratch_shapes=state_scratch()
            + [
                pltpu.VMEM((LAYERS, ROWS, 128), jnp.bfloat16),
                pltpu.VMEM((2, 2, 4, 256, 384), jnp.bfloat16),
                pltpu.VMEM((2, 1024, 768), jnp.bfloat16),
                pltpu.VMEM((2, LAYERS, 8, 128), jnp.float32),
                pltpu.SemaphoreType.DMA((2, LAYERS + 1)),
            ],
            input_output_aliases={6: 0, 7: 1, 8: 2} if kept else {},
            compiler_params=params,
            cost_estimate=pl.CostEstimate(flops=2 * LAYERS * layer_flops, bytes_accessed=4 << 20, transcendentals=0),
        )(*operands)
        kept = (weights, cycles, rows)
        if level + 1 < levels:
            arrived[level + 1] = after(arrived[level + 1], hidden)
            swapped[level + 1] = between_cores(arrived[level + 1])
            if level + 2 < levels:
                arrived[level + 2] = hand_on(arrived[level + 1], level + 2)
    x, hidden = pl.pallas_call(
        renew_kernel,
        out_shape=(x_shape, h_shape),
        in_specs=[vmem] * 4,
        out_specs=(vmem, vmem),
        compiler_params=params,
    )(x, hidden, lift, proj)
    hidden = pl.pallas_call(
        second_kernel,
        grid=(segments,),
        out_shape=h_shape,
        in_specs=[
            vmem,
            pl.BlockSpec((1, 2, 4, 256, 384), lambda s: (s, 0, 0, 0, 0)),
            pl.BlockSpec((1, 1024, 768), lambda s: (s, 0, 0)),
            pl.BlockSpec((1, LAYERS, 8, 128), lambda s: (s, 0, 0, 0)),
        ],
        out_specs=vmem,
        scratch_shapes=state_scratch(),
        compiler_params=params,
        cost_estimate=pl.CostEstimate(flops=segments * LAYERS * layer_flops, bytes_accessed=16 << 20, transcendentals=0),
    )(hidden, weights, cycles, rows)
    kept, given = pl.pallas_call(
        result_kernel,
        out_shape=(jax.ShapeDtypeStruct((128, 128), jnp.bfloat16),) * 2,
        in_specs=[smem] + [vmem] * 3,
        out_specs=(vmem, vmem),
        scratch_shapes=[pltpu.VMEM((16, 2048), jnp.float32)],
        compiler_params=params,
    )(ids, x, hidden, proj)

    share = z_cells // segments
    got = between_cores(given)
    pair = jnp.where(slab_id == 0, jnp.stack([kept, got]), jnp.stack([got, kept]))
    pair = pair.reshape(slabs, levels, lines, share * 8, 128)
    mine = lax.dynamic_index_in_dim(pair, line, 2, keepdims=False)
    got = lax.ppermute(lax.dynamic_index_in_dim(pair, 1 - line, 2, keepdims=False), "segment", swap)
    crops = jnp.where(line == 0, jnp.concatenate([mine, got]), jnp.concatenate([got, mine]))
    out = jnp.where(segment_id < lines, crops[:, 0], 0)
    for level in range(1, levels):
        pairs = [(s, level * lines + s) for s in range(lines)]
        out = out + lax.ppermute(crops[:, level], "segment", pairs)
    out = out.reshape(crop_count, share, 8, STEPS, 4, 2, 8)[..., : 2 * comps]
    out = out.reshape(crop_count, share, 8, STEPS, 4, 2, 2, comps).transpose(3, 0, 7, 6, 4, 5, 2, 1)
    return out.reshape(STEPS, crop_count, comps, slab_rows, y_cells, share).astype(jnp.float32)


def solution(mesh):
    in_specs = (
        P("groups", None, "slab", None, None),
        P("groups", None),
        P(),
        P("segment", None, None, None, None),
        P("segment", None, None),
        P(),
    )
    out_specs = P(None, "groups", None, "slab", None, "segment")
    return jax.shard_map(shards, mesh=mesh, in_specs=in_specs, out_specs=out_specs, check_vma=False)
```

```python
import functools

import jax
import jax.numpy as jnp
from jax import lax
from jax.experimental import pallas as pl
from jax.experimental.pallas import tpu as pltpu
from jax.sharding import PartitionSpec as P

STEPS = 2
FIELD = 4096
LAYERS = 3
CH = 64
ROWS = 896
VMEM_BYTES = 48 * 1024 * 1024

MOVES = (
    [(4 * b + m, 4 * b + 2 + m, 4 * m + b, 4 * m + 2 + b) for b in range(2) for m in range(2)],
    [(2 * m, 2 * m + 1, m, 4 + m) for m in range(4)],
    [(4 * p + 2 * m, 4 * p + 2 * m + 1, 2 * p + m, 2 * (2 + p) + m) for p in range(2) for m in range(2)],
)
CYCLES = (
    [list(range(8))],
    [list(range(4)), list(range(4, 8))],
    [[2 * r, 2 * r + 1] for r in range(4)],
)


GROUPS = ((0, 1), (2, 3))


def neighbour(layer, tile, step):
    cycle = next(cycle for cycle in CYCLES[layer] if tile in cycle)
    return cycle[(cycle.index(tile) + step) % len(cycle)]


def low_lanes(shape):
    return lax.broadcasted_iota(jnp.int32, shape, len(shape) - 1) < CH


def nt_dot(a, b):
    return lax.dot_general(a, b, (((1,), (1,)), ((), ())), preferred_element_type=jnp.float32)


def pack_kernel(raw_hbm, bias_hbm, packed, raw_ref, bias_ref, sems):
    copies = [pltpu.make_async_copy(raw_hbm.at[0, i], raw_ref.at[i], sems.at[i]) for i in range(LAYERS)]
    copies.append(pltpu.make_async_copy(bias_hbm, bias_ref, sems.at[LAYERS]))
    for copy in copies:
        copy.start()
    row = lax.broadcasted_iota(jnp.int32, (192, 192), 0)
    eye = jnp.where(row == lax.broadcasted_iota(jnp.int32, (192, 192), 1), 1.0, 0.0).astype(jnp.bfloat16)
    low = low_lanes((CH, 128))
    copies[LAYERS].wait()
    for layer in range(LAYERS):
        copies[layer].wait()
        for ty in range(3):
            pair = jnp.concatenate([raw_ref[layer, 3 + ty], raw_ref[layer, ty]], axis=0)
            packed[layer, ty * 192 : (ty + 1) * 192, :] = nt_dot(eye, pair).astype(jnp.bfloat16)
        pair = jnp.concatenate([raw_ref[layer, 6], raw_ref[layer, 7]], axis=0)
        packed[layer, 576:768, :] = nt_dot(eye, pair).astype(jnp.bfloat16)
        pair = jnp.concatenate([raw_ref[layer, 8], raw_ref[layer, 8]], axis=0)
        twice = nt_dot(eye, pair)
        packed[layer, 768:832, :] = jnp.where(low, twice[0:64], twice[64:128]).astype(jnp.bfloat16)
        terms = [term.astype(jnp.float32) for term in split_terms(bias_ref[layer])]
        terms = jnp.concatenate(terms + [jnp.zeros((CH - 3, CH), jnp.float32)], axis=0)
        terms = jnp.concatenate([terms, terms], axis=1)
        packed[layer, 832:896, :] = jnp.where(low, twice[128:192], terms).astype(jnp.bfloat16)


def pair_forms(taps):
    before, here, behind = taps
    ends = 0.25 * (before + behind)
    here = 0.25 * here
    return 0.5 * before, ends + here, ends - here, 0.5 * behind


def cycle_forms(taps):
    before, here, behind = taps
    ends = 0.125 * (before + behind)
    near = 0.125 * here
    return near + ends, near - ends, 0.25 * here, 0.25 * (behind - before)


def expand(packed, w_ref, bias_ref, layer):
    low = low_lanes((192, 128))
    zero = jnp.zeros((192, 128), jnp.float32)
    forms = pair_forms if layer < 2 else cycle_forms
    mids = forms([packed[ty * 192 : (ty + 1) * 192, :].astype(jnp.float32) for ty in range(3)])
    both = packed[576:768, :].astype(jnp.float32)
    ends = packed[768:832, :].astype(jnp.float32)
    rest = packed[832:896, :].astype(jnp.float32)
    ends = jnp.concatenate([ends, pltpu.roll(ends, CH, 1), rest], axis=0)
    lasts = forms([both, pltpu.roll(both, CH, 1), ends])
    for index, (mid, last) in enumerate(zip(mids, lasts)):
        rolled = pltpu.roll(mid, CH, 1)
        blocks = (
            mid,
            jnp.where(low, last, rolled),
            jnp.where(low, zero, pltpu.roll(last, CH, 1)),
            jnp.where(low, rolled, zero),
        )
        blocks = [block.astype(jnp.bfloat16) for block in blocks]
        for tz in range(3):
            for a in range(4):
                if layer < 2:
                    w_ref[index, a * CH : (a + 1) * CH, tz * 128 : (tz + 1) * 128] = blocks[a][tz * CH : (tz + 1) * CH]
                else:
                    row = index * 256 + a * CH
                    for half in range(2):
                        chosen = blocks[((0, 2), (1, 3), (2, 0), (3, 1))[a][half]]
                        column = tz * 256 + half * 128
                        w_ref[row : row + CH, column : column + 128] = chosen[tz * CH : (tz + 1) * CH]
    bias = 0.5 * (rest[0:1] + rest[1:2] + rest[2:3])
    bias = jnp.where(low_lanes((1, 128)), pltpu.roll(bias, CH, 1), bias)
    bias_ref[...] = jnp.broadcast_to(bias, (8, 128))


def z_moved(values, tap, layer):
    even, odd = values[:, :8], values[:, 8:]
    if layer > 0:
        shift = -tap * 2 ** (layer - 1) % 8
        return pltpu.roll(even, shift, 1), pltpu.roll(odd, shift, 1)
    if tap > 0:
        return odd, pltpu.roll(even, 7, 1)
    return pltpu.roll(odd, 1, 1), even


def z_summed(products, width, layer):
    products = products.reshape(products.shape[0] // 16, 16, products.shape[1])
    here = products[:, :, width : 2 * width]
    before = z_moved(products[:, :, :width], -1, layer)
    behind = z_moved(products[:, :, 2 * width :], 1, layer)
    parts = [here[:, 8 * i : 8 * i + 8] + before[i] + behind[i] for i in range(2)]
    return jnp.concatenate(parts, axis=1)


def activate_into(v_ref, tile, value, layer):
    activated = value * jnp.tanh(value) + value
    if layer < 2:
        d = 2**layer
        pairs = activated.reshape(8 // d, 2, d, 16, 128)
        first, second = pairs[:, 0], pairs[:, 1]
        before = jnp.concatenate([second[-1:], second[:-1]], axis=0)
        behind = jnp.concatenate([first[1:], first[:1]], axis=0)
        mixed = (before - second, first + second, second - first, first - behind)
    else:
        cycle = activated.reshape(4, 4, 16, 128)
        even, odd = cycle[0] + cycle[2], cycle[1] + cycle[3]
        sine = cycle[3] - cycle[1]
        mixed = (even + odd, even - odd, cycle[0] - cycle[2], sine, -sine)
    for index, value in enumerate(mixed):
        v_ref[index, tile] = value.reshape(-1, 128).astype(jnp.bfloat16)


def spread(move, u, v, state_out, v_ref, layer):
    low = low_lanes((16, 16, 128))
    for at, value in (
        (move[2], jnp.where(low, u, pltpu.roll(v, CH, 2))),
        (move[3], jnp.where(low, pltpu.roll(u, CH, 2), v)),
    ):
        state_out[at] = value
        activate_into(v_ref, at, value, layer)


def convolve_pairs(v_ref, w_ref, tiles, layer):
    d = 2**layer
    low = low_lanes((128, 128))
    sums = []
    for index in range(4):
        rows = []
        for tile in tiles:
            after = v_ref[index, neighbour(layer, tile, 1)]
            before = v_ref[index, neighbour(layer, tile, -1)]
            rows.append(jnp.concatenate([v_ref[index, tile], jnp.where(low, after, before)], axis=1))
        rows = jnp.concatenate(rows, axis=0)
        sums.append(z_summed(jnp.dot(rows, w_ref[index], preferred_element_type=jnp.float32), 128, layer))
    first = sums[0] + sums[1] + sums[2]
    second = sums[1] - sums[2] - sums[3]
    results = []
    for at in range(len(tiles)):
        halves = [half[at * 8 : (at + 1) * 8].reshape(8 // d, 1, d, 16, 128) for half in (first, second)]
        results.append(jnp.concatenate(halves, axis=1).reshape(16, 16, 128))
    return results


def convolve_cycles(v_ref, w_ref, units, layer):
    def rows(*forms):
        parts = [jnp.concatenate([v_ref[form, 2 * r + m] for form in forms for m in range(2)], axis=1) for r in units]
        return jnp.concatenate(parts, axis=0)

    def summed(lhs, begin, end):
        return z_summed(jnp.dot(lhs, w_ref[begin:end, :], preferred_element_type=jnp.float32), 256, layer)

    flat = summed(rows(0), 0, 256)
    alternate = summed(rows(1), 256, 512)
    waves = summed(jnp.concatenate([rows(2, 4), rows(3, 2)], axis=0), 512, 1024)
    count = 4 * len(units)
    cosine, sine = waves[:count], waves[count:]
    even, odd = flat + alternate, flat - alternate
    cells = [value.reshape(len(units), 1, 4, 16, 256) for value in (even + cosine, odd - sine, even - cosine, odd + sine)]
    cells = jnp.concatenate(cells, axis=1).reshape(len(units), 16, 16, 256)
    return [cells[at, :, :, m * 128 : m * 128 + 128] for at in range(len(units)) for m in range(2)]


def begin_section(state, v_refs):
    for move in MOVES[0]:
        spread(move, state[0][move[0]], state[0][move[1]], state[1], v_refs[0], 0)


def run_section(state, v_refs, w_refs, bias_refs, prepare):
    s_a, *held_in = state
    begin_section(state, v_refs)
    prepare(0)
    for layer in range(LAYERS):
        held, following = held_in[layer], held_in[(layer + 1) % LAYERS]
        if layer + 1 < LAYERS:
            prepare(layer + 1)
        bias = bias_refs[layer][0:1][None]
        if layer == LAYERS - 1:
            for tile, total in enumerate(convolve_cycles(v_refs[2], w_refs[layer], range(4), layer)):
                s_a[tile] = (held[tile] + bias + total).astype(jnp.bfloat16).astype(jnp.float32)
            break
        for chosen in GROUPS:
            moves = [MOVES[layer + 1][at] for at in chosen]
            tiles = [tile for move in moves for tile in move[:2]]
            sums = convolve_pairs(v_refs[layer], w_refs[layer], tiles, layer)
            sums = [held[tile] + bias + total for tile, total in zip(tiles, sums)]
            for at, move in enumerate(moves):
                spread(move, sums[2 * at], sums[2 * at + 1], following, v_refs[layer + 1], layer + 1)


def by_parity(x):
    row = lax.broadcasted_iota(jnp.int32, (128, 128), 0)
    lane = lax.broadcasted_iota(jnp.int32, (128, 128), 1)
    place = (row & 112) | ((row & 1) << 3) | ((row >> 1) & 7)
    turned = jnp.where(place == lane, 1.0, 0.0).astype(jnp.bfloat16)
    blocks = jnp.concatenate([x[:, at * 128 : (at + 1) * 128] for at in range(16)], axis=0)
    moved = sum(jnp.dot(term, turned, preferred_element_type=jnp.float32) for term in split_terms(blocks))
    return jnp.concatenate([moved[at * 16 : (at + 1) * 16] for at in range(16)], axis=1)


def lift_into(x, lift_ref, s_a):
    high = x.astype(jnp.bfloat16).astype(jnp.float32)
    columns = jnp.concatenate([high, x - high, high], axis=0).T.astype(jnp.bfloat16)
    hidden = jnp.dot(columns, lift_ref[...], preferred_element_type=jnp.float32)
    s_a[...] = hidden.astype(jnp.bfloat16).astype(jnp.float32).reshape(8, 16, 16, 128)


def renewed_fields(x, proj_ref, s_a):
    gain = nt_dot(proj_ref[...], s_a[...].reshape(2048, 128).astype(jnp.bfloat16))
    return x + gain[:16] + gain[16:32] + gain[32:48]


def level_kernel(level, first, last, *refs):
    (ids_ref, own_0, own_1, far_0, far_1, x_ref, lift_ref, proj_ref) = refs[:8]
    (w_out, c_out, b_out, leaving, x_out, s_a, s_b, s_c, s_d, v_a, v_b, v_c) = refs[-17:-5]
    (packed, w_pair, w_cycle, b_all, sems) = refs[-5:]
    slab, line = ids_ref[0], ids_ref[1]
    x = by_parity(x_ref[...]) if first else x_ref[...]
    if first:
        lift_into(x, lift_ref, s_a)
    else:
        s_a[...] = refs[8][...].astype(jnp.float32)
    state, v_refs = (s_a, s_b, s_c, s_d), (v_a, v_b, v_c)

    def copy(turn, part):
        at = 2 * level + turn
        source = (w_pair.at[turn, 0], w_pair.at[turn, 1], w_cycle.at[turn], b_all.at[turn])[part]
        target = (w_out.at[at, 0], w_out.at[at, 1], c_out.at[at], b_out.at[at])[part]
        return pltpu.make_async_copy(source, target, sems.at[turn, part])

    def section(turn, unused):
        for wanted, sources in ((True, (own_0, own_1)), (False, (far_0, far_1))):
            for core, source in enumerate(sources):

                @pl.when(((turn == line) == wanted) & (slab == core))
                def take(source=source):
                    packed[...] = source[...]

        w_refs = [w_pair.at[turn, 0], w_pair.at[turn, 1], w_cycle.at[turn]]

        def prepare(layer):
            expand(packed.at[layer], w_refs[layer], b_all.at[turn, layer], layer)
            copy(turn, layer).start()

        run_section(state, v_refs, w_refs, [b_all.at[turn, i] for i in range(LAYERS)], prepare)
        copy(turn, LAYERS).start()
        return 0

    lax.fori_loop(0, 2, section, 0)
    leaving[...] = s_a[...].astype(jnp.bfloat16)
    x_out[...] = renewed_fields(x, proj_ref, s_a) if last else x
    for turn in range(2):
        for part in range(LAYERS + 1):
            copy(turn, part).wait()


def feature_kernel(ids_ref, anchor_ref, kept_ref, got_ref, lift_ref, proj_ref, x_ref, lift_out, proj_out):
    slab, slot = ids_ref[0], ids_ref[2]
    kept, got = kept_ref[slot], got_ref[slot]
    halves = (jnp.where(slab == 0, kept, got), jnp.where(slab == 0, got, kept))
    columns = []
    for r in range(4):
        for m in range(2):
            columns.append(jnp.concatenate([halves[m][:, r], halves[m][:, 4 + r]], axis=0))
    current = jnp.concatenate([jnp.concatenate(columns, axis=1), jnp.zeros((10, 2048), jnp.float32)], axis=0)
    row = lax.broadcasted_iota(jnp.int32, (16, 2048), 0)
    column = lax.broadcasted_iota(jnp.int32, (16, 2048), 1)
    along_x = ((column >> 8) & 1) * 8 + (column >> 9) + jnp.where(row >= 9, 4, 0)
    along_x = along_x + anchor_ref[slot, 0]
    along_y = ((column >> 4) & 15) + anchor_ref[slot, 1]
    along_z = (column & 15) + anchor_ref[slot, 2]
    axis = jnp.where(row >= 9, row - 9, row - 6)
    position = jnp.where(axis == 0, along_x, jnp.where(axis == 1, along_y, along_z)) & (FIELD - 1)
    waves = jnp.sin(2.0 * jnp.pi * position.astype(jnp.float32) / FIELD)
    x_ref[...] = jnp.where(row < 6, current, jnp.where(row < 12, waves, 0.0))

    def two_halves(part):
        blank = jnp.zeros(part.shape, jnp.float32)
        return [jnp.concatenate([part, blank], axis=1), jnp.concatenate([blank, part], axis=1)]

    lift = 0.5 * lift_ref[...]
    lift = two_halves(lift[0:3]) + two_halves(lift[3:6]) + [jnp.zeros((4, 128), jnp.float32)]
    first, second, unused = [term.astype(jnp.float32) for term in split_terms(jnp.concatenate(lift, axis=0))]
    lift_out[...] = jnp.concatenate([first, first, second], axis=0).astype(jnp.bfloat16)
    proj = two_halves(2.0 * proj_ref[...]) + [jnp.zeros((10, 128), jnp.float32)]
    proj = [term.astype(jnp.float32) for term in split_terms(jnp.concatenate(proj, axis=0))]
    proj_out[...] = jnp.concatenate(proj, axis=0).astype(jnp.bfloat16)


def cells_in_rows(both, half):
    blocks = []
    for x_ref in both:
        for r in range(4):
            for upper in range(2):
                begin = pl.multiple_of(((2 * r + half) * 2 + upper) * 128, 128)
                blocks.append(x_ref[0:8, pl.ds(begin, 128)])
    row = lax.broadcasted_iota(jnp.int32, (128, 128), 0)
    lane = lax.broadcasted_iota(jnp.int32, (128, 128), 1)
    z = ((lane & 7) << 1) | ((lane >> 3) & 1)
    turned = ((row >> 3) == z) & ((row & 7) == (lane >> 4))
    turned = jnp.where(turned, 1.0, 0.0).astype(jnp.bfloat16)
    return nt_dot(turned, jnp.concatenate(blocks, axis=0).astype(jnp.bfloat16)).astype(jnp.bfloat16)


def second_kernel(ids_ref, x_ref, lift_ref, proj_ref, w_ref, c_ref, b_ref, kept, given, s_a, s_b, s_c, s_d, v_a, v_b, v_c, x_new):
    s = pl.program_id(0)

    state, v_refs = (s_a, s_b, s_c, s_d), (v_a, v_b, v_c)

    @pl.when(s == 0)
    def begin():
        lift_into(x_ref[...], lift_ref, s_a)

    w_refs = [w_ref.at[0, 0], w_ref.at[0, 1], c_ref.at[0]]
    run_section(state, v_refs, w_refs, [b_ref.at[0, i] for i in range(LAYERS)], lambda layer: None)

    @pl.when(s == pl.num_programs(0) - 1)
    def finish():
        x_new[...] = renewed_fields(x_ref[...], proj_ref, s_a)
        kept[...] = cells_in_rows((x_ref, x_new), ids_ref[0])
        given[...] = cells_in_rows((x_ref, x_new), 1 - ids_ref[0])


def place_kernel(share, *refs):
    ids_ref, own, *others, out_ref = refs
    y_cells = out_ref.shape[-1]
    first = ids_ref[3] == 0
    got = others[0][...]
    for other in others[1:]:
        got = got + other[...]
    count = 48 * share
    row = lax.broadcasted_iota(jnp.int32, (count, 128), 0) >> (share.bit_length() - 1)
    lane = lax.broadcasted_iota(jnp.int32, (count, 128), 1)
    step = jnp.where(row >= 24, 1, 0)
    place = step * 64 + (row & 3) * 16 + ((row >> 2) & 1) * 3 + ((row >> 3) - 3 * step)
    chosen = [jnp.where(lane == place + 8 * upper, 1.0, 0.0).astype(jnp.bfloat16) for upper in range(2)]
    own_z = lax.broadcasted_iota(jnp.int32, (count, y_cells), 0) & (share - 1)
    for crop in range(own.shape[0]):
        piece = jnp.where(first, own[crop].astype(jnp.float32), got[crop].astype(jnp.float32)).astype(jnp.bfloat16)
        lower, upper = [nt_dot(one, piece) for one in chosen]
        cells = jnp.zeros((count, y_cells), jnp.float32)
        for z in range(share):
            both = jnp.concatenate([lower[:, 8 * z : 8 * z + 8], upper[:, 8 * z : 8 * z + 8]], axis=1)
            cells = jnp.where(own_z == z, both, cells)
        for step in range(STEPS):
            for comp in range(3):
                for x in range(8):
                    begin = ((3 * step + comp) * 8 + x) * share
                    out_ref[step, crop, comp, x] = cells[begin : begin + share]


def split_terms(matrix):
    first = matrix.astype(jnp.bfloat16)
    rest = matrix - first.astype(jnp.float32)
    second = rest.astype(jnp.bfloat16)
    third = (rest - second.astype(jnp.float32)).astype(jnp.bfloat16)
    return first, second, third


def state_scratch():
    return (
        [pltpu.VMEM((8, 16, 16, 128), jnp.float32)] * 4
        + [pltpu.VMEM((4, 8, 128, 128), jnp.bfloat16)] * 2
        + [pltpu.VMEM((5, 8, 64, 128), jnp.bfloat16)]
    )


def shards(fields, anchors, lift_weight, conv_weight, conv_bias, proj_weight):
    segments = lax.axis_size("segment")
    slabs = lax.axis_size("slab")
    segment_id = lax.axis_index("segment")
    slab_id = lax.axis_index("slab")
    crop_count, comps, slab_rows, y_cells, z_cells = fields.shape
    lines = crop_count // slabs
    levels = segments // lines
    line = segment_id % lines
    slot = line * slabs + slab_id
    swap = [(0, 1), (1, 0)]
    vmem = pl.BlockSpec(memory_space=pltpu.VMEM)
    smem = pl.BlockSpec(memory_space=pltpu.SMEM)
    anyspace = pl.BlockSpec(memory_space=pl.ANY)
    params = pltpu.CompilerParams(vmem_limit_bytes=VMEM_BYTES)
    ids = jnp.stack([slab_id, line, slot, segment_id // lines]).astype(jnp.int32)

    def after(value, earlier):
        return lax.optimization_barrier((value, earlier))[0]

    def between_cores(value):
        return lax.ppermute(value, "slab", swap)

    packed = pl.pallas_call(
        pack_kernel,
        out_shape=jax.ShapeDtypeStruct((LAYERS, ROWS, 128), jnp.bfloat16),
        in_specs=[pl.BlockSpec(memory_space=pltpu.HBM)] * 2,
        out_specs=vmem,
        scratch_shapes=[
            pltpu.VMEM(conv_weight.shape[1:], jnp.bfloat16),
            pltpu.VMEM((LAYERS, 1, CH), jnp.float32),
            pltpu.SemaphoreType.DMA((LAYERS + 1,)),
        ],
        compiler_params=params,
    )(conv_weight, conv_bias.transpose(1, 0, 2))

    flat = after(fields, packed).reshape(crop_count, comps, slab_rows, y_cells * z_cells)
    x, lift, proj = pl.pallas_call(
        feature_kernel,
        out_shape=(
            jax.ShapeDtypeStruct((16, 2048), jnp.float32),
            jax.ShapeDtypeStruct((48, 128), jnp.bfloat16),
            jax.ShapeDtypeStruct((48, 128), jnp.bfloat16),
        ),
        in_specs=[smem, smem] + [vmem] * 4,
        out_specs=(vmem, vmem, vmem),
        compiler_params=params,
    )(ids, anchors, flat, between_cores(flat), lift_weight.T, proj_weight)

    w_shape = jax.ShapeDtypeStruct((segments, 2, 4, 256, 384), jnp.bfloat16)
    c_shape = jax.ShapeDtypeStruct((segments, 1024, 768), jnp.bfloat16)
    b_shape = jax.ShapeDtypeStruct((segments, LAYERS, 8, 128), jnp.float32)
    h_shape = jax.ShapeDtypeStruct((8, 16, 16, 128), jnp.bfloat16)
    x_shape = jax.ShapeDtypeStruct((16, 2048), jnp.float32)
    layer_flops = 2 * 4 * 1024 * 256 * 512
    def hand_on(value, level):
        pairs = [(s * slabs, (s - lines) * slabs) for s in range(lines, segments - lines * level)]
        pairs += [(0, slabs + 1), (slabs, 1)]
        return lax.ppermute(value, ("segment", "slab"), pairs)

    arrived = {0: after(hand_on(packed, 0), x)}
    swapped = {0: between_cores(arrived[0])}
    arrived[1] = hand_on(arrived[0], 1)
    kept = ()
    current = x
    for level in range(levels):
        own = (packed, packed) if level == 0 else (arrived[level - 1], swapped[level - 1])
        operands = (ids, *own, swapped[level], arrived[level], current, lift, proj, *kept)
        weights, cycles, rows, hidden, current = pl.pallas_call(
            functools.partial(level_kernel, level, level == 0, level == levels - 1),
            out_shape=(w_shape, c_shape, b_shape, h_shape, x_shape),
            in_specs=[smem] + [vmem] * 7 + ([vmem] + [anyspace] * 3 if kept else []),
            out_specs=(anyspace, anyspace, anyspace, vmem, vmem),
            scratch_shapes=state_scratch()
            + [
                pltpu.VMEM((LAYERS, ROWS, 128), jnp.bfloat16),
                pltpu.VMEM((2, 2, 4, 256, 384), jnp.bfloat16),
                pltpu.VMEM((2, 1024, 768), jnp.bfloat16),
                pltpu.VMEM((2, LAYERS, 8, 128), jnp.float32),
                pltpu.SemaphoreType.DMA((2, LAYERS + 1)),
            ],
            input_output_aliases={9: 0, 10: 1, 11: 2} if kept else {},
            compiler_params=params,
            cost_estimate=pl.CostEstimate(flops=2 * LAYERS * layer_flops, bytes_accessed=4 << 20, transcendentals=0),
        )(*operands)
        kept = (hidden, weights, cycles, rows)
        if level + 1 < levels:
            arrived[level + 1] = after(arrived[level + 1], hidden)
            swapped[level + 1] = between_cores(arrived[level + 1])
            if level + 2 < levels:
                arrived[level + 2] = hand_on(arrived[level + 1], level + 2)
    first_result = current
    kept, given = pl.pallas_call(
        second_kernel,
        grid=(segments,),
        out_shape=(jax.ShapeDtypeStruct((128, 128), jnp.bfloat16),) * 2,
        in_specs=[smem]
        + [vmem] * 3
        + [
            pl.BlockSpec((1, 2, 4, 256, 384), lambda s: (s, 0, 0, 0, 0)),
            pl.BlockSpec((1, 1024, 768), lambda s: (s, 0, 0)),
            pl.BlockSpec((1, LAYERS, 8, 128), lambda s: (s, 0, 0, 0)),
        ],
        out_specs=(vmem, vmem),
        scratch_shapes=state_scratch() + [pltpu.VMEM((16, 2048), jnp.float32)],
        compiler_params=params,
        cost_estimate=pl.CostEstimate(flops=segments * LAYERS * layer_flops, bytes_accessed=16 << 20, transcendentals=0),
    )(ids, first_result, lift, proj, weights, cycles, rows)

    share = z_cells // segments
    got = between_cores(given)
    pair = jnp.where(slab_id == 0, jnp.stack([kept, got]), jnp.stack([got, kept]))
    pair = pair.reshape(slabs, levels, lines, share * 8, 128)
    mine = lax.dynamic_index_in_dim(pair, line, 2, keepdims=False)
    got = lax.ppermute(lax.dynamic_index_in_dim(pair, 1 - line, 2, keepdims=False), "segment", swap)
    crops = jnp.where(line == 0, jnp.concatenate([mine, got]), jnp.concatenate([got, mine]))
    pieces = [crops[:, 0]]
    for level in range(1, levels):
        pairs = [(s, level * lines + s) for s in range(lines)]
        pieces.append(lax.ppermute(crops[:, level], "segment", pairs))
    out = pl.pallas_call(
        functools.partial(place_kernel, share),
        out_shape=jax.ShapeDtypeStruct((STEPS, crop_count, comps, slab_rows, share, y_cells), jnp.float32),
        in_specs=[smem] + [vmem] * levels,
        out_specs=vmem,
        compiler_params=params,
    )(ids, *pieces)
    return out.transpose(0, 1, 2, 3, 5, 4)


def solution(mesh):
    in_specs = (
        P("groups", None, "slab", None, None),
        P("groups", None),
        P(),
        P("segment", None, None, None, None),
        P("segment", None, None),
        P(),
    )
    out_specs = P(None, "groups", None, "slab", None, "segment")
    return jax.shard_map(shards, mesh=mesh, in_specs=in_specs, out_specs=out_specs, check_vma=False)
```

```python
import functools

import jax
import jax.numpy as jnp
from jax import lax
from jax.experimental import pallas as pl
from jax.experimental.pallas import tpu as pltpu
from jax.sharding import PartitionSpec as P

STEPS = 2
FIELD = 4096
LAYERS = 3
CH = 64
ROWS = 896
VMEM_BYTES = 48 * 1024 * 1024

MOVES = (
    [(4 * b + m, 4 * b + 2 + m, 4 * m + b, 4 * m + 2 + b) for b in range(2) for m in range(2)],
    [(2 * m, 2 * m + 1, m, 4 + m) for m in range(4)],
    [(4 * p + 2 * m, 4 * p + 2 * m + 1, 2 * p + m, 2 * (2 + p) + m) for p in range(2) for m in range(2)],
)
CYCLES = (
    [list(range(8))],
    [list(range(4)), list(range(4, 8))],
    [[2 * r, 2 * r + 1] for r in range(4)],
)


GROUPS = ((0,), (1,), (2,), (3,))


def neighbour(layer, tile, step):
    cycle = next(cycle for cycle in CYCLES[layer] if tile in cycle)
    return cycle[(cycle.index(tile) + step) % len(cycle)]


def low_lanes(shape):
    return lax.broadcasted_iota(jnp.int32, shape, len(shape) - 1) < CH


def nt_dot(a, b):
    return lax.dot_general(a, b, (((1,), (1,)), ((), ())), preferred_element_type=jnp.float32)


def pack_kernel(raw_ref, bias_ref, eye_ref, packed):
    eye = eye_ref[...]
    low = low_lanes((CH, 128))
    for layer in range(LAYERS):
        for ty in range(3):
            pair = jnp.concatenate([raw_ref[layer, 3 + ty], raw_ref[layer, ty]], axis=0)
            packed[layer, ty * 192 : (ty + 1) * 192, :] = nt_dot(eye, pair).astype(jnp.bfloat16)
        pair = jnp.concatenate([raw_ref[layer, 6], raw_ref[layer, 7]], axis=0)
        packed[layer, 576:768, :] = nt_dot(eye, pair).astype(jnp.bfloat16)
        pair = jnp.concatenate([raw_ref[layer, 8], raw_ref[layer, 8]], axis=0)
        twice = nt_dot(eye, pair)
        packed[layer, 768:832, :] = jnp.where(low, twice[0:64], twice[64:128]).astype(jnp.bfloat16)
        terms = [term.astype(jnp.float32) for term in split_terms(bias_ref[layer])]
        terms = jnp.concatenate(terms + [jnp.zeros((CH - 3, CH), jnp.float32)], axis=0)
        terms = jnp.concatenate([terms, terms], axis=1)
        packed[layer, 832:896, :] = jnp.where(low, twice[128:192], terms).astype(jnp.bfloat16)


def pair_forms(taps):
    before, here, behind = taps
    ends = 0.25 * (before + behind)
    here = 0.25 * here
    return 0.5 * before, ends + here, ends - here, 0.5 * behind


def cycle_forms(taps):
    before, here, behind = taps
    ends = 0.125 * (before + behind)
    near = 0.125 * here
    return near + ends, near - ends, 0.25 * here, 0.25 * (behind - before)


def expand(packed, w_ref, bias_ref, layer):
    low = low_lanes((192, 128))
    zero = jnp.zeros((192, 128), jnp.float32)
    forms = pair_forms if layer < 2 else cycle_forms
    mids = forms([packed[ty * 192 : (ty + 1) * 192, :].astype(jnp.float32) for ty in range(3)])
    both = packed[576:768, :].astype(jnp.float32)
    ends = packed[768:832, :].astype(jnp.float32)
    rest = packed[832:896, :].astype(jnp.float32)
    ends = jnp.concatenate([ends, pltpu.roll(ends, CH, 1), rest], axis=0)
    lasts = forms([both, pltpu.roll(both, CH, 1), ends])
    for index, (mid, last) in enumerate(zip(mids, lasts)):
        rolled = pltpu.roll(mid, CH, 1)
        blocks = (
            mid,
            jnp.where(low, last, rolled),
            jnp.where(low, zero, pltpu.roll(last, CH, 1)),
            jnp.where(low, rolled, zero),
        )
        blocks = [block.astype(jnp.bfloat16) for block in blocks]
        for tz in range(3):
            for a in range(4):
                if layer < 2:
                    w_ref[index, a * CH : (a + 1) * CH, tz * 128 : (tz + 1) * 128] = blocks[a][tz * CH : (tz + 1) * CH]
                else:
                    row = index * 256 + a * CH
                    for half in range(2):
                        chosen = blocks[((0, 2), (1, 3), (2, 0), (3, 1))[a][half]]
                        column = tz * 256 + half * 128
                        w_ref[row : row + CH, column : column + 128] = chosen[tz * CH : (tz + 1) * CH]
    bias = 0.5 * (rest[0:1] + rest[1:2] + rest[2:3])
    bias = jnp.where(low_lanes((1, 128)), pltpu.roll(bias, CH, 1), bias)
    bias_ref[...] = jnp.broadcast_to(bias, (8, 128))


def z_moved(values, tap, layer):
    even, odd = values[:, :8], values[:, 8:]
    if layer > 0:
        shift = -tap * 2 ** (layer - 1) % 8
        return pltpu.roll(even, shift, 1), pltpu.roll(odd, shift, 1)
    if tap > 0:
        return odd, pltpu.roll(even, 7, 1)
    return pltpu.roll(odd, 1, 1), even


def z_summed(products, width, layer):
    products = products.reshape(products.shape[0] // 16, 16, products.shape[1])
    here = products[:, :, width : 2 * width]
    before = z_moved(products[:, :, :width], -1, layer)
    behind = z_moved(products[:, :, 2 * width :], 1, layer)
    parts = [here[:, 8 * i : 8 * i + 8] + before[i] + behind[i] for i in range(2)]
    return jnp.concatenate(parts, axis=1)


def activate_into(v_ref, tile, value, layer):
    activated = value * jnp.tanh(value) + value
    if layer < 2:
        d = 2**layer
        pairs = activated.reshape(8 // d, 2, d, 16, 128)
        first, second = pairs[:, 0], pairs[:, 1]
        before = jnp.concatenate([second[-1:], second[:-1]], axis=0)
        behind = jnp.concatenate([first[1:], first[:1]], axis=0)
        mixed = (before - second, first + second, second - first, first - behind)
    else:
        cycle = activated.reshape(4, 4, 16, 128)
        even, odd = cycle[0] + cycle[2], cycle[1] + cycle[3]
        sine = cycle[3] - cycle[1]
        mixed = (even + odd, even - odd, cycle[0] - cycle[2], sine, -sine)
    for index, value in enumerate(mixed):
        v_ref[index, tile] = value.reshape(-1, 128).astype(jnp.bfloat16)


def spread(move, u, v, state_out, v_ref, layer):
    low = low_lanes((16, 16, 128))
    for at, value in (
        (move[2], jnp.where(low, u, pltpu.roll(v, CH, 2))),
        (move[3], jnp.where(low, pltpu.roll(u, CH, 2), v)),
    ):
        state_out[at] = value
        activate_into(v_ref, at, value, layer)


def convolve_pairs(v_ref, w_ref, tiles, layer):
    d = 2**layer
    low = low_lanes((128, 128))
    sums = []
    for index in range(4):
        rows = []
        for tile in tiles:
            after = v_ref[index, neighbour(layer, tile, 1)]
            before = v_ref[index, neighbour(layer, tile, -1)]
            rows.append(jnp.concatenate([v_ref[index, tile], jnp.where(low, after, before)], axis=1))
        rows = jnp.concatenate(rows, axis=0)
        sums.append(z_summed(jnp.dot(rows, w_ref[index], preferred_element_type=jnp.float32), 128, layer))
    first = sums[0] + sums[1] + sums[2]
    second = sums[1] - sums[2] - sums[3]
    results = []
    for at in range(len(tiles)):
        halves = [half[at * 8 : (at + 1) * 8].reshape(8 // d, 1, d, 16, 128) for half in (first, second)]
        results.append(jnp.concatenate(halves, axis=1).reshape(16, 16, 128))
    return results


def convolve_cycles(v_ref, w_ref, units, layer):
    def rows(*forms):
        parts = [jnp.concatenate([v_ref[form, 2 * r + m] for form in forms for m in range(2)], axis=1) for r in units]
        return jnp.concatenate(parts, axis=0)

    def summed(lhs, begin, end):
        return z_summed(jnp.dot(lhs, w_ref[begin:end, :], preferred_element_type=jnp.float32), 256, layer)

    flat = summed(rows(0), 0, 256)
    alternate = summed(rows(1), 256, 512)
    cosine = summed(rows(2, 4), 512, 1024)
    sine = summed(rows(3, 2), 512, 1024)
    even, odd = flat + alternate, flat - alternate
    cells = [value.reshape(len(units), 1, 4, 16, 256) for value in (even + cosine, odd - sine, even - cosine, odd + sine)]
    cells = jnp.concatenate(cells, axis=1).reshape(len(units), 16, 16, 256)
    return [cells[at, :, :, m * 128 : m * 128 + 128] for at in range(len(units)) for m in range(2)]


def begin_section(state, v_refs):
    for move in MOVES[0]:
        spread(move, state[0][move[0]], state[0][move[1]], state[1], v_refs[0], 0)


def run_section(state, v_refs, w_refs, bias_refs, prepare):
    s_a, *held_in = state
    begin_section(state, v_refs)
    prepare(0)
    for layer in range(LAYERS):
        held, following = held_in[layer], held_in[(layer + 1) % LAYERS]
        if layer + 1 < LAYERS:
            prepare(layer + 1)
        bias = bias_refs[layer][0:1][None]
        if layer == LAYERS - 1:
            for tile, total in enumerate(convolve_cycles(v_refs[2], w_refs[layer], range(4), layer)):
                s_a[tile] = (held[tile] + bias + total).astype(jnp.bfloat16).astype(jnp.float32)
            break
        for chosen in GROUPS:
            moves = [MOVES[layer + 1][at] for at in chosen]
            tiles = [tile for move in moves for tile in move[:2]]
            sums = convolve_pairs(v_refs[layer], w_refs[layer], tiles, layer)
            sums = [held[tile] + bias + total for tile, total in zip(tiles, sums)]
            for at, move in enumerate(moves):
                spread(move, sums[2 * at], sums[2 * at + 1], following, v_refs[layer + 1], layer + 1)


def by_parity(x):
    row = lax.broadcasted_iota(jnp.int32, (128, 128), 0)
    lane = lax.broadcasted_iota(jnp.int32, (128, 128), 1)
    place = (row & 112) | ((row & 1) << 3) | ((row >> 1) & 7)
    turned = jnp.where(place == lane, 1.0, 0.0).astype(jnp.bfloat16)
    blocks = jnp.concatenate([x[:, at * 128 : (at + 1) * 128] for at in range(16)], axis=0)
    moved = sum(jnp.dot(term, turned, preferred_element_type=jnp.float32) for term in split_terms(blocks))
    return jnp.concatenate([moved[at * 16 : (at + 1) * 16] for at in range(16)], axis=1)


def lift_into(x, lift_ref, s_a):
    high = x.astype(jnp.bfloat16).astype(jnp.float32)
    columns = jnp.concatenate([high, x - high, high], axis=0).T.astype(jnp.bfloat16)
    hidden = jnp.dot(columns, lift_ref[...], preferred_element_type=jnp.float32)
    s_a[...] = hidden.astype(jnp.bfloat16).astype(jnp.float32).reshape(8, 16, 16, 128)


def renewed_fields(x, proj_ref, s_a):
    gain = nt_dot(proj_ref[...], s_a[...].reshape(2048, 128).astype(jnp.bfloat16))
    return x + gain[:16] + gain[16:32] + gain[32:48]


def level_kernel(level, first, last, *refs):
    (ids_ref, own_0, own_1, far_0, far_1, x_ref, lift_ref, proj_ref) = refs[:8]
    (w_out, c_out, b_out, leaving, x_out, s_a, s_b, s_c, s_d, v_a, v_b, v_c) = refs[-17:-5]
    (packed, w_pair, w_cycle, b_all, sems) = refs[-5:]
    slab, line = ids_ref[0], ids_ref[1]
    x = by_parity(x_ref[...]) if first else x_ref[...]
    if first:
        lift_into(x, lift_ref, s_a)
    else:
        s_a[...] = refs[8][...].astype(jnp.float32)
    state, v_refs = (s_a, s_b, s_c, s_d), (v_a, v_b, v_c)

    def copy(turn, part):
        at = 2 * level + turn
        source = (w_pair.at[turn, 0], w_pair.at[turn, 1], w_cycle.at[turn], b_all.at[turn])[part]
        target = (w_out.at[at, 0], w_out.at[at, 1], c_out.at[at], b_out.at[at])[part]
        return pltpu.make_async_copy(source, target, sems.at[turn, part])

    def section(turn, unused):
        for wanted, sources in ((True, (own_0, own_1)), (False, (far_0, far_1))):
            for core, source in enumerate(sources):

                @pl.when(((turn == line) == wanted) & (slab == core))
                def take(source=source):
                    packed[...] = source[...]

        w_refs = [w_pair.at[turn, 0], w_pair.at[turn, 1], w_cycle.at[turn]]

        def prepare(layer):
            expand(packed.at[layer], w_refs[layer], b_all.at[turn, layer], layer)
            copy(turn, layer).start()

        run_section(state, v_refs, w_refs, [b_all.at[turn, i] for i in range(LAYERS)], prepare)
        copy(turn, LAYERS).start()
        return 0

    lax.fori_loop(0, 2, section, 0)
    leaving[...] = s_a[...].astype(jnp.bfloat16)
    x_out[...] = renewed_fields(x, proj_ref, s_a) if last else x
    for turn in range(2):
        for part in range(LAYERS + 1):
            copy(turn, part).wait()


def feature_kernel(ids_ref, anchor_ref, kept_ref, got_ref, lift_ref, proj_ref, x_ref, lift_out, proj_out):
    slab, slot = ids_ref[0], ids_ref[2]
    kept, got = kept_ref[slot], got_ref[slot]
    halves = (jnp.where(slab == 0, kept, got), jnp.where(slab == 0, got, kept))
    columns = []
    for r in range(4):
        for m in range(2):
            columns.append(jnp.concatenate([halves[m][:, r], halves[m][:, 4 + r]], axis=0))
    current = jnp.concatenate([jnp.concatenate(columns, axis=1), jnp.zeros((10, 2048), jnp.float32)], axis=0)
    row = lax.broadcasted_iota(jnp.int32, (16, 2048), 0)
    column = lax.broadcasted_iota(jnp.int32, (16, 2048), 1)
    along_x = ((column >> 8) & 1) * 8 + (column >> 9) + jnp.where(row >= 9, 4, 0)
    along_x = along_x + anchor_ref[slot, 0]
    along_y = ((column >> 4) & 15) + anchor_ref[slot, 1]
    along_z = (column & 15) + anchor_ref[slot, 2]
    axis = jnp.where(row >= 9, row - 9, row - 6)
    position = jnp.where(axis == 0, along_x, jnp.where(axis == 1, along_y, along_z)) & (FIELD - 1)
    waves = jnp.sin(2.0 * jnp.pi * position.astype(jnp.float32) / FIELD)
    x_ref[...] = jnp.where(row < 6, current, jnp.where(row < 12, waves, 0.0))

    def two_halves(part):
        blank = jnp.zeros(part.shape, jnp.float32)
        return [jnp.concatenate([part, blank], axis=1), jnp.concatenate([blank, part], axis=1)]

    lift = 0.5 * lift_ref[...]
    lift = two_halves(lift[0:3]) + two_halves(lift[3:6]) + [jnp.zeros((4, 128), jnp.float32)]
    first, second, unused = [term.astype(jnp.float32) for term in split_terms(jnp.concatenate(lift, axis=0))]
    lift_out[...] = jnp.concatenate([first, first, second], axis=0).astype(jnp.bfloat16)
    proj = two_halves(2.0 * proj_ref[...]) + [jnp.zeros((10, 128), jnp.float32)]
    proj = [term.astype(jnp.float32) for term in split_terms(jnp.concatenate(proj, axis=0))]
    proj_out[...] = jnp.concatenate(proj, axis=0).astype(jnp.bfloat16)


def cells_in_rows(both, half):
    blocks = []
    for x_ref in both:
        for r in range(4):
            for upper in range(2):
                begin = pl.multiple_of(((2 * r + half) * 2 + upper) * 128, 128)
                blocks.append(x_ref[0:8, pl.ds(begin, 128)])
    row = lax.broadcasted_iota(jnp.int32, (128, 128), 0)
    lane = lax.broadcasted_iota(jnp.int32, (128, 128), 1)
    z = ((lane & 7) << 1) | ((lane >> 3) & 1)
    turned = ((row >> 3) == z) & ((row & 7) == (lane >> 4))
    turned = jnp.where(turned, 1.0, 0.0).astype(jnp.bfloat16)
    return nt_dot(turned, jnp.concatenate(blocks, axis=0).astype(jnp.bfloat16)).astype(jnp.bfloat16)


def second_kernel(ids_ref, x_ref, lift_ref, proj_ref, w_ref, c_ref, b_ref, kept, given, s_a, s_b, s_c, s_d, v_a, v_b, v_c, x_new):
    s = pl.program_id(0)

    state, v_refs = (s_a, s_b, s_c, s_d), (v_a, v_b, v_c)

    @pl.when(s == 0)
    def begin():
        lift_into(x_ref[...], lift_ref, s_a)

    w_refs = [w_ref.at[0, 0], w_ref.at[0, 1], c_ref.at[0]]
    run_section(state, v_refs, w_refs, [b_ref.at[0, i] for i in range(LAYERS)], lambda layer: None)

    @pl.when(s == pl.num_programs(0) - 1)
    def finish():
        x_new[...] = renewed_fields(x_ref[...], proj_ref, s_a)
        kept[...] = cells_in_rows((x_ref, x_new), ids_ref[0])
        given[...] = cells_in_rows((x_ref, x_new), 1 - ids_ref[0])


def place_kernel(share, *refs):
    ids_ref, own, *others, out_ref = refs
    y_cells = out_ref.shape[-1]
    first = ids_ref[3] == 0
    got = others[0][...]
    for other in others[1:]:
        got = got + other[...]
    count = 48 * share
    row = lax.broadcasted_iota(jnp.int32, (count, 128), 0) >> (share.bit_length() - 1)
    lane = lax.broadcasted_iota(jnp.int32, (count, 128), 1)
    step = jnp.where(row >= 24, 1, 0)
    place = step * 64 + (row & 3) * 16 + ((row >> 2) & 1) * 3 + ((row >> 3) - 3 * step)
    chosen = [jnp.where(lane == place + 8 * upper, 1.0, 0.0).astype(jnp.bfloat16) for upper in range(2)]
    own_z = lax.broadcasted_iota(jnp.int32, (count, y_cells), 0) & (share - 1)
    for crop in range(own.shape[0]):
        piece = jnp.where(first, own[crop].astype(jnp.float32), got[crop].astype(jnp.float32)).astype(jnp.bfloat16)
        lower, upper = [nt_dot(one, piece) for one in chosen]
        cells = jnp.zeros((count, y_cells), jnp.float32)
        for z in range(share):
            both = jnp.concatenate([lower[:, 8 * z : 8 * z + 8], upper[:, 8 * z : 8 * z + 8]], axis=1)
            cells = jnp.where(own_z == z, both, cells)
        for step in range(STEPS):
            for comp in range(3):
                for x in range(8):
                    begin = ((3 * step + comp) * 8 + x) * share
                    out_ref[step, crop, comp, x] = cells[begin : begin + share]


def split_terms(matrix):
    first = matrix.astype(jnp.bfloat16)
    rest = matrix - first.astype(jnp.float32)
    second = rest.astype(jnp.bfloat16)
    third = (rest - second.astype(jnp.float32)).astype(jnp.bfloat16)
    return first, second, third


def state_scratch():
    return (
        [pltpu.VMEM((8, 16, 16, 128), jnp.float32)] * 4
        + [pltpu.VMEM((4, 8, 128, 128), jnp.bfloat16)] * 2
        + [pltpu.VMEM((5, 8, 64, 128), jnp.bfloat16)]
    )


def shards(fields, anchors, lift_weight, conv_weight, conv_bias, proj_weight):
    segments = lax.axis_size("segment")
    slabs = lax.axis_size("slab")
    segment_id = lax.axis_index("segment")
    slab_id = lax.axis_index("slab")
    crop_count, comps, slab_rows, y_cells, z_cells = fields.shape
    lines = crop_count // slabs
    levels = segments // lines
    line = segment_id % lines
    slot = line * slabs + slab_id
    swap = [(0, 1), (1, 0)]
    vmem = pl.BlockSpec(memory_space=pltpu.VMEM)
    smem = pl.BlockSpec(memory_space=pltpu.SMEM)
    anyspace = pl.BlockSpec(memory_space=pl.ANY)
    params = pltpu.CompilerParams(vmem_limit_bytes=VMEM_BYTES)
    ids = jnp.stack([slab_id, line, slot, segment_id // lines]).astype(jnp.int32)

    def after(value, earlier):
        return lax.optimization_barrier((value, earlier))[0]

    def between_cores(value):
        return lax.ppermute(value, "slab", swap)

    packed = pl.pallas_call(
        pack_kernel,
        out_shape=jax.ShapeDtypeStruct((LAYERS, ROWS, 128), jnp.bfloat16),
        in_specs=[vmem] * 3,
        out_specs=vmem,
        compiler_params=params,
    )(conv_weight[0], conv_bias.transpose(1, 0, 2), jnp.eye(192, dtype=jnp.bfloat16))

    flat = after(fields, packed).reshape(crop_count, comps, slab_rows, y_cells * z_cells)
    x, lift, proj = pl.pallas_call(
        feature_kernel,
        out_shape=(
            jax.ShapeDtypeStruct((16, 2048), jnp.float32),
            jax.ShapeDtypeStruct((48, 128), jnp.bfloat16),
            jax.ShapeDtypeStruct((48, 128), jnp.bfloat16),
        ),
        in_specs=[smem, smem] + [vmem] * 4,
        out_specs=(vmem, vmem, vmem),
        compiler_params=params,
    )(ids, anchors, flat, between_cores(flat), lift_weight.T, proj_weight)

    w_shape = jax.ShapeDtypeStruct((segments, 2, 4, 256, 384), jnp.bfloat16)
    c_shape = jax.ShapeDtypeStruct((segments, 1024, 768), jnp.bfloat16)
    b_shape = jax.ShapeDtypeStruct((segments, LAYERS, 8, 128), jnp.float32)
    h_shape = jax.ShapeDtypeStruct((8, 16, 16, 128), jnp.bfloat16)
    x_shape = jax.ShapeDtypeStruct((16, 2048), jnp.float32)
    layer_flops = 2 * 4 * 1024 * 256 * 512
    def hand_on(value, level):
        pairs = [(s * slabs, (s - lines) * slabs) for s in range(lines, segments - lines * level)]
        pairs += [(0, slabs + 1), (slabs, 1)]
        return lax.ppermute(value, ("segment", "slab"), pairs)

    arrived = {0: after(hand_on(packed, 0), x)}
    swapped = {0: between_cores(arrived[0])}
    arrived[1] = hand_on(arrived[0], 1)
    kept = ()
    current = x
    for level in range(levels):
        own = (packed, packed) if level == 0 else (arrived[level - 1], swapped[level - 1])
        operands = (ids, *own, swapped[level], arrived[level], current, lift, proj, *kept)
        weights, cycles, rows, hidden, current = pl.pallas_call(
            functools.partial(level_kernel, level, level == 0, level == levels - 1),
            out_shape=(w_shape, c_shape, b_shape, h_shape, x_shape),
            in_specs=[smem] + [vmem] * 7 + ([vmem] + [anyspace] * 3 if kept else []),
            out_specs=(anyspace, anyspace, anyspace, vmem, vmem),
            scratch_shapes=state_scratch()
            + [
                pltpu.VMEM((LAYERS, ROWS, 128), jnp.bfloat16),
                pltpu.VMEM((2, 2, 4, 256, 384), jnp.bfloat16),
                pltpu.VMEM((2, 1024, 768), jnp.bfloat16),
                pltpu.VMEM((2, LAYERS, 8, 128), jnp.float32),
                pltpu.SemaphoreType.DMA((2, LAYERS + 1)),
            ],
            input_output_aliases={9: 0, 10: 1, 11: 2} if kept else {},
            compiler_params=params,
            cost_estimate=pl.CostEstimate(flops=2 * LAYERS * layer_flops, bytes_accessed=4 << 20, transcendentals=0),
        )(*operands)
        kept = (hidden, weights, cycles, rows)
        if level + 1 < levels:
            arrived[level + 1] = after(arrived[level + 1], hidden)
            swapped[level + 1] = between_cores(arrived[level + 1])
            if level + 2 < levels:
                arrived[level + 2] = hand_on(arrived[level + 1], level + 2)
    first_result = current
    kept, given = pl.pallas_call(
        second_kernel,
        grid=(segments,),
        out_shape=(jax.ShapeDtypeStruct((128, 128), jnp.bfloat16),) * 2,
        in_specs=[smem]
        + [vmem] * 3
        + [
            pl.BlockSpec((1, 2, 4, 256, 384), lambda s: (s, 0, 0, 0, 0)),
            pl.BlockSpec((1, 1024, 768), lambda s: (s, 0, 0)),
            pl.BlockSpec((1, LAYERS, 8, 128), lambda s: (s, 0, 0, 0)),
        ],
        out_specs=(vmem, vmem),
        scratch_shapes=state_scratch() + [pltpu.VMEM((16, 2048), jnp.float32)],
        compiler_params=params,
        cost_estimate=pl.CostEstimate(flops=segments * LAYERS * layer_flops, bytes_accessed=16 << 20, transcendentals=0),
    )(ids, first_result, lift, proj, weights, cycles, rows)

    share = z_cells // segments
    got = between_cores(given)
    pair = jnp.where(slab_id == 0, jnp.stack([kept, got]), jnp.stack([got, kept]))
    pair = pair.reshape(slabs, levels, lines, share * 8, 128)
    mine = lax.dynamic_index_in_dim(pair, line, 2, keepdims=False)
    got = lax.ppermute(lax.dynamic_index_in_dim(pair, 1 - line, 2, keepdims=False), "segment", swap)
    crops = jnp.where(line == 0, jnp.concatenate([mine, got]), jnp.concatenate([got, mine]))
    pieces = [crops[:, 0]]
    for level in range(1, levels):
        pairs = [(s, level * lines + s) for s in range(lines)]
        pieces.append(lax.ppermute(crops[:, level], "segment", pairs))
    out = pl.pallas_call(
        functools.partial(place_kernel, share),
        out_shape=jax.ShapeDtypeStruct((STEPS, crop_count, comps, slab_rows, share, y_cells), jnp.float32),
        in_specs=[smem] + [vmem] * levels,
        out_specs=vmem,
        compiler_params=params,
    )(ids, *pieces)
    return out.transpose(0, 1, 2, 3, 5, 4)


def solution(mesh):
    in_specs = (
        P("groups", None, "slab", None, None),
        P("groups", None),
        P(),
        P("segment", None, None, None, None),
        P("segment", None, None),
        P(),
    )
    out_specs = P(None, "groups", None, "slab", None, "segment")
    return jax.shard_map(shards, mesh=mesh, in_specs=in_specs, out_specs=out_specs, check_vma=False)
```

```python
import functools

import jax
import jax.numpy as jnp
from jax import lax
from jax.experimental import pallas as pl
from jax.experimental.pallas import tpu as pltpu
from jax.sharding import PartitionSpec as P

STEPS = 2
FIELD = 4096
LAYERS = 3
CH = 64
ROWS = 896
VMEM_BYTES = 48 * 1024 * 1024

MOVES = (
    [(4 * b + m, 4 * b + 2 + m, 4 * m + b, 4 * m + 2 + b) for b in range(2) for m in range(2)],
    [(2 * m, 2 * m + 1, m, 4 + m) for m in range(4)],
    [(4 * p + 2 * m, 4 * p + 2 * m + 1, 2 * p + m, 2 * (2 + p) + m) for p in range(2) for m in range(2)],
)
CYCLES = (
    [list(range(8))],
    [list(range(4)), list(range(4, 8))],
    [[2 * r, 2 * r + 1] for r in range(4)],
)


GROUPS = ((0,), (1,), (2,), (3,))


def neighbour(layer, tile, step):
    cycle = next(cycle for cycle in CYCLES[layer] if tile in cycle)
    return cycle[(cycle.index(tile) + step) % len(cycle)]


def low_lanes(shape):
    return lax.broadcasted_iota(jnp.int32, shape, len(shape) - 1) < CH


def nt_dot(a, b):
    return lax.dot_general(a, b, (((1,), (1,)), ((), ())), preferred_element_type=jnp.float32)


def pack_kernel(raw_ref, bias_ref, eye_ref, packed):
    eye = eye_ref[...]
    low = low_lanes((CH, 128))
    for layer in range(LAYERS):
        for ty in range(3):
            pair = jnp.concatenate([raw_ref[layer, 3 + ty], raw_ref[layer, ty]], axis=0)
            packed[layer, ty * 192 : (ty + 1) * 192, :] = nt_dot(eye, pair).astype(jnp.bfloat16)
        pair = jnp.concatenate([raw_ref[layer, 6], raw_ref[layer, 7]], axis=0)
        packed[layer, 576:768, :] = nt_dot(eye, pair).astype(jnp.bfloat16)
        pair = jnp.concatenate([raw_ref[layer, 8], raw_ref[layer, 8]], axis=0)
        twice = nt_dot(eye, pair)
        packed[layer, 768:832, :] = jnp.where(low, twice[0:64], twice[64:128]).astype(jnp.bfloat16)
        terms = [term.astype(jnp.float32) for term in split_terms(bias_ref[layer])]
        terms = jnp.concatenate(terms + [jnp.zeros((CH - 3, CH), jnp.float32)], axis=0)
        terms = jnp.concatenate([terms, terms], axis=1)
        packed[layer, 832:896, :] = jnp.where(low, twice[128:192], terms).astype(jnp.bfloat16)


def pair_forms(taps):
    before, here, behind = taps
    ends = 0.25 * (before + behind)
    here = 0.25 * here
    return 0.5 * before, ends + here, ends - here, 0.5 * behind


def cycle_forms(taps):
    before, here, behind = taps
    ends = 0.125 * (before + behind)
    near = 0.125 * here
    return near + ends, near - ends, 0.25 * here, 0.25 * (behind - before)


def expand(packed, w_ref, bias_ref, layer):
    low = low_lanes((192, 128))
    zero = jnp.zeros((192, 128), jnp.float32)
    forms = pair_forms if layer < 2 else cycle_forms
    mids = forms([packed[ty * 192 : (ty + 1) * 192, :].astype(jnp.float32) for ty in range(3)])
    both = packed[576:768, :].astype(jnp.float32)
    ends = packed[768:832, :].astype(jnp.float32)
    rest = packed[832:896, :].astype(jnp.float32)
    ends = jnp.concatenate([ends, pltpu.roll(ends, CH, 1), rest], axis=0)
    lasts = forms([both, pltpu.roll(both, CH, 1), ends])
    for index, (mid, last) in enumerate(zip(mids, lasts)):
        rolled = pltpu.roll(mid, CH, 1)
        blocks = (
            mid,
            jnp.where(low, last, rolled),
            jnp.where(low, zero, pltpu.roll(last, CH, 1)),
            jnp.where(low, rolled, zero),
        )
        blocks = [block.astype(jnp.bfloat16) for block in blocks]
        for tz in range(3):
            for a in range(4):
                if layer < 2:
                    w_ref[index, a * CH : (a + 1) * CH, tz * 128 : (tz + 1) * 128] = blocks[a][tz * CH : (tz + 1) * CH]
                else:
                    row = index * 256 + a * CH
                    for half in range(2):
                        chosen = blocks[((0, 2), (1, 3), (2, 0), (3, 1))[a][half]]
                        column = tz * 256 + half * 128
                        w_ref[row : row + CH, column : column + 128] = chosen[tz * CH : (tz + 1) * CH]
    bias = 0.5 * (rest[0:1] + rest[1:2] + rest[2:3])
    bias = jnp.where(low_lanes((1, 128)), pltpu.roll(bias, CH, 1), bias)
    bias_ref[...] = jnp.broadcast_to(bias, (8, 128))


def z_moved(values, tap, layer):
    even, odd = values[:, :8], values[:, 8:]
    if layer > 0:
        shift = -tap * 2 ** (layer - 1) % 8
        return pltpu.roll(even, shift, 1), pltpu.roll(odd, shift, 1)
    if tap > 0:
        return odd, pltpu.roll(even, 7, 1)
    return pltpu.roll(odd, 1, 1), even


def z_summed(products, width, layer):
    products = products.reshape(products.shape[0] // 16, 16, products.shape[1])
    here = products[:, :, width : 2 * width]
    before = z_moved(products[:, :, :width], -1, layer)
    behind = z_moved(products[:, :, 2 * width :], 1, layer)
    parts = [here[:, 8 * i : 8 * i + 8] + before[i] + behind[i] for i in range(2)]
    return jnp.concatenate(parts, axis=1)


def activate_into(v_ref, tile, value, layer):
    activated = value * jnp.tanh(value) + value
    if layer < 2:
        d = 2**layer
        pairs = activated.reshape(8 // d, 2, d, 16, 128)
        first, second = pairs[:, 0], pairs[:, 1]
        before = jnp.concatenate([second[-1:], second[:-1]], axis=0)
        behind = jnp.concatenate([first[1:], first[:1]], axis=0)
        mixed = (before - second, first + second, second - first, first - behind)
    else:
        cycle = activated.reshape(4, 4, 16, 128)
        even, odd = cycle[0] + cycle[2], cycle[1] + cycle[3]
        sine = cycle[3] - cycle[1]
        mixed = (even + odd, even - odd, cycle[0] - cycle[2], sine, -sine)
    for index, value in enumerate(mixed):
        v_ref[index, tile] = value.reshape(-1, 128).astype(jnp.bfloat16)


def spread(move, u, v, state_out, v_ref, layer):
    low = low_lanes((16, 16, 128))
    for at, value in (
        (move[2], jnp.where(low, u, pltpu.roll(v, CH, 2))),
        (move[3], jnp.where(low, pltpu.roll(u, CH, 2), v)),
    ):
        state_out[at] = value
        activate_into(v_ref, at, value, layer)


def convolve_pairs(v_ref, w_ref, tiles, layer):
    d = 2**layer
    low = low_lanes((128, 128))
    sums = []
    for index in range(4):
        rows = []
        for tile in tiles:
            after = v_ref[index, neighbour(layer, tile, 1)]
            before = v_ref[index, neighbour(layer, tile, -1)]
            rows.append(jnp.concatenate([v_ref[index, tile], jnp.where(low, after, before)], axis=1))
        rows = jnp.concatenate(rows, axis=0)
        sums.append(z_summed(jnp.dot(rows, w_ref[index], preferred_element_type=jnp.float32), 128, layer))
    first = sums[0] + sums[1] + sums[2]
    second = sums[1] - sums[2] - sums[3]
    results = []
    for at in range(len(tiles)):
        halves = [half[at * 8 : (at + 1) * 8].reshape(8 // d, 1, d, 16, 128) for half in (first, second)]
        results.append(jnp.concatenate(halves, axis=1).reshape(16, 16, 128))
    return results


def convolve_cycles(v_ref, w_ref, units, layer):
    def rows(*forms):
        parts = [jnp.concatenate([v_ref[form, 2 * r + m] for form in forms for m in range(2)], axis=1) for r in units]
        return jnp.concatenate(parts, axis=0)

    def summed(lhs, begin, end):
        return z_summed(jnp.dot(lhs, w_ref[begin:end, :], preferred_element_type=jnp.float32), 256, layer)

    flat = summed(rows(0), 0, 256)
    alternate = summed(rows(1), 256, 512)
    cosine = summed(rows(2, 4), 512, 1024)
    sine = summed(rows(3, 2), 512, 1024)
    even, odd = flat + alternate, flat - alternate
    cells = [value.reshape(len(units), 1, 4, 16, 256) for value in (even + cosine, odd - sine, even - cosine, odd + sine)]
    cells = jnp.concatenate(cells, axis=1).reshape(len(units), 16, 16, 256)
    return [cells[at, :, :, m * 128 : m * 128 + 128] for at in range(len(units)) for m in range(2)]


def begin_section(state, v_refs):
    for move in MOVES[0]:
        spread(move, state[0][move[0]], state[0][move[1]], state[1], v_refs[0], 0)


def run_section(state, v_refs, w_refs, bias_refs, prepare):
    s_a, *held_in = state
    begin_section(state, v_refs)
    prepare(0)
    for layer in range(LAYERS):
        held, following = held_in[layer], held_in[(layer + 1) % LAYERS]
        if layer + 1 < LAYERS:
            prepare(layer + 1)
        bias = bias_refs[layer][0:1][None]
        if layer == LAYERS - 1:
            for tile, total in enumerate(convolve_cycles(v_refs[2], w_refs[layer], range(4), layer)):
                s_a[tile] = (held[tile] + bias + total).astype(jnp.bfloat16).astype(jnp.float32)
            break
        for chosen in GROUPS:
            moves = [MOVES[layer + 1][at] for at in chosen]
            tiles = [tile for move in moves for tile in move[:2]]
            sums = [convolve_pairs(v_refs[layer], w_refs[layer], [tile], layer)[0] for tile in tiles]
            sums = [held[tile] + bias + total for tile, total in zip(tiles, sums)]
            for at, move in enumerate(moves):
                spread(move, sums[2 * at], sums[2 * at + 1], following, v_refs[layer + 1], layer + 1)


def by_parity(x):
    row = lax.broadcasted_iota(jnp.int32, (128, 128), 0)
    lane = lax.broadcasted_iota(jnp.int32, (128, 128), 1)
    place = (row & 112) | ((row & 1) << 3) | ((row >> 1) & 7)
    turned = jnp.where(place == lane, 1.0, 0.0).astype(jnp.bfloat16)
    blocks = jnp.concatenate([x[:, at * 128 : (at + 1) * 128] for at in range(16)], axis=0)
    moved = sum(jnp.dot(term, turned, preferred_element_type=jnp.float32) for term in split_terms(blocks))
    return jnp.concatenate([moved[at * 16 : (at + 1) * 16] for at in range(16)], axis=1)


def lift_into(x, lift_ref, s_a):
    high = x.astype(jnp.bfloat16).astype(jnp.float32)
    columns = jnp.concatenate([high, x - high, high], axis=0).T.astype(jnp.bfloat16)
    hidden = jnp.dot(columns, lift_ref[...], preferred_element_type=jnp.float32)
    s_a[...] = hidden.astype(jnp.bfloat16).astype(jnp.float32).reshape(8, 16, 16, 128)


def renewed_fields(x, proj_ref, s_a):
    gain = nt_dot(proj_ref[...], s_a[...].reshape(2048, 128).astype(jnp.bfloat16))
    return x + gain[:16] + gain[16:32] + gain[32:48]


def level_kernel(level, first, last, *refs):
    (ids_ref, own_0, own_1, far_0, far_1, x_ref, lift_ref, proj_ref) = refs[:8]
    (w_out, c_out, b_out, leaving, x_out, s_a, s_b, s_c, s_d, v_a, v_b, v_c) = refs[-17:-5]
    (packed, w_pair, w_cycle, b_all, sems) = refs[-5:]
    slab, line = ids_ref[0], ids_ref[1]
    x = by_parity(x_ref[...]) if first else x_ref[...]
    if first:
        lift_into(x, lift_ref, s_a)
    else:
        s_a[...] = refs[8][...].astype(jnp.float32)
    state, v_refs = (s_a, s_b, s_c, s_d), (v_a, v_b, v_c)

    def copy(turn, part):
        at = 2 * level + turn
        source = (w_pair.at[turn, 0], w_pair.at[turn, 1], w_cycle.at[turn], b_all.at[turn])[part]
        target = (w_out.at[at, 0], w_out.at[at, 1], c_out.at[at], b_out.at[at])[part]
        return pltpu.make_async_copy(source, target, sems.at[turn, part])

    def section(turn, unused):
        for wanted, sources in ((True, (own_0, own_1)), (False, (far_0, far_1))):
            for core, source in enumerate(sources):

                @pl.when(((turn == line) == wanted) & (slab == core))
                def take(source=source):
                    packed[...] = source[...]

        w_refs = [w_pair.at[turn, 0], w_pair.at[turn, 1], w_cycle.at[turn]]

        def prepare(layer):
            expand(packed.at[layer], w_refs[layer], b_all.at[turn, layer], layer)
            copy(turn, layer).start()

        run_section(state, v_refs, w_refs, [b_all.at[turn, i] for i in range(LAYERS)], prepare)
        copy(turn, LAYERS).start()
        return 0

    lax.fori_loop(0, 2, section, 0)
    leaving[...] = s_a[...].astype(jnp.bfloat16)
    x_out[...] = renewed_fields(x, proj_ref, s_a) if last else x
    for turn in range(2):
        for part in range(LAYERS + 1):
            copy(turn, part).wait()


def feature_kernel(ids_ref, anchor_ref, kept_ref, got_ref, lift_ref, proj_ref, x_ref, lift_out, proj_out):
    slab, slot = ids_ref[0], ids_ref[2]
    kept, got = kept_ref[slot], got_ref[slot]
    halves = (jnp.where(slab == 0, kept, got), jnp.where(slab == 0, got, kept))
    columns = []
    for r in range(4):
        for m in range(2):
            columns.append(jnp.concatenate([halves[m][:, r], halves[m][:, 4 + r]], axis=0))
    current = jnp.concatenate([jnp.concatenate(columns, axis=1), jnp.zeros((10, 2048), jnp.float32)], axis=0)
    row = lax.broadcasted_iota(jnp.int32, (16, 2048), 0)
    column = lax.broadcasted_iota(jnp.int32, (16, 2048), 1)
    along_x = ((column >> 8) & 1) * 8 + (column >> 9) + jnp.where(row >= 9, 4, 0)
    along_x = along_x + anchor_ref[slot, 0]
    along_y = ((column >> 4) & 15) + anchor_ref[slot, 1]
    along_z = (column & 15) + anchor_ref[slot, 2]
    axis = jnp.where(row >= 9, row - 9, row - 6)
    position = jnp.where(axis == 0, along_x, jnp.where(axis == 1, along_y, along_z)) & (FIELD - 1)
    waves = jnp.sin(2.0 * jnp.pi * position.astype(jnp.float32) / FIELD)
    x_ref[...] = jnp.where(row < 6, current, jnp.where(row < 12, waves, 0.0))

    def two_halves(part):
        blank = jnp.zeros(part.shape, jnp.float32)
        return [jnp.concatenate([part, blank], axis=1), jnp.concatenate([blank, part], axis=1)]

    lift = 0.5 * lift_ref[...]
    lift = two_halves(lift[0:3]) + two_halves(lift[3:6]) + [jnp.zeros((4, 128), jnp.float32)]
    first, second, unused = [term.astype(jnp.float32) for term in split_terms(jnp.concatenate(lift, axis=0))]
    lift_out[...] = jnp.concatenate([first, first, second], axis=0).astype(jnp.bfloat16)
    proj = two_halves(2.0 * proj_ref[...]) + [jnp.zeros((10, 128), jnp.float32)]
    proj = [term.astype(jnp.float32) for term in split_terms(jnp.concatenate(proj, axis=0))]
    proj_out[...] = jnp.concatenate(proj, axis=0).astype(jnp.bfloat16)


def cells_in_rows(both, half):
    blocks = []
    for x_ref in both:
        for r in range(4):
            for upper in range(2):
                begin = pl.multiple_of(((2 * r + half) * 2 + upper) * 128, 128)
                blocks.append(x_ref[0:8, pl.ds(begin, 128)])
    row = lax.broadcasted_iota(jnp.int32, (128, 128), 0)
    lane = lax.broadcasted_iota(jnp.int32, (128, 128), 1)
    z = ((lane & 7) << 1) | ((lane >> 3) & 1)
    turned = ((row >> 3) == z) & ((row & 7) == (lane >> 4))
    turned = jnp.where(turned, 1.0, 0.0).astype(jnp.bfloat16)
    return nt_dot(turned, jnp.concatenate(blocks, axis=0).astype(jnp.bfloat16)).astype(jnp.bfloat16)


def second_kernel(ids_ref, x_ref, lift_ref, proj_ref, w_ref, c_ref, b_ref, kept, given, s_a, s_b, s_c, s_d, v_a, v_b, v_c, x_new):
    s = pl.program_id(0)

    state, v_refs = (s_a, s_b, s_c, s_d), (v_a, v_b, v_c)

    @pl.when(s == 0)
    def begin():
        lift_into(x_ref[...], lift_ref, s_a)

    w_refs = [w_ref.at[0, 0], w_ref.at[0, 1], c_ref.at[0]]
    run_section(state, v_refs, w_refs, [b_ref.at[0, i] for i in range(LAYERS)], lambda layer: None)

    @pl.when(s == pl.num_programs(0) - 1)
    def finish():
        x_new[...] = renewed_fields(x_ref[...], proj_ref, s_a)
        kept[...] = cells_in_rows((x_ref, x_new), ids_ref[0])
        given[...] = cells_in_rows((x_ref, x_new), 1 - ids_ref[0])


def place_kernel(share, pieces, out_ref):
    y_cells = out_ref.shape[-1]
    count = 48 * share
    row = lax.broadcasted_iota(jnp.int32, (count, 128), 0) >> (share.bit_length() - 1)
    lane = lax.broadcasted_iota(jnp.int32, (count, 128), 1)
    step = jnp.where(row >= 24, 1, 0)
    place = step * 64 + (row & 3) * 16 + ((row >> 2) & 1) * 3 + ((row >> 3) - 3 * step)
    chosen = [jnp.where(lane == place + 8 * upper, 1.0, 0.0).astype(jnp.bfloat16) for upper in range(2)]
    own_z = lax.broadcasted_iota(jnp.int32, (count, y_cells), 0) & (share - 1)
    for crop in range(pieces.shape[0]):
        lower, upper = [nt_dot(one, pieces[crop]) for one in chosen]
        cells = jnp.zeros((count, y_cells), jnp.float32)
        for z in range(share):
            both = jnp.concatenate([lower[:, 8 * z : 8 * z + 8], upper[:, 8 * z : 8 * z + 8]], axis=1)
            cells = jnp.where(own_z == z, both, cells)
        for step in range(STEPS):
            for comp in range(3):
                for x in range(8):
                    begin = ((3 * step + comp) * 8 + x) * share
                    out_ref[step, crop, comp, x] = cells[begin : begin + share]


def split_terms(matrix):
    first = matrix.astype(jnp.bfloat16)
    rest = matrix - first.astype(jnp.float32)
    second = rest.astype(jnp.bfloat16)
    third = (rest - second.astype(jnp.float32)).astype(jnp.bfloat16)
    return first, second, third


def state_scratch():
    return (
        [pltpu.VMEM((8, 16, 16, 128), jnp.float32)] * 4
        + [pltpu.VMEM((4, 8, 128, 128), jnp.bfloat16)] * 2
        + [pltpu.VMEM((5, 8, 64, 128), jnp.bfloat16)]
    )


def shards(fields, anchors, lift_weight, conv_weight, conv_bias, proj_weight):
    segments = lax.axis_size("segment")
    slabs = lax.axis_size("slab")
    segment_id = lax.axis_index("segment")
    slab_id = lax.axis_index("slab")
    crop_count, comps, slab_rows, y_cells, z_cells = fields.shape
    lines = crop_count // slabs
    levels = segments // lines
    line = segment_id % lines
    slot = line * slabs + slab_id
    swap = [(0, 1), (1, 0)]
    vmem = pl.BlockSpec(memory_space=pltpu.VMEM)
    smem = pl.BlockSpec(memory_space=pltpu.SMEM)
    anyspace = pl.BlockSpec(memory_space=pl.ANY)
    params = pltpu.CompilerParams(vmem_limit_bytes=VMEM_BYTES)
    ids = jnp.stack([slab_id, line, slot, segment_id // lines]).astype(jnp.int32)

    def after(value, earlier):
        return lax.optimization_barrier((value, earlier))[0]

    def between_cores(value):
        return lax.ppermute(value, "slab", swap)

    packed = pl.pallas_call(
        pack_kernel,
        out_shape=jax.ShapeDtypeStruct((LAYERS, ROWS, 128), jnp.bfloat16),
        in_specs=[vmem] * 3,
        out_specs=vmem,
        compiler_params=params,
    )(conv_weight[0], conv_bias.transpose(1, 0, 2), jnp.eye(192, dtype=jnp.bfloat16))

    flat = after(fields, packed).reshape(crop_count, comps, slab_rows, y_cells * z_cells)
    x, lift, proj = pl.pallas_call(
        feature_kernel,
        out_shape=(
            jax.ShapeDtypeStruct((16, 2048), jnp.float32),
            jax.ShapeDtypeStruct((48, 128), jnp.bfloat16),
            jax.ShapeDtypeStruct((48, 128), jnp.bfloat16),
        ),
        in_specs=[smem, smem] + [vmem] * 4,
        out_specs=(vmem, vmem, vmem),
        compiler_params=params,
    )(ids, anchors, flat, between_cores(flat), lift_weight.T, proj_weight)

    w_shape = jax.ShapeDtypeStruct((segments, 2, 4, 256, 384), jnp.bfloat16)
    c_shape = jax.ShapeDtypeStruct((segments, 1024, 768), jnp.bfloat16)
    b_shape = jax.ShapeDtypeStruct((segments, LAYERS, 8, 128), jnp.float32)
    h_shape = jax.ShapeDtypeStruct((8, 16, 16, 128), jnp.bfloat16)
    x_shape = jax.ShapeDtypeStruct((16, 2048), jnp.float32)
    layer_flops = 2 * 4 * 1024 * 256 * 512
    def hand_on(value, level):
        pairs = [(s * slabs, (s - lines) * slabs) for s in range(lines, segments - lines * level)]
        pairs += [(0, slabs + 1), (slabs, 1)]
        return lax.ppermute(value, ("segment", "slab"), pairs)

    arrived = {0: after(hand_on(packed, 0), x)}
    swapped = {0: between_cores(arrived[0])}
    arrived[1] = hand_on(arrived[0], 1)
    kept = ()
    current = x
    for level in range(levels):
        own = (packed, packed) if level == 0 else (arrived[level - 1], swapped[level - 1])
        operands = (ids, *own, swapped[level], arrived[level], current, lift, proj, *kept)
        weights, cycles, rows, hidden, current = pl.pallas_call(
            functools.partial(level_kernel, level, level == 0, level == levels - 1),
            out_shape=(w_shape, c_shape, b_shape, h_shape, x_shape),
            in_specs=[smem] + [vmem] * 7 + ([vmem] + [anyspace] * 3 if kept else []),
            out_specs=(anyspace, anyspace, anyspace, vmem, vmem),
            scratch_shapes=state_scratch()
            + [
                pltpu.VMEM((LAYERS, ROWS, 128), jnp.bfloat16),
                pltpu.VMEM((2, 2, 4, 256, 384), jnp.bfloat16),
                pltpu.VMEM((2, 1024, 768), jnp.bfloat16),
                pltpu.VMEM((2, LAYERS, 8, 128), jnp.float32),
                pltpu.SemaphoreType.DMA((2, LAYERS + 1)),
            ],
            input_output_aliases={9: 0, 10: 1, 11: 2} if kept else {},
            compiler_params=params,
            cost_estimate=pl.CostEstimate(flops=2 * LAYERS * layer_flops, bytes_accessed=4 << 20, transcendentals=0),
        )(*operands)
        kept = (hidden, weights, cycles, rows)
        if level + 1 < levels:
            arrived[level + 1] = after(arrived[level + 1], hidden)
            swapped[level + 1] = between_cores(arrived[level + 1])
            if level + 2 < levels:
                arrived[level + 2] = hand_on(arrived[level + 1], level + 2)
    first_result = current
    kept, given = pl.pallas_call(
        second_kernel,
        grid=(segments,),
        out_shape=(jax.ShapeDtypeStruct((128, 128), jnp.bfloat16),) * 2,
        in_specs=[smem]
        + [vmem] * 3
        + [
            pl.BlockSpec((1, 2, 4, 256, 384), lambda s: (s, 0, 0, 0, 0)),
            pl.BlockSpec((1, 1024, 768), lambda s: (s, 0, 0)),
            pl.BlockSpec((1, LAYERS, 8, 128), lambda s: (s, 0, 0, 0)),
        ],
        out_specs=(vmem, vmem),
        scratch_shapes=state_scratch() + [pltpu.VMEM((16, 2048), jnp.float32)],
        compiler_params=params,
        cost_estimate=pl.CostEstimate(flops=segments * LAYERS * layer_flops, bytes_accessed=16 << 20, transcendentals=0),
    )(ids, first_result, lift, proj, weights, cycles, rows)

    share = z_cells // segments
    got = between_cores(given)
    pair = jnp.where(slab_id == 0, jnp.stack([kept, got]), jnp.stack([got, kept]))
    pieces = pair.reshape(slabs, segments, share * 8, 128).transpose(1, 0, 2, 3)
    pieces = lax.all_to_all(pieces, "segment", 0, 0, tiled=True)
    pieces = pieces[:lines].reshape(crop_count, share * 8, 128)
    out = pl.pallas_call(
        functools.partial(place_kernel, share),
        out_shape=jax.ShapeDtypeStruct((STEPS, crop_count, comps, slab_rows, share, y_cells), jnp.float32),
        in_specs=[vmem],
        out_specs=vmem,
        compiler_params=params,
    )(pieces)
    return out.transpose(0, 1, 2, 3, 5, 4)


def solution(mesh):
    in_specs = (
        P("groups", None, "slab", None, None),
        P("groups", None),
        P(),
        P("segment", None, None, None, None),
        P("segment", None, None),
        P(),
    )
    out_specs = P(None, "groups", None, "slab", None, "segment")
    return jax.shard_map(shards, mesh=mesh, in_specs=in_specs, out_specs=out_specs, check_vma=False)
```

```python
import functools

import jax
import jax.numpy as jnp
from jax import lax
from jax.experimental import pallas as pl
from jax.experimental.pallas import tpu as pltpu
from jax.sharding import PartitionSpec as P

STEPS = 2
FIELD = 4096
LAYERS = 3
CH = 64
ROWS = 896
VMEM_BYTES = 48 * 1024 * 1024

MOVES = (
    [(4 * b + m, 4 * b + 2 + m, 4 * m + b, 4 * m + 2 + b) for b in range(2) for m in range(2)],
    [(2 * m, 2 * m + 1, m, 4 + m) for m in range(4)],
    [(4 * p + 2 * m, 4 * p + 2 * m + 1, 2 * p + m, 2 * (2 + p) + m) for p in range(2) for m in range(2)],
)
CYCLES = (
    [list(range(8))],
    [list(range(4)), list(range(4, 8))],
    [[2 * r, 2 * r + 1] for r in range(4)],
)


GROUPS = ((0,), (1,), (2,), (3,))


def neighbour(layer, tile, step):
    cycle = next(cycle for cycle in CYCLES[layer] if tile in cycle)
    return cycle[(cycle.index(tile) + step) % len(cycle)]


def low_lanes(shape):
    return lax.broadcasted_iota(jnp.int32, shape, len(shape) - 1) < CH


def nt_dot(a, b):
    return lax.dot_general(a, b, (((1,), (1,)), ((), ())), preferred_element_type=jnp.float32)


def pack_kernel(raw_ref, bias_ref, eye_ref, packed):
    eye = eye_ref[...]
    low = low_lanes((CH, 128))
    for layer in range(LAYERS):
        for ty in range(3):
            pair = jnp.concatenate([raw_ref[layer, 3 + ty], raw_ref[layer, ty]], axis=0)
            packed[layer, ty * 192 : (ty + 1) * 192, :] = nt_dot(eye, pair).astype(jnp.bfloat16)
        pair = jnp.concatenate([raw_ref[layer, 6], raw_ref[layer, 7]], axis=0)
        packed[layer, 576:768, :] = nt_dot(eye, pair).astype(jnp.bfloat16)
        pair = jnp.concatenate([raw_ref[layer, 8], raw_ref[layer, 8]], axis=0)
        twice = nt_dot(eye, pair)
        packed[layer, 768:832, :] = jnp.where(low, twice[0:64], twice[64:128]).astype(jnp.bfloat16)
        terms = [term.astype(jnp.float32) for term in split_terms(bias_ref[layer])]
        terms = jnp.concatenate(terms + [jnp.zeros((CH - 3, CH), jnp.float32)], axis=0)
        terms = jnp.concatenate([terms, terms], axis=1)
        packed[layer, 832:896, :] = jnp.where(low, twice[128:192], terms).astype(jnp.bfloat16)


def pair_forms(taps):
    before, here, behind = taps
    ends = 0.25 * (before + behind)
    here = 0.25 * here
    return 0.5 * before, ends + here, ends - here, 0.5 * behind


def cycle_forms(taps):
    before, here, behind = taps
    ends = 0.125 * (before + behind)
    near = 0.125 * here
    return near + ends, near - ends, 0.25 * here, 0.25 * (behind - before)


def expand(packed, w_ref, bias_ref, layer):
    low = low_lanes((192, 128))
    zero = jnp.zeros((192, 128), jnp.float32)
    forms = pair_forms if layer < 2 else cycle_forms
    mids = forms([packed[ty * 192 : (ty + 1) * 192, :].astype(jnp.float32) for ty in range(3)])
    both = packed[576:768, :].astype(jnp.float32)
    ends = packed[768:832, :].astype(jnp.float32)
    rest = packed[832:896, :].astype(jnp.float32)
    ends = jnp.concatenate([ends, pltpu.roll(ends, CH, 1), rest], axis=0)
    lasts = forms([both, pltpu.roll(both, CH, 1), ends])
    for index, (mid, last) in enumerate(zip(mids, lasts)):
        rolled = pltpu.roll(mid, CH, 1)
        blocks = (
            mid,
            jnp.where(low, last, rolled),
            jnp.where(low, zero, pltpu.roll(last, CH, 1)),
            jnp.where(low, rolled, zero),
        )
        blocks = [block.astype(jnp.bfloat16) for block in blocks]
        for tz in range(3):
            for a in range(4):
                if layer < 2:
                    w_ref[index, a * CH : (a + 1) * CH, tz * 128 : (tz + 1) * 128] = blocks[a][tz * CH : (tz + 1) * CH]
                else:
                    row = index * 256 + a * CH
                    for half in range(2):
                        chosen = blocks[((0, 2), (1, 3), (2, 0), (3, 1))[a][half]]
                        column = tz * 256 + half * 128
                        w_ref[row : row + CH, column : column + 128] = chosen[tz * CH : (tz + 1) * CH]
    bias = 0.5 * (rest[0:1] + rest[1:2] + rest[2:3])
    bias = jnp.where(low_lanes((1, 128)), pltpu.roll(bias, CH, 1), bias)
    bias_ref[...] = jnp.broadcast_to(bias, (8, 128))


def z_moved(values, tap, layer):
    even, odd = values[:, :8], values[:, 8:]
    if layer > 0:
        shift = -tap * 2 ** (layer - 1) % 8
        return pltpu.roll(even, shift, 1), pltpu.roll(odd, shift, 1)
    if tap > 0:
        return odd, pltpu.roll(even, 7, 1)
    return pltpu.roll(odd, 1, 1), even


def z_summed(products, width, layer):
    products = products.reshape(products.shape[0] // 16, 16, products.shape[1])
    here = products[:, :, width : 2 * width]
    before = z_moved(products[:, :, :width], -1, layer)
    behind = z_moved(products[:, :, 2 * width :], 1, layer)
    parts = [here[:, 8 * i : 8 * i + 8] + before[i] + behind[i] for i in range(2)]
    return jnp.concatenate(parts, axis=1)


def activate_into(v_ref, tile, value, layer):
    activated = value * jnp.tanh(value) + value
    if layer < 2:
        d = 2**layer
        pairs = activated.reshape(8 // d, 2, d, 16, 128)
        first, second = pairs[:, 0], pairs[:, 1]
        before = jnp.concatenate([second[-1:], second[:-1]], axis=0)
        behind = jnp.concatenate([first[1:], first[:1]], axis=0)
        mixed = (before - second, first + second, second - first, first - behind)
    else:
        cycle = activated.reshape(4, 4, 16, 128)
        even, odd = cycle[0] + cycle[2], cycle[1] + cycle[3]
        sine = cycle[3] - cycle[1]
        mixed = (even + odd, even - odd, cycle[0] - cycle[2], sine, -sine)
    for index, value in enumerate(mixed):
        v_ref[index, tile] = value.reshape(-1, 128).astype(jnp.bfloat16)


def spread(move, u, v, state_out, v_ref, layer):
    low = low_lanes((16, 16, 128))
    for at, value in (
        (move[2], jnp.where(low, u, pltpu.roll(v, CH, 2))),
        (move[3], jnp.where(low, pltpu.roll(u, CH, 2), v)),
    ):
        state_out[at] = value
        activate_into(v_ref, at, value, layer)


def convolve_pairs(v_ref, w_ref, tiles, layer):
    d = 2**layer
    low = low_lanes((128, 128))
    sums = []
    for index in range(4):
        rows = []
        for tile in tiles:
            after = v_ref[index, neighbour(layer, tile, 1)]
            before = v_ref[index, neighbour(layer, tile, -1)]
            rows.append(jnp.concatenate([v_ref[index, tile], jnp.where(low, after, before)], axis=1))
        rows = jnp.concatenate(rows, axis=0)
        sums.append(z_summed(jnp.dot(rows, w_ref[index], preferred_element_type=jnp.float32), 128, layer))
    first = sums[0] + sums[1] + sums[2]
    second = sums[1] - sums[2] - sums[3]
    results = []
    for at in range(len(tiles)):
        halves = [half[at * 8 : (at + 1) * 8].reshape(8 // d, 1, d, 16, 128) for half in (first, second)]
        results.append(jnp.concatenate(halves, axis=1).reshape(16, 16, 128))
    return results


def convolve_cycles(v_ref, w_ref, units, layer):
    def rows(*forms):
        parts = [jnp.concatenate([v_ref[form, 2 * r + m] for form in forms for m in range(2)], axis=1) for r in units]
        return jnp.concatenate(parts, axis=0)

    def summed(lhs, begin, end):
        return z_summed(jnp.dot(lhs, w_ref[begin:end, :], preferred_element_type=jnp.float32), 256, layer)

    flat = summed(rows(0), 0, 256)
    alternate = summed(rows(1), 256, 512)
    cosine = summed(rows(2, 4), 512, 1024)
    sine = summed(rows(3, 2), 512, 1024)
    even, odd = flat + alternate, flat - alternate
    cells = [value.reshape(len(units), 1, 4, 16, 256) for value in (even + cosine, odd - sine, even - cosine, odd + sine)]
    cells = jnp.concatenate(cells, axis=1).reshape(len(units), 16, 16, 256)
    return [cells[at, :, :, m * 128 : m * 128 + 128] for at in range(len(units)) for m in range(2)]


def begin_section(state, v_refs):
    for move in MOVES[0]:
        spread(move, state[0][move[0]], state[0][move[1]], state[1], v_refs[0], 0)


def run_section(state, v_refs, w_refs, bias_refs, prepare):
    s_a, *held_in = state
    begin_section(state, v_refs)
    prepare(0)
    for layer in range(LAYERS):
        held, following = held_in[layer], held_in[(layer + 1) % LAYERS]
        if layer + 1 < LAYERS:
            prepare(layer + 1)
        bias = bias_refs[layer][0:1][None]
        if layer == LAYERS - 1:
            for tile, total in enumerate(convolve_cycles(v_refs[2], w_refs[layer], range(4), layer)):
                s_a[tile] = (held[tile] + bias + total).astype(jnp.bfloat16).astype(jnp.float32)
            break
        for chosen in GROUPS:
            moves = [MOVES[layer + 1][at] for at in chosen]
            tiles = [tile for move in moves for tile in move[:2]]
            sums = convolve_pairs(v_refs[layer], w_refs[layer], tiles, layer)
            sums = [held[tile] + bias + total for tile, total in zip(tiles, sums)]
            for at, move in enumerate(moves):
                spread(move, sums[2 * at], sums[2 * at + 1], following, v_refs[layer + 1], layer + 1)


def by_parity(x):
    row = lax.broadcasted_iota(jnp.int32, (128, 128), 0)
    lane = lax.broadcasted_iota(jnp.int32, (128, 128), 1)
    place = (row & 112) | ((row & 1) << 3) | ((row >> 1) & 7)
    turned = jnp.where(place == lane, 1.0, 0.0).astype(jnp.bfloat16)
    blocks = jnp.concatenate([x[:, at * 128 : (at + 1) * 128] for at in range(16)], axis=0)
    moved = sum(jnp.dot(term, turned, preferred_element_type=jnp.float32) for term in split_terms(blocks))
    return jnp.concatenate([moved[at * 16 : (at + 1) * 16] for at in range(16)], axis=1)


def lifted(x, lift):
    high = x.astype(jnp.bfloat16).astype(jnp.float32)
    columns = jnp.concatenate([high, x - high, high], axis=0).T.astype(jnp.bfloat16)
    hidden = jnp.dot(columns, lift, preferred_element_type=jnp.float32)
    return hidden.astype(jnp.bfloat16).reshape(8, 16, 16, 128)


def renewed_fields(x, proj_ref, s_a):
    gain = nt_dot(proj_ref[...], s_a[...].reshape(2048, 128).astype(jnp.bfloat16))
    return x + gain[:16] + gain[16:32] + gain[32:48]


def level_kernel(level, last, *refs):
    (ids_ref, own_0, own_1, far_0, far_1, x_ref, lift_ref, proj_ref) = refs[:8]
    (w_out, c_out, b_out, leaving, x_out, s_a, s_b, s_c, s_d, v_a, v_b, v_c) = refs[-17:-5]
    (packed, w_pair, w_cycle, b_all, sems) = refs[-5:]
    slab, line = ids_ref[0], ids_ref[1]
    x = x_ref[...]
    s_a[...] = refs[8][...].astype(jnp.float32)
    state, v_refs = (s_a, s_b, s_c, s_d), (v_a, v_b, v_c)

    def copy(turn, part):
        at = 2 * level + turn
        source = (w_pair.at[turn, 0], w_pair.at[turn, 1], w_cycle.at[turn], b_all.at[turn])[part]
        target = (w_out.at[at, 0], w_out.at[at, 1], c_out.at[at], b_out.at[at])[part]
        return pltpu.make_async_copy(source, target, sems.at[turn, part])

    def section(turn, unused):
        for wanted, sources in ((True, (own_0, own_1)), (False, (far_0, far_1))):
            for core, source in enumerate(sources):

                @pl.when(((turn == line) == wanted) & (slab == core))
                def take(source=source):
                    packed[...] = source[...]

        w_refs = [w_pair.at[turn, 0], w_pair.at[turn, 1], w_cycle.at[turn]]

        def prepare(layer):
            expand(packed.at[layer], w_refs[layer], b_all.at[turn, layer], layer)
            copy(turn, layer).start()

        run_section(state, v_refs, w_refs, [b_all.at[turn, i] for i in range(LAYERS)], prepare)
        copy(turn, LAYERS).start()
        return 0

    lax.fori_loop(0, 2, section, 0)
    leaving[...] = s_a[...].astype(jnp.bfloat16)
    x_out[...] = renewed_fields(x, proj_ref, s_a) if last else x
    for turn in range(2):
        for part in range(LAYERS + 1):
            copy(turn, part).wait()


def feature_kernel(ids_ref, anchor_ref, kept_ref, got_ref, lift_ref, proj_ref, x_ref, lift_out, proj_out, hidden_out):
    slab, slot = ids_ref[0], ids_ref[2]
    kept, got = kept_ref[slot], got_ref[slot]
    halves = (jnp.where(slab == 0, kept, got), jnp.where(slab == 0, got, kept))
    columns = []
    for r in range(4):
        for m in range(2):
            columns.append(jnp.concatenate([halves[m][:, r], halves[m][:, 4 + r]], axis=0))
    current = jnp.concatenate([jnp.concatenate(columns, axis=1), jnp.zeros((10, 2048), jnp.float32)], axis=0)
    row = lax.broadcasted_iota(jnp.int32, (16, 2048), 0)
    column = lax.broadcasted_iota(jnp.int32, (16, 2048), 1)
    along_x = ((column >> 8) & 1) * 8 + (column >> 9) + jnp.where(row >= 9, 4, 0)
    along_x = along_x + anchor_ref[slot, 0]
    along_y = ((column >> 4) & 15) + anchor_ref[slot, 1]
    along_z = (column & 15) + anchor_ref[slot, 2]
    axis = jnp.where(row >= 9, row - 9, row - 6)
    position = jnp.where(axis == 0, along_x, jnp.where(axis == 1, along_y, along_z)) & (FIELD - 1)
    waves = jnp.sin(2.0 * jnp.pi * position.astype(jnp.float32) / FIELD)
    x = by_parity(jnp.where(row < 6, current, jnp.where(row < 12, waves, 0.0)))
    x_ref[...] = x

    def two_halves(part):
        blank = jnp.zeros(part.shape, jnp.float32)
        return [jnp.concatenate([part, blank], axis=1), jnp.concatenate([blank, part], axis=1)]

    lift = 0.5 * lift_ref[...]
    lift = two_halves(lift[0:3]) + two_halves(lift[3:6]) + [jnp.zeros((4, 128), jnp.float32)]
    first, second, unused = [term.astype(jnp.float32) for term in split_terms(jnp.concatenate(lift, axis=0))]
    lift = jnp.concatenate([first, first, second], axis=0).astype(jnp.bfloat16)
    lift_out[...] = lift
    hidden_out[...] = lifted(x, lift)
    proj = two_halves(2.0 * proj_ref[...]) + [jnp.zeros((10, 128), jnp.float32)]
    proj = [term.astype(jnp.float32) for term in split_terms(jnp.concatenate(proj, axis=0))]
    proj_out[...] = jnp.concatenate(proj, axis=0).astype(jnp.bfloat16)


def cells_in_rows(both, half):
    blocks = []
    for x_ref in both:
        for r in range(4):
            for upper in range(2):
                begin = pl.multiple_of(((2 * r + half) * 2 + upper) * 128, 128)
                blocks.append(x_ref[0:8, pl.ds(begin, 128)])
    row = lax.broadcasted_iota(jnp.int32, (128, 128), 0)
    lane = lax.broadcasted_iota(jnp.int32, (128, 128), 1)
    z = ((lane & 7) << 1) | ((lane >> 3) & 1)
    turned = ((row >> 3) == z) & ((row & 7) == (lane >> 4))
    turned = jnp.where(turned, 1.0, 0.0).astype(jnp.bfloat16)
    return nt_dot(turned, jnp.concatenate(blocks, axis=0).astype(jnp.bfloat16)).astype(jnp.bfloat16)


def second_kernel(ids_ref, x_ref, lift_ref, proj_ref, w_ref, c_ref, b_ref, kept, given, s_a, s_b, s_c, s_d, v_a, v_b, v_c, x_new):
    s = pl.program_id(0)

    state, v_refs = (s_a, s_b, s_c, s_d), (v_a, v_b, v_c)

    @pl.when(s == 0)
    def begin():
        s_a[...] = lifted(x_ref[...], lift_ref[...]).astype(jnp.float32)

    w_refs = [w_ref.at[0, 0], w_ref.at[0, 1], c_ref.at[0]]
    run_section(state, v_refs, w_refs, [b_ref.at[0, i] for i in range(LAYERS)], lambda layer: None)

    @pl.when(s == pl.num_programs(0) - 1)
    def finish():
        x_new[...] = renewed_fields(x_ref[...], proj_ref, s_a)
        kept[...] = cells_in_rows((x_ref, x_new), ids_ref[0])
        given[...] = cells_in_rows((x_ref, x_new), 1 - ids_ref[0])


def place_kernel(share, pieces, out_ref):
    y_cells = out_ref.shape[-1]
    count = 48 * share
    row = lax.broadcasted_iota(jnp.int32, (count, 128), 0) >> (share.bit_length() - 1)
    lane = lax.broadcasted_iota(jnp.int32, (count, 128), 1)
    step = jnp.where(row >= 24, 1, 0)
    place = step * 64 + (row & 3) * 16 + ((row >> 2) & 1) * 3 + ((row >> 3) - 3 * step)
    chosen = [jnp.where(lane == place + 8 * upper, 1.0, 0.0).astype(jnp.bfloat16) for upper in range(2)]
    own_z = lax.broadcasted_iota(jnp.int32, (count, y_cells), 0) & (share - 1)
    for crop in range(pieces.shape[0]):
        lower, upper = [nt_dot(one, pieces[crop]) for one in chosen]
        cells = jnp.zeros((count, y_cells), jnp.float32)
        for z in range(share):
            both = jnp.concatenate([lower[:, 8 * z : 8 * z + 8], upper[:, 8 * z : 8 * z + 8]], axis=1)
            cells = jnp.where(own_z == z, both, cells)
        for step in range(STEPS):
            for comp in range(3):
                for x in range(8):
                    begin = ((3 * step + comp) * 8 + x) * share
                    out_ref[step, crop, comp, x] = cells[begin : begin + share]


def split_terms(matrix):
    first = matrix.astype(jnp.bfloat16)
    rest = matrix - first.astype(jnp.float32)
    second = rest.astype(jnp.bfloat16)
    third = (rest - second.astype(jnp.float32)).astype(jnp.bfloat16)
    return first, second, third


def state_scratch():
    return (
        [pltpu.VMEM((8, 16, 16, 128), jnp.float32)] * 4
        + [pltpu.VMEM((4, 8, 128, 128), jnp.bfloat16)] * 2
        + [pltpu.VMEM((5, 8, 64, 128), jnp.bfloat16)]
    )


def shards(fields, anchors, lift_weight, conv_weight, conv_bias, proj_weight):
    segments = lax.axis_size("segment")
    slabs = lax.axis_size("slab")
    segment_id = lax.axis_index("segment")
    slab_id = lax.axis_index("slab")
    crop_count, comps, slab_rows, y_cells, z_cells = fields.shape
    lines = crop_count // slabs
    levels = segments // lines
    line = segment_id % lines
    slot = line * slabs + slab_id
    swap = [(0, 1), (1, 0)]
    vmem = pl.BlockSpec(memory_space=pltpu.VMEM)
    smem = pl.BlockSpec(memory_space=pltpu.SMEM)
    anyspace = pl.BlockSpec(memory_space=pl.ANY)
    params = pltpu.CompilerParams(vmem_limit_bytes=VMEM_BYTES)
    ids = jnp.stack([slab_id, line, slot, segment_id // lines]).astype(jnp.int32)

    def after(value, earlier):
        return lax.optimization_barrier((value, earlier))[0]

    def between_cores(value):
        return lax.ppermute(value, "slab", swap)

    packed = pl.pallas_call(
        pack_kernel,
        out_shape=jax.ShapeDtypeStruct((LAYERS, ROWS, 128), jnp.bfloat16),
        in_specs=[vmem] * 3,
        out_specs=vmem,
        compiler_params=params,
    )(conv_weight[0], conv_bias.transpose(1, 0, 2), jnp.eye(192, dtype=jnp.bfloat16))

    flat = after(fields, packed).reshape(crop_count, comps, slab_rows, y_cells * z_cells)
    h_shape = jax.ShapeDtypeStruct((8, 16, 16, 128), jnp.bfloat16)
    x, lift, proj, hidden = pl.pallas_call(
        feature_kernel,
        out_shape=(
            jax.ShapeDtypeStruct((16, 2048), jnp.float32),
            jax.ShapeDtypeStruct((48, 128), jnp.bfloat16),
            jax.ShapeDtypeStruct((48, 128), jnp.bfloat16),
            h_shape,
        ),
        in_specs=[smem, smem] + [vmem] * 4,
        out_specs=(vmem, vmem, vmem, vmem),
        compiler_params=params,
    )(ids, anchors, flat, between_cores(flat), lift_weight.T, proj_weight)

    w_shape = jax.ShapeDtypeStruct((segments, 2, 4, 256, 384), jnp.bfloat16)
    c_shape = jax.ShapeDtypeStruct((segments, 1024, 768), jnp.bfloat16)
    b_shape = jax.ShapeDtypeStruct((segments, LAYERS, 8, 128), jnp.float32)
    x_shape = jax.ShapeDtypeStruct((16, 2048), jnp.float32)
    layer_flops = 2 * 4 * 1024 * 256 * 512
    def hand_on(value, level):
        pairs = [(s * slabs, (s - lines) * slabs) for s in range(lines, segments - lines * level)]
        pairs += [(0, slabs + 1), (slabs, 1)]
        return lax.ppermute(value, ("segment", "slab"), pairs)

    arrived = {0: after(hand_on(packed, 0), x)}
    swapped = {0: between_cores(arrived[0])}
    arrived[1] = hand_on(arrived[0], 1)
    kept = ()
    current = x
    for level in range(levels):
        own = (packed, packed) if level == 0 else (arrived[level - 1], swapped[level - 1])
        operands = (ids, *own, swapped[level], arrived[level], current, lift, proj, hidden, *kept)
        weights, cycles, rows, hidden, current = pl.pallas_call(
            functools.partial(level_kernel, level, level == levels - 1),
            out_shape=(w_shape, c_shape, b_shape, h_shape, x_shape),
            in_specs=[smem] + [vmem] * 8 + ([anyspace] * 3 if kept else []),
            out_specs=(anyspace, anyspace, anyspace, vmem, vmem),
            scratch_shapes=state_scratch()
            + [
                pltpu.VMEM((LAYERS, ROWS, 128), jnp.bfloat16),
                pltpu.VMEM((2, 2, 4, 256, 384), jnp.bfloat16),
                pltpu.VMEM((2, 1024, 768), jnp.bfloat16),
                pltpu.VMEM((2, LAYERS, 8, 128), jnp.float32),
                pltpu.SemaphoreType.DMA((2, LAYERS + 1)),
            ],
            input_output_aliases={9: 0, 10: 1, 11: 2} if kept else {},
            compiler_params=params,
            cost_estimate=pl.CostEstimate(flops=2 * LAYERS * layer_flops, bytes_accessed=4 << 20, transcendentals=0),
        )(*operands)
        kept = (weights, cycles, rows)
        if level + 1 < levels:
            arrived[level + 1] = after(arrived[level + 1], hidden)
            swapped[level + 1] = between_cores(arrived[level + 1])
            if level + 2 < levels:
                arrived[level + 2] = hand_on(arrived[level + 1], level + 2)
    first_result = current
    kept, given = pl.pallas_call(
        second_kernel,
        grid=(segments,),
        out_shape=(jax.ShapeDtypeStruct((128, 128), jnp.bfloat16),) * 2,
        in_specs=[smem]
        + [vmem] * 3
        + [
            pl.BlockSpec((1, 2, 4, 256, 384), lambda s: (s, 0, 0, 0, 0)),
            pl.BlockSpec((1, 1024, 768), lambda s: (s, 0, 0)),
            pl.BlockSpec((1, LAYERS, 8, 128), lambda s: (s, 0, 0, 0)),
        ],
        out_specs=(vmem, vmem),
        scratch_shapes=state_scratch() + [pltpu.VMEM((16, 2048), jnp.float32)],
        compiler_params=params,
        cost_estimate=pl.CostEstimate(flops=segments * LAYERS * layer_flops, bytes_accessed=16 << 20, transcendentals=0),
    )(ids, first_result, lift, proj, weights, cycles, rows)

    share = z_cells // segments
    got = between_cores(given)
    pair = jnp.where(slab_id == 0, jnp.stack([kept, got]), jnp.stack([got, kept]))
    pieces = pair.reshape(slabs, segments, share * 8, 128).transpose(1, 0, 2, 3)
    pieces = lax.all_to_all(pieces, "segment", 0, 0, tiled=True)
    pieces = pieces[:lines].reshape(crop_count, share * 8, 128)
    out = pl.pallas_call(
        functools.partial(place_kernel, share),
        out_shape=jax.ShapeDtypeStruct((STEPS, crop_count, comps, slab_rows, share, y_cells), jnp.float32),
        in_specs=[vmem],
        out_specs=vmem,
        compiler_params=params,
    )(pieces)
    return out.transpose(0, 1, 2, 3, 5, 4)


def solution(mesh):
    in_specs = (
        P("groups", None, "slab", None, None),
        P("groups", None),
        P(),
        P("segment", None, None, None, None),
        P("segment", None, None),
        P(),
    )
    out_specs = P(None, "groups", None, "slab", None, "segment")
    return jax.shard_map(shards, mesh=mesh, in_specs=in_specs, out_specs=out_specs, check_vma=False)
```

```python
import functools

import jax
import jax.numpy as jnp
from jax import lax
from jax.experimental import pallas as pl
from jax.experimental.pallas import tpu as pltpu
from jax.sharding import PartitionSpec as P

STEPS = 2
FIELD = 4096
LAYERS = 3
CH = 64
ROWS = 896
VMEM_BYTES = 48 * 1024 * 1024

MOVES = (
    [(4 * b + m, 4 * b + 2 + m, 4 * m + b, 4 * m + 2 + b) for b in range(2) for m in range(2)],
    [(2 * m, 2 * m + 1, m, 4 + m) for m in range(4)],
    [(4 * p + 2 * m, 4 * p + 2 * m + 1, 2 * p + m, 2 * (2 + p) + m) for p in range(2) for m in range(2)],
)
CYCLES = (
    [list(range(8))],
    [list(range(4)), list(range(4, 8))],
    [[2 * r, 2 * r + 1] for r in range(4)],
)


GROUPS = ((0,), (1,), (2,), (3,))


def neighbour(layer, tile, step):
    cycle = next(cycle for cycle in CYCLES[layer] if tile in cycle)
    return cycle[(cycle.index(tile) + step) % len(cycle)]


def low_lanes(shape):
    return lax.broadcasted_iota(jnp.int32, shape, len(shape) - 1) < CH


def nt_dot(a, b):
    return lax.dot_general(a, b, (((1,), (1,)), ((), ())), preferred_element_type=jnp.float32)


def pack_kernel(raw_ref, bias_ref, eye_ref, packed):
    eye = eye_ref[...]
    low = low_lanes((CH, 128))
    for layer in range(LAYERS):
        for ty in range(3):
            pair = jnp.concatenate([raw_ref[layer, 3 + ty], raw_ref[layer, ty]], axis=0)
            packed[layer, ty * 192 : (ty + 1) * 192, :] = nt_dot(eye, pair).astype(jnp.bfloat16)
        pair = jnp.concatenate([raw_ref[layer, 6], raw_ref[layer, 7]], axis=0)
        packed[layer, 576:768, :] = nt_dot(eye, pair).astype(jnp.bfloat16)
        pair = jnp.concatenate([raw_ref[layer, 8], raw_ref[layer, 8]], axis=0)
        twice = nt_dot(eye, pair)
        packed[layer, 768:832, :] = jnp.where(low, twice[0:64], twice[64:128]).astype(jnp.bfloat16)
        terms = [term.astype(jnp.float32) for term in split_terms(bias_ref[layer])]
        terms = jnp.concatenate(terms + [jnp.zeros((CH - 3, CH), jnp.float32)], axis=0)
        terms = jnp.concatenate([terms, terms], axis=1)
        packed[layer, 832:896, :] = jnp.where(low, twice[128:192], terms).astype(jnp.bfloat16)


def pair_forms(taps):
    before, here, behind = taps
    ends = 0.25 * (before + behind)
    here = 0.25 * here
    return 0.5 * before, ends + here, ends - here, 0.5 * behind


def cycle_forms(taps):
    before, here, behind = taps
    ends = 0.125 * (before + behind)
    near = 0.125 * here
    return near + ends, near - ends, 0.25 * here, 0.25 * (behind - before)


def expand(packed, w_ref, bias_ref, layer):
    low = low_lanes((192, 128))
    zero = jnp.zeros((192, 128), jnp.float32)
    forms = pair_forms if layer < 2 else cycle_forms
    mids = forms([packed[ty * 192 : (ty + 1) * 192, :].astype(jnp.float32) for ty in range(3)])
    both = packed[576:768, :].astype(jnp.float32)
    ends = packed[768:832, :].astype(jnp.float32)
    rest = packed[832:896, :].astype(jnp.float32)
    ends = jnp.concatenate([ends, pltpu.roll(ends, CH, 1), rest], axis=0)
    lasts = forms([both, pltpu.roll(both, CH, 1), ends])
    for index, (mid, last) in enumerate(zip(mids, lasts)):
        rolled = pltpu.roll(mid, CH, 1)
        blocks = (
            mid,
            jnp.where(low, last, rolled),
            jnp.where(low, zero, pltpu.roll(last, CH, 1)),
            jnp.where(low, rolled, zero),
        )
        blocks = [block.astype(jnp.bfloat16) for block in blocks]
        for tz in range(3):
            for a in range(4):
                if layer < 2:
                    w_ref[index, a * CH : (a + 1) * CH, tz * 128 : (tz + 1) * 128] = blocks[a][tz * CH : (tz + 1) * CH]
                else:
                    row = index * 256 + a * CH
                    for half in range(2):
                        chosen = blocks[((0, 2), (1, 3), (2, 0), (3, 1))[a][half]]
                        column = tz * 256 + half * 128
                        w_ref[row : row + CH, column : column + 128] = chosen[tz * CH : (tz + 1) * CH]
    bias = 0.5 * (rest[0:1] + rest[1:2] + rest[2:3])
    bias = jnp.where(low_lanes((1, 128)), pltpu.roll(bias, CH, 1), bias)
    bias_ref[...] = jnp.broadcast_to(bias, (8, 128))


def z_moved(values, tap, layer):
    even, odd = values[:, :8], values[:, 8:]
    if layer > 0:
        shift = -tap * 2 ** (layer - 1) % 8
        return pltpu.roll(even, shift, 1), pltpu.roll(odd, shift, 1)
    if tap > 0:
        return odd, pltpu.roll(even, 7, 1)
    return pltpu.roll(odd, 1, 1), even


def z_summed(products, width, layer):
    products = products.reshape(products.shape[0] // 16, 16, products.shape[1])
    here = products[:, :, width : 2 * width]
    before = z_moved(products[:, :, :width], -1, layer)
    behind = z_moved(products[:, :, 2 * width :], 1, layer)
    parts = [here[:, 8 * i : 8 * i + 8] + before[i] + behind[i] for i in range(2)]
    return jnp.concatenate(parts, axis=1)


def activate_into(v_ref, tile, value, layer):
    activated = value * jnp.tanh(value) + value
    if layer < 2:
        d = 2**layer
        pairs = activated.reshape(8 // d, 2, d, 16, 128)
        first, second = pairs[:, 0], pairs[:, 1]
        before = jnp.concatenate([second[-1:], second[:-1]], axis=0)
        behind = jnp.concatenate([first[1:], first[:1]], axis=0)
        mixed = (before - second, first + second, second - first, first - behind)
    else:
        cycle = activated.reshape(4, 4, 16, 128)
        even, odd = cycle[0] + cycle[2], cycle[1] + cycle[3]
        sine = cycle[3] - cycle[1]
        mixed = (even + odd, even - odd, cycle[0] - cycle[2], sine, -sine)
    for index, value in enumerate(mixed):
        v_ref[index, tile] = value.reshape(-1, 128).astype(jnp.bfloat16)


def spread(move, u, v, state_out, v_ref, layer):
    low = low_lanes((16, 16, 128))
    for at, value in (
        (move[2], jnp.where(low, u, pltpu.roll(v, CH, 2))),
        (move[3], jnp.where(low, pltpu.roll(u, CH, 2), v)),
    ):
        state_out[at] = value
        activate_into(v_ref, at, value, layer)


def convolve_pairs(v_ref, w_ref, tiles, layer):
    d = 2**layer
    low = low_lanes((128, 128))
    sums = []
    for index in range(4):
        rows = []
        for tile in tiles:
            after = v_ref[index, neighbour(layer, tile, 1)]
            before = v_ref[index, neighbour(layer, tile, -1)]
            rows.append(jnp.concatenate([v_ref[index, tile], jnp.where(low, after, before)], axis=1))
        rows = jnp.concatenate(rows, axis=0)
        sums.append(z_summed(jnp.dot(rows, w_ref[index], preferred_element_type=jnp.float32), 128, layer))
    first = sums[0] + sums[1] + sums[2]
    second = sums[1] - sums[2] - sums[3]
    results = []
    for at in range(len(tiles)):
        halves = [half[at * 8 : (at + 1) * 8].reshape(8 // d, 1, d, 16, 128) for half in (first, second)]
        results.append(jnp.concatenate(halves, axis=1).reshape(16, 16, 128))
    return results


def convolve_cycles(v_ref, w_ref, units, layer):
    def rows(*forms):
        parts = [jnp.concatenate([v_ref[form, 2 * r + m] for form in forms for m in range(2)], axis=1) for r in units]
        return jnp.concatenate(parts, axis=0)

    def summed(lhs, begin, end):
        return z_summed(jnp.dot(lhs, w_ref[begin:end, :], preferred_element_type=jnp.float32), 256, layer)

    flat = summed(rows(0), 0, 256)
    alternate = summed(rows(1), 256, 512)
    cosine = summed(rows(2, 4), 512, 1024)
    sine = summed(rows(3, 2), 512, 1024)
    even, odd = flat + alternate, flat - alternate
    cells = [value.reshape(len(units), 1, 4, 16, 256) for value in (even + cosine, odd - sine, even - cosine, odd + sine)]
    cells = jnp.concatenate(cells, axis=1).reshape(len(units), 16, 16, 256)
    return [cells[at, :, :, m * 128 : m * 128 + 128] for at in range(len(units)) for m in range(2)]


def begin_section(state, v_refs):
    for move in MOVES[0]:
        spread(move, state[0][move[0]], state[0][move[1]], state[1], v_refs[0], 0)


def run_section(state, v_refs, w_refs, bias_refs, prepare):
    s_a, *held_in = state
    begin_section(state, v_refs)
    prepare(0)
    for layer in range(LAYERS):
        held, following = held_in[layer], held_in[(layer + 1) % LAYERS]
        if layer + 1 < LAYERS:
            prepare(layer + 1)
        bias = bias_refs[layer][0:1][None]
        if layer == LAYERS - 1:
            for tile, total in enumerate(convolve_cycles(v_refs[2], w_refs[layer], range(4), layer)):
                s_a[tile] = (held[tile] + bias + total).astype(jnp.bfloat16).astype(jnp.float32)
            break
        for chosen in GROUPS:
            moves = [MOVES[layer + 1][at] for at in chosen]
            tiles = [tile for move in moves for tile in move[:2]]
            sums = convolve_pairs(v_refs[layer], w_refs[layer], tiles, layer)
            sums = [held[tile] + bias + total for tile, total in zip(tiles, sums)]
            for at, move in enumerate(moves):
                spread(move, sums[2 * at], sums[2 * at + 1], following, v_refs[layer + 1], layer + 1)


def by_parity(x):
    row = lax.broadcasted_iota(jnp.int32, (128, 128), 0)
    lane = lax.broadcasted_iota(jnp.int32, (128, 128), 1)
    place = (row & 112) | ((row & 1) << 3) | ((row >> 1) & 7)
    turned = jnp.where(place == lane, 1.0, 0.0).astype(jnp.bfloat16)
    blocks = jnp.concatenate([x[:, at * 128 : (at + 1) * 128] for at in range(16)], axis=0)
    moved = sum(jnp.dot(term, turned, preferred_element_type=jnp.float32) for term in split_terms(blocks))
    return jnp.concatenate([moved[at * 16 : (at + 1) * 16] for at in range(16)], axis=1)


def lifted(x, lift):
    high = x.astype(jnp.bfloat16).astype(jnp.float32)
    columns = jnp.concatenate([high, x - high, high], axis=0).T.astype(jnp.bfloat16)
    hidden = jnp.dot(columns, lift, preferred_element_type=jnp.float32)
    return hidden.astype(jnp.bfloat16).reshape(8, 16, 16, 128)


def renewed_fields(x, proj_ref, s_a):
    gain = nt_dot(proj_ref[...], s_a[...].reshape(2048, 128).astype(jnp.bfloat16))
    return x + gain[:16] + gain[16:32] + gain[32:48]


def level_kernel(level, last, *refs):
    (ids_ref, own_0, own_1, far_0, far_1, x_ref, lift_ref, proj_ref) = refs[:8]
    (w_out, c_out, b_out, leaving, x_out, s_a, s_b, s_c, s_d, v_a, v_b, v_c) = refs[-17:-5]
    (packed, w_pair, w_cycle, b_all, sems) = refs[-5:]
    slab, line = ids_ref[0], ids_ref[1]
    x = x_ref[...]
    s_a[...] = refs[8][...].astype(jnp.float32)
    state, v_refs = (s_a, s_b, s_c, s_d), (v_a, v_b, v_c)

    def copy(turn, part):
        at = 2 * level + turn
        source = (w_pair.at[turn, 0], w_pair.at[turn, 1], w_cycle.at[turn], b_all.at[turn])[part]
        target = (w_out.at[at, 0], w_out.at[at, 1], c_out.at[at], b_out.at[at])[part]
        return pltpu.make_async_copy(source, target, sems.at[turn, part])

    def section(turn, unused):
        for wanted, sources in ((True, (own_0, own_1)), (False, (far_0, far_1))):
            for core, source in enumerate(sources):

                @pl.when(((turn == line) == wanted) & (slab == core))
                def take(source=source):
                    packed[...] = source[...]

        w_refs = [w_pair.at[turn, 0], w_pair.at[turn, 1], w_cycle.at[turn]]

        def prepare(layer):
            expand(packed.at[layer], w_refs[layer], b_all.at[turn, layer], layer)
            copy(turn, layer).start()

        run_section(state, v_refs, w_refs, [b_all.at[turn, i] for i in range(LAYERS)], prepare)
        copy(turn, LAYERS).start()
        return 0

    lax.fori_loop(0, 2, section, 0)
    leaving[...] = s_a[...].astype(jnp.bfloat16)
    x_out[...] = renewed_fields(x, proj_ref, s_a) if last else x
    for turn in range(2):
        for part in range(LAYERS + 1):
            copy(turn, part).wait()


def feature_kernel(ids_ref, anchor_ref, kept_ref, got_ref, lift_ref, proj_ref, x_ref, lift_out, proj_out, hidden_out):
    slab, slot = ids_ref[0], ids_ref[2]
    kept, got = kept_ref[slot], got_ref[slot]
    halves = (jnp.where(slab == 0, kept, got), jnp.where(slab == 0, got, kept))
    columns = []
    for r in range(4):
        for m in range(2):
            columns.append(jnp.concatenate([halves[m][:, r], halves[m][:, 4 + r]], axis=0))
    current = jnp.concatenate([jnp.concatenate(columns, axis=1), jnp.zeros((10, 2048), jnp.float32)], axis=0)
    row = lax.broadcasted_iota(jnp.int32, (16, 2048), 0)
    column = lax.broadcasted_iota(jnp.int32, (16, 2048), 1)
    along_x = ((column >> 8) & 1) * 8 + (column >> 9) + jnp.where(row >= 9, 4, 0)
    along_x = along_x + anchor_ref[slot, 0]
    along_y = ((column >> 4) & 15) + anchor_ref[slot, 1]
    along_z = (column & 15) + anchor_ref[slot, 2]
    axis = jnp.where(row >= 9, row - 9, row - 6)
    position = jnp.where(axis == 0, along_x, jnp.where(axis == 1, along_y, along_z)) & (FIELD - 1)
    waves = jnp.sin(2.0 * jnp.pi * position.astype(jnp.float32) / FIELD)
    x = by_parity(jnp.where(row < 6, current, jnp.where(row < 12, waves, 0.0)))
    x_ref[...] = x

    def two_halves(part):
        blank = jnp.zeros(part.shape, jnp.float32)
        return [jnp.concatenate([part, blank], axis=1), jnp.concatenate([blank, part], axis=1)]

    lift = 0.5 * lift_ref[...]
    lift = two_halves(lift[0:3]) + two_halves(lift[3:6]) + [jnp.zeros((4, 128), jnp.float32)]
    first, second, unused = [term.astype(jnp.float32) for term in split_terms(jnp.concatenate(lift, axis=0))]
    lift = jnp.concatenate([first, first, second], axis=0).astype(jnp.bfloat16)
    lift_out[...] = lift
    hidden_out[...] = lifted(x, lift)
    proj = two_halves(2.0 * proj_ref[...]) + [jnp.zeros((10, 128), jnp.float32)]
    proj = [term.astype(jnp.float32) for term in split_terms(jnp.concatenate(proj, axis=0))]
    proj_out[...] = jnp.concatenate(proj, axis=0).astype(jnp.bfloat16)


def cells_in_rows(both, half):
    blocks = []
    for x_ref in both:
        for r in range(4):
            for upper in range(2):
                begin = pl.multiple_of(((2 * r + half) * 2 + upper) * 128, 128)
                blocks.append(x_ref[0:8, pl.ds(begin, 128)])
    row = lax.broadcasted_iota(jnp.int32, (128, 128), 0)
    lane = lax.broadcasted_iota(jnp.int32, (128, 128), 1)
    z = ((lane & 7) << 1) | ((lane >> 3) & 1)
    turned = ((row >> 3) == z) & ((row & 7) == (lane >> 4))
    turned = jnp.where(turned, 1.0, 0.0).astype(jnp.bfloat16)
    return nt_dot(turned, jnp.concatenate(blocks, axis=0).astype(jnp.bfloat16)).astype(jnp.bfloat16)


def second_kernel(ids_ref, x_ref, lift_ref, proj_ref, w_hbm, c_hbm, b_hbm, kept, given, *scratch):
    s_a, s_b, s_c, s_d, v_a, v_b, v_c, x_new, w_all, c_all, b_all, sems = scratch
    sections = w_hbm.shape[0]

    def copy(s, slot, part):
        source, target = ((w_hbm, w_all), (c_hbm, c_all), (b_hbm, b_all))[part]
        return pltpu.make_async_copy(source.at[s], target.at[slot], sems.at[slot, part])

    for part in range(3):
        copy(0, 0, part).start()
    s_a[...] = lifted(x_ref[...], lift_ref[...]).astype(jnp.float32)

    def section(s, unused):
        slot = lax.rem(s, 2)
        for part in range(3):
            copy(s, slot, part).wait()

        @pl.when(s + 1 < sections)
        def fetch():
            for part in range(3):
                copy(s + 1, 1 - slot, part).start()

        w_refs = [w_all.at[slot, 0], w_all.at[slot, 1], c_all.at[slot]]
        biases = [b_all.at[slot, i] for i in range(LAYERS)]
        run_section((s_a, s_b, s_c, s_d), (v_a, v_b, v_c), w_refs, biases, lambda layer: None)
        return 0

    lax.fori_loop(0, sections, section, 0)
    x_new[...] = renewed_fields(x_ref[...], proj_ref, s_a)
    kept[...] = cells_in_rows((x_ref, x_new), ids_ref[0])
    given[...] = cells_in_rows((x_ref, x_new), 1 - ids_ref[0])


def place_kernel(share, pieces, out_ref):
    y_cells = out_ref.shape[-1]
    count = 48 * share
    row = lax.broadcasted_iota(jnp.int32, (count, 128), 0) >> (share.bit_length() - 1)
    lane = lax.broadcasted_iota(jnp.int32, (count, 128), 1)
    step = jnp.where(row >= 24, 1, 0)
    place = step * 64 + (row & 3) * 16 + ((row >> 2) & 1) * 3 + ((row >> 3) - 3 * step)
    chosen = [jnp.where(lane == place + 8 * upper, 1.0, 0.0).astype(jnp.bfloat16) for upper in range(2)]
    own_z = lax.broadcasted_iota(jnp.int32, (count, y_cells), 0) & (share - 1)
    for crop in range(pieces.shape[0]):
        lower, upper = [nt_dot(one, pieces[crop]) for one in chosen]
        cells = jnp.zeros((count, y_cells), jnp.float32)
        for z in range(share):
            both = jnp.concatenate([lower[:, 8 * z : 8 * z + 8], upper[:, 8 * z : 8 * z + 8]], axis=1)
            cells = jnp.where(own_z == z, both, cells)
        for step in range(STEPS):
            for comp in range(3):
                for x in range(8):
                    begin = ((3 * step + comp) * 8 + x) * share
                    out_ref[step, crop, comp, x] = cells[begin : begin + share]


def split_terms(matrix):
    first = matrix.astype(jnp.bfloat16)
    rest = matrix - first.astype(jnp.float32)
    second = rest.astype(jnp.bfloat16)
    third = (rest - second.astype(jnp.float32)).astype(jnp.bfloat16)
    return first, second, third


def state_scratch():
    return (
        [pltpu.VMEM((8, 16, 16, 128), jnp.float32)] * 4
        + [pltpu.VMEM((4, 8, 128, 128), jnp.bfloat16)] * 2
        + [pltpu.VMEM((5, 8, 64, 128), jnp.bfloat16)]
    )


def shards(fields, anchors, lift_weight, conv_weight, conv_bias, proj_weight):
    segments = lax.axis_size("segment")
    slabs = lax.axis_size("slab")
    segment_id = lax.axis_index("segment")
    slab_id = lax.axis_index("slab")
    crop_count, comps, slab_rows, y_cells, z_cells = fields.shape
    lines = crop_count // slabs
    levels = segments // lines
    line = segment_id % lines
    slot = line * slabs + slab_id
    swap = [(0, 1), (1, 0)]
    vmem = pl.BlockSpec(memory_space=pltpu.VMEM)
    smem = pl.BlockSpec(memory_space=pltpu.SMEM)
    anyspace = pl.BlockSpec(memory_space=pl.ANY)
    params = pltpu.CompilerParams(vmem_limit_bytes=VMEM_BYTES)
    ids = jnp.stack([slab_id, line, slot, segment_id // lines]).astype(jnp.int32)

    def after(value, earlier):
        return lax.optimization_barrier((value, earlier))[0]

    def between_cores(value):
        return lax.ppermute(value, "slab", swap)

    packed = pl.pallas_call(
        pack_kernel,
        out_shape=jax.ShapeDtypeStruct((LAYERS, ROWS, 128), jnp.bfloat16),
        in_specs=[vmem] * 3,
        out_specs=vmem,
        compiler_params=params,
    )(conv_weight[0], conv_bias.transpose(1, 0, 2), jnp.eye(192, dtype=jnp.bfloat16))

    flat = after(fields, packed).reshape(crop_count, comps, slab_rows, y_cells * z_cells)
    h_shape = jax.ShapeDtypeStruct((8, 16, 16, 128), jnp.bfloat16)
    x, lift, proj, hidden = pl.pallas_call(
        feature_kernel,
        out_shape=(
            jax.ShapeDtypeStruct((16, 2048), jnp.float32),
            jax.ShapeDtypeStruct((48, 128), jnp.bfloat16),
            jax.ShapeDtypeStruct((48, 128), jnp.bfloat16),
            h_shape,
        ),
        in_specs=[smem, smem] + [vmem] * 4,
        out_specs=(vmem, vmem, vmem, vmem),
        compiler_params=params,
    )(ids, anchors, flat, between_cores(flat), lift_weight.T, proj_weight)

    w_shape = jax.ShapeDtypeStruct((segments, 2, 4, 256, 384), jnp.bfloat16)
    c_shape = jax.ShapeDtypeStruct((segments, 1024, 768), jnp.bfloat16)
    b_shape = jax.ShapeDtypeStruct((segments, LAYERS, 8, 128), jnp.float32)
    x_shape = jax.ShapeDtypeStruct((16, 2048), jnp.float32)
    layer_flops = 2 * 4 * 1024 * 256 * 512
    def hand_on(value, level):
        pairs = [(s * slabs, (s - lines) * slabs) for s in range(lines, segments - lines * level)]
        pairs += [(0, slabs + 1), (slabs, 1)]
        return lax.ppermute(value, ("segment", "slab"), pairs)

    arrived = {0: after(hand_on(packed, 0), x)}
    swapped = {0: between_cores(arrived[0])}
    arrived[1] = hand_on(arrived[0], 1)
    kept = ()
    current = x
    for level in range(levels):
        own = (packed, packed) if level == 0 else (arrived[level - 1], swapped[level - 1])
        operands = (ids, *own, swapped[level], arrived[level], current, lift, proj, hidden, *kept)
        weights, cycles, rows, hidden, current = pl.pallas_call(
            functools.partial(level_kernel, level, level == levels - 1),
            out_shape=(w_shape, c_shape, b_shape, h_shape, x_shape),
            in_specs=[smem] + [vmem] * 8 + ([anyspace] * 3 if kept else []),
            out_specs=(anyspace, anyspace, anyspace, vmem, vmem),
            scratch_shapes=state_scratch()
            + [
                pltpu.VMEM((LAYERS, ROWS, 128), jnp.bfloat16),
                pltpu.VMEM((2, 2, 4, 256, 384), jnp.bfloat16),
                pltpu.VMEM((2, 1024, 768), jnp.bfloat16),
                pltpu.VMEM((2, LAYERS, 8, 128), jnp.float32),
                pltpu.SemaphoreType.DMA((2, LAYERS + 1)),
            ],
            input_output_aliases={9: 0, 10: 1, 11: 2} if kept else {},
            compiler_params=params,
            cost_estimate=pl.CostEstimate(flops=2 * LAYERS * layer_flops, bytes_accessed=4 << 20, transcendentals=0),
        )(*operands)
        kept = (weights, cycles, rows)
        if level + 1 < levels:
            arrived[level + 1] = after(arrived[level + 1], hidden)
            swapped[level + 1] = between_cores(arrived[level + 1])
            if level + 2 < levels:
                arrived[level + 2] = hand_on(arrived[level + 1], level + 2)
    first_result = current
    kept, given = pl.pallas_call(
        second_kernel,
        out_shape=(jax.ShapeDtypeStruct((128, 128), jnp.bfloat16),) * 2,
        in_specs=[smem] + [vmem] * 3 + [anyspace] * 3,
        out_specs=(vmem, vmem),
        scratch_shapes=state_scratch()
        + [
            pltpu.VMEM((16, 2048), jnp.float32),
            pltpu.VMEM((2, 2, 4, 256, 384), jnp.bfloat16),
            pltpu.VMEM((2, 1024, 768), jnp.bfloat16),
            pltpu.VMEM((2, LAYERS, 8, 128), jnp.float32),
            pltpu.SemaphoreType.DMA((2, 3)),
        ],
        compiler_params=params,
        cost_estimate=pl.CostEstimate(flops=segments * LAYERS * layer_flops, bytes_accessed=16 << 20, transcendentals=0),
    )(ids, first_result, lift, proj, weights, cycles, rows)

    share = z_cells // segments
    got = between_cores(given)
    pair = jnp.where(slab_id == 0, jnp.stack([kept, got]), jnp.stack([got, kept]))
    pieces = pair.reshape(slabs, segments, share * 8, 128).transpose(1, 0, 2, 3)
    pieces = lax.all_to_all(pieces, "segment", 0, 0, tiled=True)
    pieces = pieces[:lines].reshape(crop_count, share * 8, 128)
    out = pl.pallas_call(
        functools.partial(place_kernel, share),
        out_shape=jax.ShapeDtypeStruct((STEPS, crop_count, comps, slab_rows, share, y_cells), jnp.float32),
        in_specs=[vmem],
        out_specs=vmem,
        compiler_params=params,
    )(pieces)
    return out.transpose(0, 1, 2, 3, 5, 4)


def solution(mesh):
    in_specs = (
        P("groups", None, "slab", None, None),
        P("groups", None),
        P(),
        P("segment", None, None, None, None),
        P("segment", None, None),
        P(),
    )
    out_specs = P(None, "groups", None, "slab", None, "segment")
    return jax.shard_map(shards, mesh=mesh, in_specs=in_specs, out_specs=out_specs, check_vma=False)
```
